32 devices in a mesh: blocks: 8 (over z, y), rows: 4 (over x, core).
Axes of the slice: x: 2, y: 2, z: 4, core: 2. Of those that a mesh axis runs over, the one named last changes fastest.
Arguments:
- hidden_in: bfloat16 [8, 512, 768], P('blocks', 'rows'), may hold values from -6 to 6
- positions: bfloat16 [8, 3, 512], P('blocks', None, 'rows'), may hold values from -8 to 8
- atom_types: int32 [8, 512], P('blocks', 'rows'), may hold values from 0 to 511
- path_hops: int32 [8, 512, 512], P('blocks', 'rows'), may hold values from 0 to 511
- edge_kinds: int32 [8, 512, 512], P('blocks', 'rows'), may hold values from 0 to 1535
- mol_lengths: int32 [8, 16], P('blocks'), may hold values from 1 to 96, 512 in all within a row
- qkv_weight: bfloat16 [768, 2304], replicated, may hold values from -0.21875 to 0.21875
- out_weight: bfloat16 [768, 768], replicated, may hold values from -0.625 to 0.625
- attn_gain: float32 [768], replicated, may hold values from 0.5 to 1.5
- ffn_gain: float32 [768], replicated, may hold values from 0.5 to 1.5
- up_weight: bfloat16 [768, 768], replicated, may hold values from -0.21875 to 0.21875
- down_weight: bfloat16 [768, 768], replicated, may hold values from -0.21875 to 0.21875
- kernel_means: float32 [128], replicated, may hold values from 0 to 10
- kernel_widths: float32 [128], replicated, may hold values from 0.5 to 3
- kernel_inner: bfloat16 [128, 128], replicated, may hold values from -2 to 2
- kernel_outer: bfloat16 [128, 32], replicated, may hold values from -0.5 to 0.5
- hop_table: bfloat16 [32, 512], replicated, may hold values from -3 to 3
- edge_table: bfloat16 [32, 1536], replicated, may hold values from -3 to 3
- atom_scale: float32 [512], replicated, may hold values from 0.3 to 0.7
- atom_shift: float32 [512], replicated, may hold values from -0.5 to 0.5
- out_grad: bfloat16 [8, 512, 768], P('blocks', 'rows'), may hold values from -6 to 6
Outputs:
- layer_out: bfloat16 [8, 512, 768], P('blocks', 'rows')
- grad_in: float32 [8, 512, 768], P('blocks', 'rows')
- grad_qkv: float32 [768, 2304], replicated
- grad_out_weight: float32 [768, 768], replicated
- grad_attn_gain: float32 [768], replicated
- grad_ffn_gain: float32 [768], replicated
- grad_up: float32 [768, 768], replicated
- grad_down: float32 [768, 768], replicated
- grad_means: float32 [128], replicated
- grad_widths: float32 [128], replicated
- grad_inner: float32 [128, 128], replicated
- grad_outer: float32 [128, 32], replicated
- grad_hops: float32 [32, 512], replicated
- grad_edges: float32 [32, 1536], replicated
- grad_atom_scale: float32 [512], replicated
- grad_atom_shift: float32 [512], replicated
The draws below stay inside these ranges and needn't reach their ends.
Inputs may be any that keep to these rules, and one draw needn't show every extreme that they name: `mol_lengths`: each block's 16 molecule lengths sum to 512; the largest of every block is exactly 96.
All inputs are finite; a program needn't handle non-finite values.
Results may differ from the reference program's by a relative error of at most 0.01225.
The reference program's roundings to bfloat16 on the way count: a program that leaves them out, or rounds other values in their place, can miss the bound.
Values may be sent and summed in bfloat16 or wider, within the bound.
A program may use at most 192 MiB of HBM per device.

```python
import math
import jax
import jax.numpy as jnp
import numpy as np
from jax import lax

D = 768
HEADS = 32
HEAD_DIM = 24
FF = 768
KERNELS = 128
HOPS = 512
EDGE_KINDS = 1536
ATOM_KINDS = 512
BLOCK_LEN = 512
MOLS = 16
MOST = 96
BLOCKS_ALL = 8


def with_ends(drawn, stream_key, smallest, largest):
    shape = drawn.shape
    place = [jax.random.randint(jax.random.fold_in(stream_key, axis), (), 0, shape[axis]) for axis in range(len(shape))]
    drawn = drawn.at[tuple(place)].set(smallest)
    longest = shape.index(max(shape))
    place[longest] = (place[longest] + 1) % shape[longest]
    return drawn.at[tuple(place)].set(largest)


def level_of(stream_key, dims, cuts, least, top_value):
    factor_of = 1.0
    for position, shards_of in cuts:
        steps = jax.random.uniform(jax.random.fold_in(jax.random.fold_in(stream_key, 6), position), (shards_of,), jnp.float32, least / len(cuts), top_value / len(cuts))
        factor_of = factor_of * jnp.repeat(jnp.exp(steps), dims[position] // shards_of).reshape((-1,) + (1,) * (len(dims) - 1 - position))
    return factor_of


def rank_bounds(number_of, slope):
    weights = [(1 << 20) // math.isqrt(standing ** slope) + 1 for standing in range(1, number_of + 1)]
    scale = 1 + sum(weights) // (1 << 30)
    return np.cumsum(np.array([max(1, weight // scale) for weight in weights]))


def skewed_ids(rng, extent, count, lean):
    listing = rank_bounds(count, lean)
    ticket = jax.random.randint(jax.random.fold_in(rng, 1), extent, 0, int(listing[count - 1]))
    rank = jnp.searchsorted(jnp.asarray(listing, jnp.int32), ticket, side="right")
    return jax.random.permutation(jax.random.fold_in(rng, 2), count)[rank].astype(jnp.int32)


def length_profile(number_of, total, bound, skew):
    portions = [(1 << 20) // math.isqrt(standing ** skew) + 1 for standing in range(2, number_of + 1)]
    surplus, counts = total - bound - (number_of - 1), [1] * (number_of - 1)
    while surplus > 0:
        movable = [i for i in range(number_of - 1) if counts[i] < bound]
        mass, left = sum([portions[i] for i in movable]), surplus
        for i in movable:
            more = min(bound - counts[i], max(1, left * portions[i] // mass), surplus)
            counts[i] = counts[i] + more
            surplus = surplus - more
    return np.array([bound] + counts)


def uneven_parts(key, amount, total, most, slope):
    if amount == 2:
        one = jax.random.randint(key, (), max(1, total - most), min(most, total - 1) + 1)
        return jnp.stack([one, total - one])
    lengths = jnp.asarray(length_profile(amount, total, most, slope), jnp.int32)
    pairs = (amount - 1) // 2
    source_of, sink = lengths[1:1 + 2 * pairs:2], lengths[2:2 + 2 * pairs:2]
    slack = jnp.minimum(source_of - 1, most - sink)
    moved = jax.random.randint(jax.random.fold_in(key, 1), (pairs,), 0, 1 << 20) % (slack + 1)
    lengths = lengths.at[1:1 + 2 * pairs:2].set(source_of - moved).at[2:2 + 2 * pairs:2].set(sink + moved)
    return lengths[jax.random.permutation(jax.random.fold_in(key, 2), amount)]


def noise(rng, shape, scale, reach, split=(), kind=jnp.bfloat16):
    values = jax.random.normal(rng, shape, jnp.float32) * scale
    if len(split) > 0:
        values = level_of(rng, shape, split, -0.22, 0.18) * values
    return jnp.clip(values, min=-reach, max=reach).astype(kind)


def setup_inputs(seed: int = 0) -> dict:
    arg_keys = jax.random.split(jax.random.key(seed), 22)
    hidden_in = noise(arg_keys[0], (BLOCKS_ALL, BLOCK_LEN, D), 1.0, 6.0, ((0, 8), (1, 4)))
    positions = noise(arg_keys[1], (BLOCKS_ALL, 3, BLOCK_LEN), 2.0, 8.0, ((0, 8), (2, 4)))
    atom_types = with_ends(skewed_ids(arg_keys[2], (BLOCKS_ALL, BLOCK_LEN), ATOM_KINDS, 2), jax.random.fold_in(arg_keys[2], 3), 0, ATOM_KINDS - 1).astype(jnp.int32)
    path_hops = with_ends(skewed_ids(arg_keys[3], (BLOCKS_ALL, BLOCK_LEN, BLOCK_LEN), HOPS, 2), jax.random.fold_in(arg_keys[3], 3), 0, HOPS - 1).astype(jnp.int32)
    edge_kinds = with_ends(skewed_ids(arg_keys[4], (BLOCKS_ALL, BLOCK_LEN, BLOCK_LEN), EDGE_KINDS, 2), jax.random.fold_in(arg_keys[4], 3), 0, EDGE_KINDS - 1).astype(jnp.int32)
    mol_lengths = jax.vmap(lambda own: uneven_parts(own, MOLS, BLOCK_LEN, MOST, 1))(jax.random.split(arg_keys[5], BLOCKS_ALL)).reshape((BLOCKS_ALL, MOLS)).astype(jnp.int32)
    qkv_weight = noise(arg_keys[6], (D, 3 * D), D ** -0.5, 0.21875)
    out_weight = noise(arg_keys[7], (D, D), (D // 8) ** -0.5, 0.625)
    attn_gain = jnp.clip(1.0 + 0.1 * jax.random.normal(arg_keys[8], (D,), jnp.float32), 0.5, 1.5)
    ffn_gain = jnp.clip(1.0 + 0.1 * jax.random.normal(arg_keys[9], (D,), jnp.float32), 0.5, 1.5)
    up_weight = noise(arg_keys[10], (D, FF), D ** -0.5, 0.21875)
    down_weight = noise(arg_keys[11], (FF, D), FF ** -0.5, 0.21875)
    kernel_means = jnp.clip(jax.random.uniform(arg_keys[12], (KERNELS,), jnp.float32, 0.0, 10.0), 0.0, 10.0)
    kernel_widths = jnp.clip(jax.random.uniform(arg_keys[13], (KERNELS,), jnp.float32, 0.5, 3.0), 0.5, 3.0)
    kernel_inner = noise(arg_keys[14], (KERNELS, KERNELS), (KERNELS // 16) ** -0.5, 2.0)
    kernel_outer = noise(arg_keys[15], (KERNELS, HEADS), KERNELS ** -0.5, 0.5)
    hop_table = noise(arg_keys[16], (HEADS, HOPS), 0.5, 3.0)
    edge_table = noise(arg_keys[17], (HEADS, EDGE_KINDS), 0.5, 3.0)
    atom_scale = jnp.clip(jax.random.uniform(arg_keys[18], (ATOM_KINDS,), jnp.float32, 0.3, 0.7), 0.3, 0.7)
    atom_shift = jnp.clip(jax.random.uniform(arg_keys[19], (ATOM_KINDS,), jnp.float32, -0.5, 0.5), -0.5, 0.5)
    out_grad = noise(arg_keys[20], (BLOCKS_ALL, BLOCK_LEN, D), 1.0, 6.0, ((0, 8), (1, 4)))
    return dict(hidden_in=hidden_in, positions=positions, atom_types=atom_types, path_hops=path_hops, edge_kinds=edge_kinds, mol_lengths=mol_lengths, qkv_weight=qkv_weight, out_weight=out_weight, attn_gain=attn_gain, ffn_gain=ffn_gain, up_weight=up_weight, down_weight=down_weight, kernel_means=kernel_means, kernel_widths=kernel_widths, kernel_inner=kernel_inner, kernel_outer=kernel_outer, hop_table=hop_table, edge_table=edge_table, atom_scale=atom_scale, atom_shift=atom_shift, out_grad=out_grad)


EPS = 1e-05
NEG = -1000000000.0
SQRT_TWO_PI = 2.5066282746310002

@jax.custom_vjp
def low(v):
    return lax.optimization_barrier(v.astype(jnp.bfloat16)).astype(jnp.float32)

@jax.custom_vjp
def low_back(v):
    return v

def low_keep(v):
    return (low(v), None)

def low_pass(kept, grad):
    return (grad,)

def back_keep(v):
    return (v, None)

def back_low(kept, grad):
    return (low(grad),)
low.defvjp(low_keep, low_pass)
low_back.defvjp(back_keep, back_low)

def high_dot(left, right):
    return jnp.dot(left, right, precision=lax.Precision.HIGHEST)

def layer_norm(values, gain):
    centre = lax.optimization_barrier(jnp.mean(values, axis=-1, keepdims=True))
    shifted = values - centre
    spread = lax.optimization_barrier(jnp.mean(shifted * shifted, axis=-1, keepdims=True))
    return shifted * lax.rsqrt(spread + EPS) * gain

def gaussian(offset, kernel_means, kernel_widths):
    scaled = (offset[None] - kernel_means[:, None, None]) / kernel_widths[:, None, None]
    return jnp.exp(-0.5 * scaled * scaled) / (SQRT_TWO_PI * kernel_widths[:, None, None])

def pair_offset(pos_block, type_block):
    between = pos_block[:, :, None] - pos_block[:, None, :]
    distance = jnp.sqrt(lax.optimization_barrier(jnp.sum(between * between, axis=0)))
    return (type_block[0][:, None] + type_block[0][None, :]) * distance + type_block[1][:, None] + type_block[1][None, :]

def reference(hidden_in, positions, atom_types, path_hops, edge_kinds, mol_lengths, qkv_weight, out_weight, attn_gain, ffn_gain, up_weight, down_weight, kernel_means, kernel_widths, kernel_inner, kernel_outer, hop_table, edge_table, atom_scale, atom_shift, out_grad):
    f32 = jnp.float32
    block_count = hidden_in.shape[0]
    ends = jnp.cumsum(mol_lengths, axis=1)
    token_ids = jnp.arange(BLOCK_LEN, dtype=jnp.int32)
    molecule = lax.optimization_barrier(jnp.sum((token_ids[None, :, None] >= ends[:, None, :]).astype(jnp.int32), axis=2))
    pos_all = positions.astype(f32)
    scaling = HEAD_DIM ** (-0.5)
    primals = (hidden_in.astype(f32), qkv_weight.astype(f32), out_weight.astype(f32), attn_gain, ffn_gain, up_weight.astype(f32), down_weight.astype(f32), kernel_means, kernel_widths, kernel_inner.astype(f32), kernel_outer.astype(f32), hop_table.astype(f32), edge_table.astype(f32), atom_scale, atom_shift)

    def forward(layer_in, w_qkv, w_out, gain_one, gain_two, w_up, w_down, means, widths, inner_w, outer_w, hop_w, edge_w, scale_w, shift_w):
        normed1 = low(layer_norm(layer_in, gain_one))
        projected = high_dot(normed1.reshape(-1, D), w_qkv).reshape(block_count, BLOCK_LEN, 3 * D)
        projected = low(low_back(projected))
        type_terms = jnp.stack([scale_w[atom_types], shift_w[atom_types]], axis=1)

        def attention_block(inputs):
            proj_block, pos_block, type_block, hop_block, edge_block, mol_block = inputs
            query_rows = proj_block[:, :D].reshape(BLOCK_LEN, HEADS, HEAD_DIM)
            key_rows = proj_block[:, D:2 * D].reshape(BLOCK_LEN, HEADS, HEAD_DIM)
            value_rows = proj_block[:, 2 * D:].reshape(BLOCK_LEN, HEADS, HEAD_DIM)
            offset = pair_offset(pos_block, type_block)
            features = low(gaussian(offset, means, widths).reshape(KERNELS, -1))
            pre_act = low_back(high_dot(inner_w.T, features))
            hidden = low(jax.nn.gelu(pre_act))
            learned = low_back(high_dot(outer_w.T, hidden))
            table = jnp.take(hop_w, hop_block.reshape(-1), axis=1) + jnp.take(edge_w, edge_block.reshape(-1), axis=1)
            pair_bias = (learned + table).reshape(HEADS, BLOCK_LEN, BLOCK_LEN)
            raw = low_back(jnp.einsum('rhe,lhe->hrl', query_rows, key_rows, precision=lax.Precision.HIGHEST) * scaling)
            visible = mol_block[:, None] == mol_block[None, :]
            scores = jnp.where(visible[None], raw + pair_bias, NEG)
            peak = lax.optimization_barrier(jnp.max(scores, axis=-1, keepdims=True))
            weights = jnp.exp(scores - peak)
            probs = weights / lax.optimization_barrier(jnp.sum(weights, axis=-1, keepdims=True))
            mixed = jnp.einsum('hrl,lhe->rhe', low(probs), value_rows, precision=lax.Precision.HIGHEST).reshape(BLOCK_LEN, D)
            return low(low_back(mixed))
        attended = lax.map(jax.checkpoint(attention_block), (projected, pos_all, type_terms, path_hops, edge_kinds, molecule))
        branch = low_back(high_dot(attended.reshape(-1, D), w_out))
        middle = layer_in.reshape(-1, D) + branch
        normed2 = low(layer_norm(middle, gain_two))
        pre_ffn = low_back(high_dot(normed2, w_up))
        act = low(jax.nn.gelu(pre_ffn))
        result = middle + high_dot(act, w_down)
        return result.reshape(block_count, BLOCK_LEN, D)
    result, pullback = jax.vjp(forward, *primals)
    grads = pullback(out_grad.astype(f32))
    return (result.astype(jnp.bfloat16), grads[0], grads[1], grads[2], grads[3], grads[4], grads[5], grads[6], grads[7], grads[8], grads[9], grads[10], grads[11], grads[12], grads[13], grads[14])
```

```python
import functools

import jax
import jax.numpy as jnp
from jax import lax
from jax.experimental import pallas as pl
from jax.experimental.pallas import tpu as pltpu
from jax.sharding import PartitionSpec as P

EPS = 1e-05
NEG = -1000000000.0
SQRT_TWO_PI = 2.5066282746310002
SQRT_2_OVER_PI = 0.7978845608028654
CUBIC = 0.044715
LOG2E = 1.4426950408889634
F32 = jnp.float32
B16 = jnp.bfloat16
T = 128
W = 3 * T
D = 768
HEADS = 32
HD = 24
NN = (((1,), (0,)), ((), ()))
NT = (((1,), (1,)), ((), ()))
GROUPS = (
    (0, 1, (0, 1, 2, 3, 4)),
    (0, 2, (5,)),
    (1, 1, (6, 7, 8, 9)),
    (1, 2, (10,)),
    (2, 1, (11, 12, 13, 14, 15)),
)
CHUNK = 8
PAIRS = CHUNK * T


def mm(a, b, dims=NN):
    return lax.dot_general(a, b, dims, preferred_element_type=F32)


def gelu_parts(x):
    x2 = x * x
    t = jnp.tanh(x * (SQRT_2_OVER_PI + (SQRT_2_OVER_PI * CUBIC) * x2))
    half = 0.5 + 0.5 * t
    slope = half + (0.5 * x) * (1.0 - t * t) * (
        SQRT_2_OVER_PI + (3.0 * SQRT_2_OVER_PI * CUBIC) * x2
    )
    return x * half, slope


def normalise(v):
    centre = jnp.mean(v, axis=-1, keepdims=True)
    shifted = v - centre
    spread = jnp.mean(shifted * shifted, axis=-1, keepdims=True)
    rstd = lax.rsqrt(spread + EPS)
    return shifted * rstd, rstd


def norm_back(grad, xhat, rstd, gain):
    g = grad * gain
    return rstd * (
        g
        - jnp.mean(g, axis=-1, keepdims=True)
        - xhat * jnp.mean(g * xhat, axis=-1, keepdims=True)
    )


def down(row):
    return jnp.transpose(jnp.broadcast_to(row, (T, T)))


def compute_kernel(
    lens_ref,
    hid_ref,
    pos_ref,
    types_ref,
    hops_ref,
    edges_ref,
    wqkv_ref,
    wout_ref,
    g1_ref,
    g2_ref,
    wup_ref,
    wdown_ref,
    means_ref,
    widths_ref,
    inner_ref,
    outer_ref,
    hop_tab_ref,
    edge_tab_ref,
    scale_ref,
    shift_ref,
    cot_ref,
    out_ref,
    gmid_ref,
    gn1_ref,
    gqkv_ref,
    gout_ref,
    gg1_ref,
    gg2_ref,
    gup_ref,
    gdown_ref,
    gmw_ref,
    ginner_ref,
    gouter_ref,
    ghop_ref,
    gedge_ref,
    gtype_ref,
    n1t_ref,
    xhat_ref,
    rstd_ref,
    q_ref,
    k_ref,
    v_ref,
    m_ref,
    mb_ref,
    mt_ref,
    off_ref,
    dist_ref,
    hopi_ref,
    edgei_ref,
    cols_ref,
    w1_ref,
    w2_ref,
    innert_ref,
    feat_ref,
    hidden_ref,
    slope_ref,
    bias_ref,
    p_ref,
    mixed_ref,
    gmix_ref,
    gq_ref,
    gk_ref,
    gv_ref,
    goff_ref,
    lhsh_ref,
    lhse_ref,
    rhsh_ref,
    rhse_ref,
    gpre_ref,
):
    row = lax.axis_index("rows")
    rows = lax.axis_size("rows")
    x = hid_ref[...].astype(F32)
    xhat, rstd = normalise(x)
    xhat_ref[...] = xhat
    rstd_ref[...] = rstd
    n1 = (xhat * g1_ref[...]).astype(B16)
    for c in range(D // T):
        for t in range(3):
            n1t_ref[c * T : (c + 1) * T, t * T : (t + 1) * T] = jnp.transpose(
                n1[t * T : (t + 1) * T, c * T : (c + 1) * T]
            )
    q_ref[...] = mm(n1[T : 2 * T], wqkv_ref[:, :D]).astype(B16)
    k_ref[...] = mm(n1, wqkv_ref[:, D : 2 * D]).astype(B16)
    v_ref[...] = mm(n1, wqkv_ref[:, 2 * D :]).astype(B16)

    first = (row - 1) * T
    ids_row = first + lax.broadcasted_iota(jnp.int32, (1, W), 1)
    mol_row = jnp.zeros((1, W), jnp.int32)
    end = jnp.int32(0)
    for m in range(lens_ref.shape[1]):
        end = end + lens_ref[0, m]
        mol_row = mol_row + jnp.where(ids_row >= end, 1, 0)
    mol_row = jnp.where((ids_row >= 0) & (ids_row < rows * T), mol_row, -1).astype(F32)
    mol_own = mol_row[:, T : 2 * T]
    mol_col = down(mol_own)
    scale_col = jnp.concatenate(
        [down(scale_ref[:, c * T : (c + 1) * T]) for c in range(4)], axis=0
    )
    shift_col = jnp.concatenate(
        [down(shift_ref[:, c * T : (c + 1) * T]) for c in range(4)], axis=0
    )
    kinds = lax.broadcasted_iota(jnp.int32, (4 * T, T), 0)
    pos = pos_ref[...].astype(F32)
    sel = [jnp.zeros((T, T), F32) for _ in range(5)]
    own = None
    hop_sel = jnp.zeros((T, T), jnp.int32)
    edge_sel = jnp.zeros((T, T), jnp.int32)
    for t in range(3):
        lanes = slice(t * T, (t + 1) * T)
        mask = mol_col == jnp.broadcast_to(mol_row[:, lanes], (T, T))
        mask_t = down(mol_row[:, lanes]) == jnp.broadcast_to(mol_own, (T, T))
        m_ref[t] = mask.astype(F32)
        mb_ref[t] = mask.astype(F32).astype(B16)
        mt_ref[t] = mask_t.astype(F32).astype(B16)
        hit = kinds == types_ref[:, lanes]
        terms = (
            pos[0:1, lanes],
            pos[1:2, lanes],
            pos[2:3, lanes],
            jnp.sum(jnp.where(hit, scale_col, 0.0), axis=0, keepdims=True),
            jnp.sum(jnp.where(hit, shift_col, 0.0), axis=0, keepdims=True),
        )
        if t == 1:
            own = terms
        sel = [jnp.where(mask, v, s) for v, s in zip(terms, sel)]
        tile = jnp.clip(row + (t - 1), 0, rows - 1)
        at = pl.ds(pl.multiple_of(tile * T, T), T)
        hop_sel = jnp.where(mask, hops_ref[:, at], hop_sel)
        edge_sel = jnp.where(mask, edges_ref[:, at], edge_sel)
    ownc = [down(v) for v in own]
    dx, dy, dz = (ownc[c] - sel[c] for c in range(3))
    dist = jnp.sqrt(dx * dx + dy * dy + dz * dz)
    dist_ref[...] = dist
    off_ref[...] = (ownc[3] + sel[3]) * dist + ownc[4] + sel[4]
    hopi_ref[...] = hop_sel
    edgei_ref[...] = edge_sel

    mean_col = down(means_ref[...])
    inv_col = 1.0 / down(widths_ref[...])
    s_col = inv_col * ((0.5 * LOG2E) ** 0.5)
    cols_ref[0] = s_col
    cols_ref[1] = mean_col * s_col
    cols_ref[2] = jnp.log2(inv_col * (1.0 / SQRT_TWO_PI))
    cols_ref[3] = inv_col * (1.0 / (0.5 * LOG2E) ** 0.5)
    innert_ref[...] = jnp.transpose(inner_ref[...])
    outer_t = outer_ref[...]
    for g in range(4):
        w1_ref[g * HEADS : (g + 1) * HEADS, 0:T] = outer_t
        w1_ref[g * HEADS : (g + 1) * HEADS, T : 2 * T] = hop_tab_ref[:, g * T : (g + 1) * T]
    for g in range(12):
        w2_ref[g * HEADS : (g + 1) * HEADS, :] = edge_tab_ref[:, g * T : (g + 1) * T]

    iota_k = lax.broadcasted_iota(jnp.int32, (T, 2 * T), 0)

    def two(block, s):
        return jnp.concatenate([block[s : s + 1], block[s + 1 : s + 2]], axis=1)

    def wide(a):
        return jnp.concatenate([a, a], axis=1)

    def hot(index):
        return jnp.where(iota_k == (index & (T - 1)), 1.0, 0.0).astype(B16)

    def bias_step(c, _):
        at = pl.ds(pl.multiple_of(c * CHUNK, CHUNK), CHUNK)
        off8 = off_ref[at, :]
        hop8 = hopi_ref[at, :]
        edge8 = edgei_ref[at, :]
        for s in range(0, CHUNK, 2):
            lanes = pl.ds(pl.multiple_of(c * PAIRS + s * T, 2 * T), 2 * T)
            z = two(off8, s) * wide(cols_ref[0]) - wide(cols_ref[1])
            feat = jnp.exp2(wide(cols_ref[2]) - z * z).astype(B16)
            feat_ref[:, lanes] = feat
            pre = mm(innert_ref[...], feat)
            act, slope = gelu_parts(pre)
            hidden = act.astype(B16)
            hidden_ref[:, lanes] = hidden
            slope_ref[:, lanes] = slope
            hop = two(hop8, s)
            edge = two(edge8, s)
            low = mm(w1_ref[...], jnp.concatenate([hidden, hot(hop)], axis=0))
            high = mm(w2_ref[...], hot(edge))
            hop_g = jnp.broadcast_to(hop >> 7, (HEADS, 2 * T))
            edge_g = jnp.broadcast_to(edge >> 7, (HEADS, 2 * T))
            bias = low[0:HEADS]
            for g in range(1, 4):
                bias = jnp.where(hop_g == g, low[g * HEADS : (g + 1) * HEADS], bias)
            more = high[0:HEADS]
            for g in range(1, 12):
                more = jnp.where(edge_g == g, high[g * HEADS : (g + 1) * HEADS], more)
            bias = bias + more
            base = (c * CHUNK + s) * HEADS
            bias_ref[pl.ds(pl.multiple_of(base, HEADS), HEADS), :] = bias[:, :T]
            bias_ref[pl.ds(pl.multiple_of(base + HEADS, HEADS), HEADS), :] = bias[:, T:]
        return 0

    lax.fori_loop(0, T // CHUNK, bias_step, 0)

    scaling = HD ** (-0.5)

    def head_mask(h, tile, tiles):
        lane = lax.broadcasted_iota(jnp.int32, (1, tiles * T), 1) + tile * T
        return ((lane >= h * HD) & (lane < (h + 1) * HD)).astype(F32)

    def spread(low):
        return jnp.concatenate([low * mb_ref[t] for t in range(3)], axis=1)

    def compact(wide_scores):
        return jnp.where(
            m_ref[0] > 0,
            wide_scores[:, :T],
            jnp.where(m_ref[1] > 0, wide_scores[:, T : 2 * T], wide_scores[:, 2 * T :]),
        )

    for half in range(2):
        mixed_half = [None, None, None]
        for tile, tiles, heads in GROUPS:
            lanes = slice(half * W + tile * T, half * W + (tile + tiles) * T)
            masks = [head_mask(h, tile, tiles) for h in heads]
            q = q_ref[:, lanes]
            qm = jnp.concatenate([q * m.astype(B16) for m in masks], axis=0)
            raw = mm(qm, k_ref[:, lanes], NT)
            probs = []
            for a, h in enumerate(heads):
                head = half * 16 + h
                bias = bias_ref[pl.ds(head, T, stride=HEADS), :]
                visible = (m_ref[0] + m_ref[1] + m_ref[2]) > 0
                scores = jnp.where(
                    visible, compact(raw[a * T : (a + 1) * T]) * scaling + bias, NEG
                )
                peak = jnp.max(scores, axis=-1, keepdims=True)
                weights = jnp.exp(scores - peak)
                p = weights / jnp.sum(weights, axis=-1, keepdims=True)
                p_ref[head] = p
                probs.append(spread(p.astype(B16)))
            o = mm(jnp.concatenate(probs, axis=0), v_ref[:, lanes])
            total = o[:T] * masks[0]
            for a in range(1, len(heads)):
                total = total + o[a * T : (a + 1) * T] * masks[a]
            for j in range(tiles):
                part = total[:, j * T : (j + 1) * T]
                before = mixed_half[tile + j]
                mixed_half[tile + j] = part if before is None else before + part
        for j in range(3):
            mixed_ref[:, half * W + j * T : half * W + (j + 1) * T] = mixed_half[j].astype(B16)

    def tr(a):
        return jnp.concatenate(
            [jnp.transpose(a[:, c * T : (c + 1) * T]) for c in range(a.shape[1] // T)], axis=0
        )

    mixed = mixed_ref[...]
    middle = hid_ref[T : 2 * T, :].astype(F32) + mm(mixed, wout_ref[...])
    xhat2, rstd2 = normalise(middle)
    n2 = (xhat2 * g2_ref[...]).astype(B16)
    act, slope = gelu_parts(mm(n2, wup_ref[...]))
    act = act.astype(B16)
    out_ref[...] = (middle + mm(act, wdown_ref[...])).astype(B16)
    cot = cot_ref[...]
    gdown_ref[...] = mm(tr(act), cot)
    grad_pre = (mm(cot, wdown_ref[...], NT) * slope).astype(B16)
    gup_ref[...] = mm(tr(n2), grad_pre)
    gn2 = mm(grad_pre, wup_ref[...], NT)
    gg2_ref[...] = jnp.sum(gn2 * xhat2, axis=0, keepdims=True)
    gmid = cot.astype(F32) + norm_back(gn2, xhat2, rstd2, g2_ref[...])
    gmid_ref[...] = gmid
    branch = gmid.astype(B16)
    gout_ref[...] = mm(tr(mixed), branch)
    gmix_ref[...] = mm(branch, wout_ref[...], NT).astype(B16)

    def spread_t(low):
        return jnp.concatenate([low * mt_ref[t] for t in range(3)], axis=0)

    for half in range(2):
        gq_half = [None, None, None]
        gk_half = [None, None, None]
        gv_half = [None, None, None]

        def put(into, value, tile, tiles):
            for j in range(tiles):
                part = value[:, j * T : (j + 1) * T]
                before = into[tile + j]
                into[tile + j] = part if before is None else before + part

        for tile, tiles, heads in GROUPS:
            lanes = slice(half * W + tile * T, half * W + (tile + tiles) * T)
            masks = [head_mask(h, tile, tiles) for h in heads]
            q = q_ref[:, lanes]
            gm = gmix_ref[:, lanes]
            qm = jnp.concatenate([q * m.astype(B16) for m in masks], axis=0)
            gmm = jnp.concatenate([gm * m.astype(B16) for m in masks], axis=0)
            grad_p = mm(gmm, v_ref[:, lanes], NT)
            wide_g, tall_g, tall_p = [], [], []
            for a, h in enumerate(heads):
                head = half * 16 + h
                p = p_ref[head]
                dp = compact(grad_p[a * T : (a + 1) * T])
                gs = p * (dp - jnp.sum(p * dp, axis=-1, keepdims=True))
                bias_ref[pl.ds(head, T, stride=HEADS), :] = gs
                wide_g.append(spread(gs.astype(B16)))
                tall_g.append(spread_t(jnp.transpose(gs).astype(B16)))
                tall_p.append(spread_t(jnp.transpose(p).astype(B16)))
            o = mm(jnp.concatenate(wide_g, axis=0), k_ref[:, lanes])
            total = o[:T] * masks[0]
            for a in range(1, len(heads)):
                total = total + o[a * T : (a + 1) * T] * masks[a]
            put(gq_half, total, tile, tiles)
            put(gk_half, mm(jnp.concatenate(tall_g, axis=1), qm), tile, tiles)
            put(gv_half, mm(jnp.concatenate(tall_p, axis=1), gmm), tile, tiles)
        for j in range(3):
            lanes = slice(half * W + j * T, half * W + (j + 1) * T)
            gq_ref[:, lanes] = (gq_half[j] * scaling).astype(B16)
            gk_ref[:, lanes] = (gk_half[j] * scaling).astype(B16)
            gv_ref[:, lanes] = gv_half[j].astype(B16)

    n1t = n1t_ref[...]
    gqkv_ref[:, :D] = mm(n1t[:, T : 2 * T], gq_ref[...])
    gqkv_ref[:, D : 2 * D] = mm(n1t, gk_ref[...])
    gqkv_ref[:, 2 * D :] = mm(n1t, gv_ref[...])
    gn1 = mm(gk_ref[...], wqkv_ref[:, D : 2 * D], NT) + mm(gv_ref[...], wqkv_ref[:, 2 * D :], NT)
    gn1_own = gn1[T : 2 * T] + mm(gq_ref[...], wqkv_ref[:, :D], NT)
    gn1_ref[0:T] = gn1[:T]
    gn1_ref[T : 2 * T] = gn1_own
    gn1_ref[2 * T :] = gn1[2 * T :]
    gg1_ref[...] = jnp.sum(gn1_ref[...] * xhat_ref[...], axis=0, keepdims=True)

    gmw_ref[...] = jnp.zeros_like(gmw_ref)
    ginner_ref[...] = jnp.zeros_like(ginner_ref)
    ghop_ref[...] = jnp.zeros_like(ghop_ref)
    gedge_ref[...] = jnp.zeros_like(gedge_ref)

    def back_step(c, _):
        at = pl.ds(pl.multiple_of(c * CHUNK, CHUNK), CHUNK)
        off8 = off_ref[at, :]
        hop8 = hopi_ref[at, :]
        edge8 = edgei_ref[at, :]
        goff = []
        sums = [jnp.zeros((T, T), F32) for _ in range(3)]
        for s in range(0, CHUNK, 2):
            here = slice(s * T, (s + 2) * T)
            lanes = pl.ds(pl.multiple_of(c * PAIRS + s * T, 2 * T), 2 * T)
            base = (c * CHUNK + s) * HEADS
            gs = jnp.concatenate(
                [
                    bias_ref[pl.ds(pl.multiple_of(base, HEADS), HEADS), :],
                    bias_ref[pl.ds(pl.multiple_of(base + HEADS, HEADS), HEADS), :],
                ],
                axis=1,
            )
            hop = two(hop8, s)
            edge = two(edge8, s)
            hop_g = jnp.broadcast_to(hop >> 7, (HEADS, 2 * T))
            edge_g = jnp.broadcast_to(edge >> 7, (HEADS, 2 * T))
            for g in range(4):
                lhsh_ref[g * HEADS : (g + 1) * HEADS, here] = jnp.where(hop_g == g, gs, 0.0).astype(B16)
            for g in range(12):
                lhse_ref[g * HEADS : (g + 1) * HEADS, here] = jnp.where(edge_g == g, gs, 0.0).astype(B16)
            rhsh_ref[0:T, here] = hot(hop)
            rhsh_ref[T : 2 * T, here] = hidden_ref[:, lanes]
            rhse_ref[:, here] = hot(edge)
            grad_hidden = mm(outer_ref[...], gs.astype(B16), (((0,), (0,)), ((), ())))
            gpre = (grad_hidden * slope_ref[:, lanes]).astype(B16)
            gpre_ref[:, here] = gpre
            gfeat = mm(inner_ref[...], gpre)
            z = two(off8, s) * wide(cols_ref[0]) - wide(cols_ref[1])
            a = gfeat * jnp.exp2(wide(cols_ref[2]) - z * z)
            az = a * z
            azz = az * z
            goff.append(jnp.sum(az * wide(cols_ref[3]), axis=0, keepdims=True))
            sums[0] = sums[0] + az[:, :T] + az[:, T:]
            sums[1] = sums[1] + azz[:, :T] + azz[:, T:]
            sums[2] = sums[2] + a[:, :T] + a[:, T:]
        for n in range(3):
            gmw_ref[n] = gmw_ref[n] + sums[n]
        goff_ref[at, :] = jnp.concatenate(
            [-g[:, n * T : (n + 1) * T] for g in goff for n in range(2)], axis=0
        ) * (LOG2E ** 0.0)
        ghop_ref[...] += mm(lhsh_ref[...], rhsh_ref[...], NT)
        gedge_ref[...] += mm(lhse_ref[...], rhse_ref[...], NT)
        ginner_ref[...] += mm(
            feat_ref[:, pl.ds(pl.multiple_of(c * PAIRS, PAIRS), PAIRS)], gpre_ref[...], NT
        )
        return 0

    lax.fori_loop(0, T // CHUNK, back_step, 0)
    gouter_ref[...] = (
        ghop_ref[0:32, T:] + ghop_ref[32:64, T:] + ghop_ref[64:96, T:] + ghop_ref[96:128, T:]
    )

    goff = goff_ref[...]
    gdist = goff * dist_ref[...]
    flat = []
    for value in (gdist, goff):
        query = jnp.sum(jnp.transpose(value), axis=0, keepdims=True)
        parts = [jnp.sum(value * m_ref[t], axis=0, keepdims=True) for t in range(3)]
        parts[1] = parts[1] + query
        flat.append(parts)
    for n in range(2):
        acc = jnp.zeros((4 * T, T), F32)
        for t in range(3):
            hit = kinds == types_ref[:, t * T : (t + 1) * T]
            acc = acc + jnp.where(hit, flat[n][t], 0.0)
        gtype_ref[n : n + 1, :] = jnp.concatenate(
            [
                jnp.sum(jnp.transpose(acc[c * T : (c + 1) * T]), axis=0, keepdims=True)
                for c in range(4)
            ],
            axis=1,
        )


def run_compute(args):
    vm = pltpu.VMEM
    out_shape = [
        jax.ShapeDtypeStruct((T, D), B16),
        jax.ShapeDtypeStruct((T, D), F32),
        jax.ShapeDtypeStruct((W, D), F32),
        jax.ShapeDtypeStruct((D, 3 * D), F32),
        jax.ShapeDtypeStruct((D, D), F32),
        jax.ShapeDtypeStruct((1, D), F32),
        jax.ShapeDtypeStruct((1, D), F32),
        jax.ShapeDtypeStruct((D, D), F32),
        jax.ShapeDtypeStruct((D, D), F32),
        jax.ShapeDtypeStruct((3, T, T), F32),
        jax.ShapeDtypeStruct((T, T), F32),
        jax.ShapeDtypeStruct((HEADS, T), F32),
        jax.ShapeDtypeStruct((T, 2 * T), F32),
        jax.ShapeDtypeStruct((3 * T, T), F32),
        jax.ShapeDtypeStruct((2, 4 * T), F32),
    ]
    scratch = [
        vm((D, W), B16),
        vm((W, D), F32),
        vm((W, 1), F32),
        vm((T, D), B16),
        vm((W, D), B16),
        vm((W, D), B16),
        vm((3, T, T), F32),
        vm((3, T, T), B16),
        vm((3, T, T), B16),
        vm((T, T), F32),
        vm((T, T), F32),
        vm((T, T), jnp.int32),
        vm((T, T), jnp.int32),
        vm((4, T, T), F32),
        vm((T, 2 * T), B16),
        vm((3 * T, T), B16),
        vm((T, T), B16),
        vm((T, T * T), B16),
        vm((T, T * T), B16),
        vm((T, T * T), F32),
        vm((T * HEADS, T), F32),
        vm((HEADS, T, T), F32),
        vm((T, D), B16),
        vm((T, D), B16),
        vm((T, D), B16),
        vm((W, D), B16),
        vm((W, D), B16),
        vm((T, T), F32),
        vm((T, PAIRS), B16),
        vm((3 * T, PAIRS), B16),
        vm((2 * T, PAIRS), B16),
        vm((T, PAIRS), B16),
        vm((T, PAIRS), B16),
    ]
    vspec = pl.BlockSpec(memory_space=pltpu.VMEM)
    sspec = pl.BlockSpec(memory_space=pltpu.SMEM)
    return pl.pallas_call(
        compute_kernel,
        out_shape=out_shape,
        in_specs=[sspec] + [vspec] * (len(args) - 1),
        out_specs=[vspec] * len(out_shape),
        scratch_shapes=scratch,
        compiler_params=pltpu.CompilerParams(vmem_limit_bytes=60 * 1024 * 1024),
        name="layer",
    )(*args)


def body(
    hidden_in,
    positions,
    atom_types,
    path_hops,
    edge_kinds,
    mol_lengths,
    qkv_weight,
    out_weight,
    attn_gain,
    ffn_gain,
    up_weight,
    down_weight,
    kernel_means,
    kernel_widths,
    kernel_inner,
    kernel_outer,
    hop_table,
    edge_table,
    atom_scale,
    atom_shift,
    out_grad,
):
    rows = lax.axis_size("rows")
    up = [(i, i + 1) for i in range(rows - 1)]
    back = [(i + 1, i) for i in range(rows - 1)]

    def window(value, axis):
        return jnp.concatenate(
            [lax.ppermute(value, "rows", up), value, lax.ppermute(value, "rows", back)], axis=axis
        )

    hid_w = window(hidden_in[0], 0)
    pos_w = window(positions[0], 1)
    types_w = window(atom_types, 1)
    (
        out, gmid, gn1, gqkv, gout, gg1, gg2, gup, gdown, gmw, ginner, gouter_t, ghop, gedge, gtype,
    ) = run_compute(
        (
            mol_lengths,
            hid_w,
            pos_w,
            types_w,
            path_hops[0],
            edge_kinds[0],
            qkv_weight,
            out_weight,
            attn_gain[None],
            ffn_gain[None],
            up_weight,
            down_weight,
            kernel_means[None],
            kernel_widths[None],
            kernel_inner,
            kernel_outer.T,
            hop_table,
            edge_table,
            atom_scale[None],
            atom_shift[None],
            out_grad[0],
        )
    )
    from_above = lax.ppermute(gn1[:T], "rows", back)
    from_below = lax.ppermute(gn1[2 * T :], "rows", up)
    gn1_own = gn1[T : 2 * T] + from_above + from_below
    xhat, rstd = normalise(hidden_in[0].astype(F32))
    grad_in = gmid + norm_back(gn1_own, xhat, rstd, attn_gain)
    inv = 1.0 / kernel_widths
    back_scale = (2.0 / LOG2E) ** 0.5
    sums = jnp.sum(gmw, axis=2)
    grad_means = sums[0] * inv * back_scale
    grad_widths = (sums[1] * (back_scale * back_scale) - sums[2]) * inv
    ghop_own = jnp.concatenate([ghop[g * HEADS : (g + 1) * HEADS, :T] for g in range(4)], axis=1)
    gedge_own = jnp.concatenate([gedge[g * HEADS : (g + 1) * HEADS] for g in range(12)], axis=1)
    summed = lax.psum(
        (
            gqkv, gout, gg1[0], gg2[0], gup, gdown, grad_means, grad_widths, ginner, gouter_t.T,
            ghop_own, gedge_own, gtype[0], gtype[1],
        ),
        ("blocks", "rows"),
    )
    return (out[None], grad_in[None]) + tuple(summed)


def solution(mesh):
    split3 = P("blocks", "rows", None)
    in_specs = (
        split3,
        P("blocks", None, "rows"),
        P("blocks", "rows"),
        split3,
        split3,
        P("blocks", None),
    ) + (P(),) * 14 + (split3,)
    out_specs = (split3, split3) + (P(),) * 14
    return jax.shard_map(body, mesh=mesh, in_specs=in_specs, out_specs=out_specs, check_vma=False)
```

```python
import functools

import jax
import jax.numpy as jnp
from jax import lax
from jax.experimental import pallas as pl
from jax.experimental.pallas import tpu as pltpu
from jax.sharding import PartitionSpec as P

EPS = 1e-05
NEG = -1000000000.0
SQRT_TWO_PI = 2.5066282746310002
SQRT_2_OVER_PI = 0.7978845608028654
CUBIC = 0.044715
LOG2E = 1.4426950408889634
F32 = jnp.float32
B16 = jnp.bfloat16
T = 128
W = 3 * T
D = 768
HEADS = 32
HD = 24
NN = (((1,), (0,)), ((), ()))
NT = (((1,), (1,)), ((), ()))
GROUPS = (
    (0, 1, (0, 1, 2, 3, 4)),
    (0, 2, (5,)),
    (1, 1, (6, 7, 8, 9)),
    (1, 2, (10,)),
    (2, 1, (11, 12, 13, 14, 15)),
)
CHUNK = 8
PAIRS = CHUNK * T


def mm(a, b, dims=NN):
    return lax.dot_general(a, b, dims, preferred_element_type=F32)


def gelu_parts(x):
    x2 = x * x
    t = jnp.tanh(x * (SQRT_2_OVER_PI + (SQRT_2_OVER_PI * CUBIC) * x2))
    half = 0.5 + 0.5 * t
    slope = half + (0.5 * x) * (1.0 - t * t) * (
        SQRT_2_OVER_PI + (3.0 * SQRT_2_OVER_PI * CUBIC) * x2
    )
    return x * half, slope


def normalise(v):
    centre = jnp.mean(v, axis=-1, keepdims=True)
    shifted = v - centre
    spread = jnp.mean(shifted * shifted, axis=-1, keepdims=True)
    rstd = lax.rsqrt(spread + EPS)
    return shifted * rstd, rstd


def norm_back(grad, xhat, rstd, gain):
    g = grad * gain
    return rstd * (
        g
        - jnp.mean(g, axis=-1, keepdims=True)
        - xhat * jnp.mean(g * xhat, axis=-1, keepdims=True)
    )


def down(row):
    return jnp.transpose(jnp.broadcast_to(row, (T, T)))


def z_split():
    count = lax.axis_size("blocks") // 2
    inner = min(count, 4)
    return inner, count // inner


def start_all(copies):
    for copy in copies:
        copy.start()


class Chain:
    def __init__(self, place, src, r0, r1, r2, rz, ro, final, out, send, recv, local, swap):
        c, x, y, z, inner, outer = place
        self.inner, self.outer = inner, outer
        self.zi = z % inner
        row, block = 2 * x + c, 2 * z + y
        pc = (block, 2 * x + 1 - c)
        px = (block, 2 * (1 - x) + c)
        py = (2 * z + 1 - y, row)
        self.bits = (c, y, x) if swap else (c, x, y)
        self.partners = (pc, py, px) if swap else (pc, px, py)
        self.peers = [
            (2 * (z - self.zi + (self.zi + k) % inner) + y, row) for k in range(1, inner)
        ]
        self.far = [
            (2 * (self.zi + inner * ((z // inner + k) % outer)) + y, row) for k in range(1, outer)
        ]
        self.src, self.bufs, self.rz, self.ro = src, (r0, r1, r2), rz, ro
        self.final, self.out = final, out
        self.send, self.recv, self.local = send, recv, local
        self.starts, self.sizes = [0], [src.shape[0]]
        for bit in self.bits:
            half = self.sizes[-1] // 2
            self.starts.append(self.starts[-1] + bit * half)
            self.sizes.append(half)
        self.piece = self.sizes[-1] // inner
        self.mine = self.starts[3] + self.zi * self.piece
        self.flying = []
        self.used = 0
        self.todo = [self.scatter(0), self.scatter(1), self.scatter(2), self.scatter_z]
        if outer > 1:
            self.todo += [self.exchange]
        self.todo += [self.gather_z, self.gather(2), self.gather(1), self.gather(0)]
        self.left = len(self.todo) + 1

    @staticmethod
    def at(start, size):
        return pl.ds(pl.multiple_of(start, 16), size)

    def go(self, src, dst, device):
        copy = pltpu.make_async_remote_copy(
            src_ref=src,
            dst_ref=dst,
            send_sem=self.send.at[self.used],
            recv_sem=self.recv.at[self.used],
            device_id=device,
            device_id_type=pl.DeviceIdType.MESH,
        )
        self.used += 1
        copy.start()
        self.flying.append(copy)

    def add(self, start, size, others, into=None):
        block = 16
        while block < 128 and size % (2 * block) == 0:
            block *= 2

        def one(i, _):
            here = pl.ds(pl.multiple_of(i * block, 16), block)
            there = self.at(start + i * block, block)
            total = self.src[there, :].astype(F32)
            for other in others:
                total = total + other[here, :].astype(F32)
            if into is None:
                self.src[there, :] = total.astype(B16)
            else:
                into[here, :] = total.astype(B16)
            return 0

        lax.fori_loop(0, size // block, one, 0)

    def scatter(self, k):
        def run():
            if k > 0:
                self.add(self.starts[k], self.sizes[k], [self.bufs[k - 1]])
            half = self.sizes[k + 1]
            start = self.starts[k] + (1 - self.bits[k]) * half
            self.go(self.src.at[self.at(start, half)], self.bufs[k], self.partners[k])

        return run

    def scatter_z(self):
        self.add(self.starts[3], self.sizes[3], [self.bufs[2]])
        for k, peer in enumerate(self.peers):
            start = self.starts[3] + ((self.zi + k + 1) % self.inner) * self.piece
            self.go(self.src.at[self.at(start, self.piece)], self.rz.at[k], peer)

    def exchange(self):
        self.add(self.mine, self.piece, [self.rz.at[k] for k in range(self.inner - 1)])
        for k, peer in enumerate(self.far):
            self.go(self.src.at[self.at(self.mine, self.piece)], self.ro.at[k], peer)

    def gather_z(self):
        last, count = (self.ro, self.outer) if self.outer > 1 else (self.rz, self.inner)
        self.add(self.mine, self.piece, [last.at[k] for k in range(count - 1)], self.final)
        where = self.at(self.mine, self.piece)
        own = pltpu.make_async_copy(self.final, self.out.at[where], self.local)
        own.start()
        self.flying.append(own)
        for peer in self.peers:
            self.go(self.final, self.out.at[where], peer)

    def gather(self, k):
        def run():
            where = self.at(self.starts[k + 1], self.sizes[k + 1])
            self.go(self.out.at[where], self.out.at[where], self.partners[k])

        return run

    def step(self):
        for copy in self.flying:
            copy.wait()
        self.flying = []
        self.left -= 1
        if self.todo:
            self.todo.pop(0)()


def compute_kernel(
    lens_ref,
    own_ref,
    pos_ref,
    types_in_ref,
    hops_ref,
    edges_ref,
    wqkv_ref,
    wout_ref,
    g1_ref,
    g2_ref,
    wup_ref,
    wdown_ref,
    means_ref,
    widths_ref,
    inner_ref,
    outer_ref,
    hop_tab_ref,
    edge_tab_ref,
    scale_ref,
    shift_ref,
    cot_ref,
    out_ref,
    gin_ref,
    *rest,
):
    sums_out, rest = rest[:7], rest[7:]
    (
        hid_ref, geo_own_ref, geo_ref, gn1_send_ref, gn1_recv_ref, halo_send, halo_recv,
        n1t_ref, xhat_ref, rstd_ref, q_ref, k_ref, v_ref, m_ref, mb_ref, mt_ref, off_ref, dist_ref,
        hopi_ref, edgei_ref, cols_ref, w1_ref, w2_ref, innert_ref, feat_ref, hidden_ref, slope_ref,
        bias_ref, p_ref, mixed_ref, gmix_ref, gq_ref, gk_ref, gv_ref, goff_ref, lhsh_ref, lhse_ref,
        rhsh_ref, rhse_ref, gpre_ref, gmid_ref, gmw_ref, ginner_ref, ghop_ref, gedge_ref, gg2_ref, gg1_ref, gn1_ref, n1_ref,
    ) = rest[:49]
    rest = rest[49:]
    row = lax.axis_index("rows")
    rows = lax.axis_size("rows")
    block = lax.axis_index("blocks")
    inner, outer = z_split()
    place = (row % 2, row // 2, block % 2, block // 2, inner, outer)
    chains = []
    for n in range(7):
        src, r0, r1, r2, rz, ro, final, send, recv, local = rest[10 * n : 10 * n + 10]
        chains.append(
            Chain(place, src, r0, r1, r2, rz, ro, final, sums_out[n], send, recv, local, n % 2 == 1)
        )

    barrier = pltpu.get_barrier_semaphore()
    others = [(block, (row + k) % rows) for k in range(1, rows)]
    others += [chains[0].partners[2]] + chains[0].peers + chains[0].far
    for other in others:
        pl.semaphore_signal(barrier, inc=1, device_id=other, device_id_type=pl.DeviceIdType.MESH)
    pl.semaphore_wait(barrier, len(others))

    geo_own_ref[...] = jnp.concatenate(
        [pos_ref[...].astype(F32), types_in_ref[...].astype(F32), jnp.zeros((4, T), F32)], axis=0
    )
    next_row, last_row = (block, (row + 1) % rows), (block, (row + rows - 1) % rows)

    def halo(src, dst, n, device):
        return pltpu.make_async_remote_copy(
            src_ref=src,
            dst_ref=dst,
            send_sem=halo_send.at[n],
            recv_sem=halo_recv.at[n],
            device_id=device,
            device_id_type=pl.DeviceIdType.MESH,
        )

    halos = [
        halo(geo_own_ref, geo_ref.at[0], 0, next_row),
        halo(geo_own_ref, geo_ref.at[1], 1, last_row),
        halo(own_ref, hid_ref.at[0], 2, next_row),
        halo(own_ref, hid_ref.at[1], 3, last_row),
    ]
    start_all(halos)

    for copy in halos:
        copy.wait()
    geo = jnp.concatenate([geo_ref[0], geo_own_ref[...], geo_ref[1]], axis=1)
    pos = geo[0:3]
    types = geo[3:4].astype(jnp.int32)
    for t, tile_ref in enumerate((hid_ref.at[0], own_ref, hid_ref.at[1])):
        here = slice(t * T, (t + 1) * T)
        xhat, rstd = normalise(tile_ref[...].astype(F32))
        xhat_ref[here, :] = xhat
        rstd_ref[here, :] = rstd
        n1_ref[here, :] = (xhat * g1_ref[...]).astype(B16)
        for c in range(D // T):
            n1t_ref[c * T : (c + 1) * T, here] = jnp.transpose(n1_ref[here, c * T : (c + 1) * T])
    for j in range(0, D, 2 * T):
        here = slice(j, j + 2 * T)
        q_ref[:, here] = mm(n1_ref[T : 2 * T, :], wqkv_ref[:, here]).astype(B16)
        k_ref[:, here] = mm(n1_ref[...], wqkv_ref[:, D + j : D + j + 2 * T]).astype(B16)
        v_ref[:, here] = mm(n1_ref[...], wqkv_ref[:, 2 * D + j : 2 * D + j + 2 * T]).astype(B16)

    first = (row - 1) * T
    ids_row = first + lax.broadcasted_iota(jnp.int32, (1, W), 1)
    mol_row = jnp.zeros((1, W), jnp.int32)
    end = jnp.int32(0)
    for m in range(lens_ref.shape[1]):
        end = end + lens_ref[0, m]
        mol_row = mol_row + jnp.where(ids_row >= end, 1, 0)
    mol_row = jnp.where((ids_row >= 0) & (ids_row < rows * T), mol_row, -1).astype(F32)
    mol_own = mol_row[:, T : 2 * T]
    mol_col = down(mol_own)
    scale_col = jnp.concatenate(
        [down(scale_ref[:, c * T : (c + 1) * T]) for c in range(4)], axis=0
    )
    shift_col = jnp.concatenate(
        [down(shift_ref[:, c * T : (c + 1) * T]) for c in range(4)], axis=0
    )
    kinds = lax.broadcasted_iota(jnp.int32, (4 * T, T), 0)
    sel = [jnp.zeros((T, T), F32) for _ in range(5)]
    own = None
    hop_sel = jnp.zeros((T, T), jnp.int32)
    edge_sel = jnp.zeros((T, T), jnp.int32)
    for t in range(3):
        lanes = slice(t * T, (t + 1) * T)
        mask = mol_col == jnp.broadcast_to(mol_row[:, lanes], (T, T))
        mask_t = down(mol_row[:, lanes]) == jnp.broadcast_to(mol_own, (T, T))
        m_ref[t] = mask.astype(F32)
        mb_ref[t] = mask.astype(F32).astype(B16)
        mt_ref[t] = mask_t.astype(F32).astype(B16)
        hit = kinds == types[:, lanes]
        terms = (
            pos[0:1, lanes],
            pos[1:2, lanes],
            pos[2:3, lanes],
            jnp.sum(jnp.where(hit, scale_col, 0.0), axis=0, keepdims=True),
            jnp.sum(jnp.where(hit, shift_col, 0.0), axis=0, keepdims=True),
        )
        if t == 1:
            own = terms
        sel = [jnp.where(mask, v, s) for v, s in zip(terms, sel)]
        tile = (row + (t - 1 + rows)) % rows
        at = pl.ds(pl.multiple_of(tile * T, T), T)
        hop_sel = jnp.where(mask, hops_ref[:, at], hop_sel)
        edge_sel = jnp.where(mask, edges_ref[:, at], edge_sel)
    ownc = [down(v) for v in own]
    dx, dy, dz = (ownc[c] - sel[c] for c in range(3))
    dist = jnp.sqrt(dx * dx + dy * dy + dz * dz)
    dist_ref[...] = dist
    off_ref[...] = (ownc[3] + sel[3]) * dist + ownc[4] + sel[4]
    hopi_ref[...] = hop_sel
    edgei_ref[...] = edge_sel

    mean_col = down(means_ref[...])
    inv_col = 1.0 / down(widths_ref[...])
    s_col = inv_col * ((0.5 * LOG2E) ** 0.5)
    cols_ref[0] = s_col
    cols_ref[1] = mean_col * s_col
    cols_ref[2] = jnp.log2(inv_col * (1.0 / SQRT_TWO_PI))
    cols_ref[3] = inv_col * (1.0 / (0.5 * LOG2E) ** 0.5)
    innert_ref[...] = jnp.transpose(inner_ref[...])
    outer_t = outer_ref[...]
    for g in range(4):
        w1_ref[g * HEADS : (g + 1) * HEADS, 0:T] = outer_t
        w1_ref[g * HEADS : (g + 1) * HEADS, T : 2 * T] = hop_tab_ref[:, g * T : (g + 1) * T]
    for g in range(12):
        w2_ref[g * HEADS : (g + 1) * HEADS, :] = edge_tab_ref[:, g * T : (g + 1) * T]

    iota_k = lax.broadcasted_iota(jnp.int32, (T, 2 * T), 0)

    def two(block, s):
        return jnp.concatenate([block[s : s + 1], block[s + 1 : s + 2]], axis=1)

    def wide(a):
        return jnp.concatenate([a, a], axis=1)

    def hot(index):
        return jnp.where(iota_k == (index & (T - 1)), 1.0, 0.0).astype(B16)

    def bias_step(c, _):
        at = pl.ds(pl.multiple_of(c * CHUNK, CHUNK), CHUNK)
        off8 = off_ref[at, :]
        hop8 = hopi_ref[at, :]
        edge8 = edgei_ref[at, :]
        for s in range(0, CHUNK, 2):
            lanes = pl.ds(pl.multiple_of(c * PAIRS + s * T, 2 * T), 2 * T)
            z = two(off8, s) * wide(cols_ref[0]) - wide(cols_ref[1])
            feat = jnp.exp2(wide(cols_ref[2]) - z * z).astype(B16)
            feat_ref[:, lanes] = feat
            pre = mm(innert_ref[...], feat)
            act, slope = gelu_parts(pre)
            hidden = act.astype(B16)
            hidden_ref[:, lanes] = hidden
            slope_ref[:, lanes] = slope
            hop = two(hop8, s)
            edge = two(edge8, s)
            low = mm(w1_ref[...], jnp.concatenate([hidden, hot(hop)], axis=0))
            high = mm(w2_ref[...], hot(edge))
            hop_g = jnp.broadcast_to(hop >> 7, (HEADS, 2 * T))
            edge_g = jnp.broadcast_to(edge >> 7, (HEADS, 2 * T))
            bias = low[0:HEADS]
            for g in range(1, 4):
                bias = jnp.where(hop_g == g, low[g * HEADS : (g + 1) * HEADS], bias)
            more = high[0:HEADS]
            for g in range(1, 12):
                more = jnp.where(edge_g == g, high[g * HEADS : (g + 1) * HEADS], more)
            bias = bias + more
            base = (c * CHUNK + s) * HEADS
            bias_ref[pl.ds(pl.multiple_of(base, HEADS), HEADS), :] = bias[:, :T]
            bias_ref[pl.ds(pl.multiple_of(base + HEADS, HEADS), HEADS), :] = bias[:, T:]
        return 0

    lax.fori_loop(0, T // CHUNK, bias_step, 0)

    scaling = HD ** (-0.5)

    def head_mask(h, tile, tiles):
        lane = lax.broadcasted_iota(jnp.int32, (1, tiles * T), 1) + tile * T
        return ((lane >= h * HD) & (lane < (h + 1) * HD)).astype(F32)

    def spread(low):
        return jnp.concatenate([low * mb_ref[t] for t in range(3)], axis=1)

    def compact(wide_scores):
        return jnp.where(
            m_ref[0] > 0,
            wide_scores[:, :T],
            jnp.where(m_ref[1] > 0, wide_scores[:, T : 2 * T], wide_scores[:, 2 * T :]),
        )

    def attend(half, _):
        mixed_half = [None, None, None]
        for tile, tiles, heads in GROUPS:
            lanes = pl.ds(pl.multiple_of(half * W + tile * T, T), tiles * T)
            masks = [head_mask(h, tile, tiles) for h in heads]
            q = q_ref[:, lanes]
            qm = jnp.concatenate([q * m.astype(B16) for m in masks], axis=0)
            raw = mm(qm, k_ref[:, lanes], NT)
            probs = []
            for a, h in enumerate(heads):
                head = half * 16 + h
                bias = bias_ref[pl.ds(head, T, stride=HEADS), :]
                visible = (m_ref[0] + m_ref[1] + m_ref[2]) > 0
                scores = jnp.where(
                    visible, compact(raw[a * T : (a + 1) * T]) * scaling + bias, NEG
                )
                peak = jnp.max(scores, axis=-1, keepdims=True)
                weights = jnp.exp(scores - peak)
                p = weights / jnp.sum(weights, axis=-1, keepdims=True)
                p_ref[head] = p
                probs.append(spread(p.astype(B16)))
            o = mm(jnp.concatenate(probs, axis=0), v_ref[:, lanes])
            total = o[:T] * masks[0]
            for a in range(1, len(heads)):
                total = total + o[a * T : (a + 1) * T] * masks[a]
            for j in range(tiles):
                part = total[:, j * T : (j + 1) * T]
                before = mixed_half[tile + j]
                mixed_half[tile + j] = part if before is None else before + part
        for j in range(3):
            mixed_ref[:, pl.ds(pl.multiple_of(half * W + j * T, T), T)] = mixed_half[j].astype(B16)
        return 0

    lax.fori_loop(0, 2, attend, 0)

    def tr(a):
        return jnp.concatenate(
            [jnp.transpose(a[:, c * T : (c + 1) * T]) for c in range(a.shape[1] // T)], axis=0
        )

    mixed = mixed_ref[...]
    middle = own_ref[...].astype(F32) + mm(mixed, wout_ref[...])
    xhat2, rstd2 = normalise(middle)
    n2 = (xhat2 * g2_ref[...]).astype(B16)
    act, slope = gelu_parts(mm(n2, wup_ref[...]))
    act = act.astype(B16)
    out_ref[...] = (middle + mm(act, wdown_ref[...])).astype(B16)
    cot = cot_ref[...]

    def fill(n, left, right):
        for j in range(0, D // T, 2):
            both = mm(left, right[:, j * T : (j + 2) * T]).astype(B16)
            chains[n].src[j * D : (j + 1) * D, :] = both[:, :T]
            chains[n].src[(j + 1) * D : (j + 2) * D, :] = both[:, T:]

    fill(0, tr(act), cot)
    chains[0].step()
    grad_pre = (mm(cot, wdown_ref[...], NT) * slope).astype(B16)
    fill(1, tr(n2), grad_pre)
    chains[1].step()
    gn2 = mm(grad_pre, wup_ref[...], NT)
    gg2_ref[...] = jnp.sum(gn2 * xhat2, axis=0, keepdims=True)
    gmid = cot.astype(F32) + norm_back(gn2, xhat2, rstd2, g2_ref[...])
    gmid_ref[...] = gmid
    branch = gmid.astype(B16)
    fill(2, tr(mixed), branch)
    chains[2].step()
    gmix_ref[...] = mm(branch, wout_ref[...], NT).astype(B16)

    def spread_t(low):
        return jnp.concatenate([low * mt_ref[t] for t in range(3)], axis=0)

    def attend_back(half, _):
        gq_half = [None, None, None]
        gk_half = [None, None, None]
        gv_half = [None, None, None]

        def put(into, value, tile, tiles):
            for j in range(tiles):
                part = value[:, j * T : (j + 1) * T]
                before = into[tile + j]
                into[tile + j] = part if before is None else before + part

        for tile, tiles, heads in GROUPS:
            lanes = pl.ds(pl.multiple_of(half * W + tile * T, T), tiles * T)
            masks = [head_mask(h, tile, tiles) for h in heads]
            q = q_ref[:, lanes]
            gm = gmix_ref[:, lanes]
            qm = jnp.concatenate([q * m.astype(B16) for m in masks], axis=0)
            gmm = jnp.concatenate([gm * m.astype(B16) for m in masks], axis=0)
            grad_p = mm(gmm, v_ref[:, lanes], NT)
            wide_g, tall_g, tall_p = [], [], []
            for a, h in enumerate(heads):
                head = half * 16 + h
                p = p_ref[head]
                dp = compact(grad_p[a * T : (a + 1) * T])
                gs = p * (dp - jnp.sum(p * dp, axis=-1, keepdims=True))
                bias_ref[pl.ds(head, T, stride=HEADS), :] = gs
                wide_g.append(spread(gs.astype(B16)))
                tall_g.append(spread_t(jnp.transpose(gs).astype(B16)))
                tall_p.append(spread_t(jnp.transpose(p).astype(B16)))
            o = mm(jnp.concatenate(wide_g, axis=0), k_ref[:, lanes])
            total = o[:T] * masks[0]
            for a in range(1, len(heads)):
                total = total + o[a * T : (a + 1) * T] * masks[a]
            put(gq_half, total, tile, tiles)
            put(gk_half, mm(jnp.concatenate(tall_g, axis=1), qm), tile, tiles)
            put(gv_half, mm(jnp.concatenate(tall_p, axis=1), gmm), tile, tiles)
        for j in range(3):
            lanes = pl.ds(pl.multiple_of(half * W + j * T, T), T)
            gq_ref[:, lanes] = (gq_half[j] * scaling).astype(B16)
            gk_ref[:, lanes] = (gk_half[j] * scaling).astype(B16)
            gv_ref[:, lanes] = gv_half[j].astype(B16)
        return 0

    lax.fori_loop(0, 2, attend_back, 0)

    for t in range(3 * D // T):
        part, lane = t // (D // T), (t % (D // T)) * T
        source = (gq_ref, gk_ref, gv_ref)[part]
        left = n1t_ref[:, T : 2 * T] if part == 0 else n1t_ref[...]
        chains[3 + t % 3].src[(t // 3) * D : (t // 3 + 1) * D, :] = mm(
            left, source[:, lane : lane + T]
        ).astype(B16)
    for n in range(3, 6):
        chains[n].step()
    for j in range(0, D, 2 * T):
        here = slice(j, j + 2 * T)
        part = mm(gk_ref[...], wqkv_ref[here, D : 2 * D], NT) + mm(
            gv_ref[...], wqkv_ref[here, 2 * D :], NT
        )
        gn1_ref[:, here] = part[T : 2 * T] + mm(gq_ref[...], wqkv_ref[here, :D], NT)
        gn1_send_ref[0, :, here] = part[:T].astype(B16)
        gn1_send_ref[1, :, here] = part[2 * T :].astype(B16)
        gg1_ref[:, here] = (
            jnp.sum(part[:T] * xhat_ref[0:T, here], axis=0, keepdims=True)
            + jnp.sum(gn1_ref[:, here] * xhat_ref[T : 2 * T, here], axis=0, keepdims=True)
            + jnp.sum(part[2 * T :] * xhat_ref[2 * T :, here], axis=0, keepdims=True)
        )
    back_halos = [
        halo(gn1_send_ref.at[0], gn1_recv_ref.at[0], 4, last_row),
        halo(gn1_send_ref.at[1], gn1_recv_ref.at[1], 5, next_row),
    ]
    start_all(back_halos)
    for copy in back_halos:
        copy.wait()
    from_next = jnp.where(row < rows - 1, gn1_recv_ref[0].astype(F32), 0.0)
    from_last = jnp.where(row > 0, gn1_recv_ref[1].astype(F32), 0.0)
    gin_ref[...] = gmid_ref[...] + norm_back(
        gn1_ref[...] + from_next + from_last,
        xhat_ref[T : 2 * T, :],
        rstd_ref[T : 2 * T, :],
        g1_ref[...],
    )

    gmw_ref[...] = jnp.zeros_like(gmw_ref)
    ginner_ref[...] = jnp.zeros_like(ginner_ref)
    ghop_ref[...] = jnp.zeros_like(ghop_ref)
    gedge_ref[...] = jnp.zeros_like(gedge_ref)

    def back_step(c, _):
        at = pl.ds(pl.multiple_of(c * CHUNK, CHUNK), CHUNK)
        off8 = off_ref[at, :]
        hop8 = hopi_ref[at, :]
        edge8 = edgei_ref[at, :]
        goff = []
        sums = [jnp.zeros((T, T), F32) for _ in range(3)]
        for s in range(0, CHUNK, 2):
            here = slice(s * T, (s + 2) * T)
            lanes = pl.ds(pl.multiple_of(c * PAIRS + s * T, 2 * T), 2 * T)
            base = (c * CHUNK + s) * HEADS
            gs = jnp.concatenate(
                [
                    bias_ref[pl.ds(pl.multiple_of(base, HEADS), HEADS), :],
                    bias_ref[pl.ds(pl.multiple_of(base + HEADS, HEADS), HEADS), :],
                ],
                axis=1,
            )
            hop = two(hop8, s)
            edge = two(edge8, s)
            hop_g = jnp.broadcast_to(hop >> 7, (HEADS, 2 * T))
            edge_g = jnp.broadcast_to(edge >> 7, (HEADS, 2 * T))
            for g in range(4):
                lhsh_ref[g * HEADS : (g + 1) * HEADS, here] = jnp.where(hop_g == g, gs, 0.0).astype(B16)
            for g in range(12):
                lhse_ref[g * HEADS : (g + 1) * HEADS, here] = jnp.where(edge_g == g, gs, 0.0).astype(B16)
            rhsh_ref[0:T, here] = hot(hop)
            rhsh_ref[T : 2 * T, here] = hidden_ref[:, lanes]
            rhse_ref[:, here] = hot(edge)
            grad_hidden = mm(outer_ref[...], gs.astype(B16), (((0,), (0,)), ((), ())))
            gpre = (grad_hidden * slope_ref[:, lanes]).astype(B16)
            gpre_ref[:, here] = gpre
            gfeat = mm(inner_ref[...], gpre)
            z = two(off8, s) * wide(cols_ref[0]) - wide(cols_ref[1])
            a = gfeat * jnp.exp2(wide(cols_ref[2]) - z * z)
            az = a * z
            azz = az * z
            goff.append(jnp.sum(az * wide(cols_ref[3]), axis=0, keepdims=True))
            sums[0] = sums[0] + az[:, :T] + az[:, T:]
            sums[1] = sums[1] + azz[:, :T] + azz[:, T:]
            sums[2] = sums[2] + a[:, :T] + a[:, T:]
        for n in range(3):
            gmw_ref[n] = gmw_ref[n] + sums[n]
        goff_ref[at, :] = jnp.concatenate(
            [-g[:, n * T : (n + 1) * T] for g in goff for n in range(2)], axis=0
        ) * (LOG2E ** 0.0)
        ghop_ref[...] += mm(lhsh_ref[...], rhsh_ref[...], NT)
        gedge_ref[...] += mm(lhse_ref[...], rhse_ref[...], NT)
        ginner_ref[...] += mm(
            feat_ref[:, pl.ds(pl.multiple_of(c * PAIRS, PAIRS), PAIRS)], gpre_ref[...], NT
        )
        return 0

    lax.fori_loop(0, T // CHUNK, back_step, 0)
    goff = goff_ref[...]
    gdist = goff * dist_ref[...]
    flat = []
    for value in (gdist, goff):
        query = jnp.sum(jnp.transpose(value), axis=0, keepdims=True)
        parts = [jnp.sum(value * m_ref[t], axis=0, keepdims=True) for t in range(3)]
        parts[1] = parts[1] + query
        flat.append(parts)
    gtype = []
    for n in range(2):
        acc = jnp.zeros((4 * T, T), F32)
        for t in range(3):
            hit = kinds == types[:, t * T : (t + 1) * T]
            acc = acc + jnp.where(hit, flat[n][t], 0.0)
        gtype += [
            jnp.sum(jnp.transpose(acc[c * T : (c + 1) * T]), axis=0, keepdims=True)
            for c in range(4)
        ]
    inv = 1.0 / widths_ref[...]
    back_scale = (2.0 / LOG2E) ** 0.5
    s0, s1, s2 = (jnp.sum(jnp.transpose(gmw_ref[n]), axis=0, keepdims=True) for n in range(3))
    small = [s0 * inv * back_scale, (s1 * (back_scale * back_scale) - s2) * inv]
    for gain in (gg1_ref[...], gg2_ref[...]):
        small += [gain[:, c * T : (c + 1) * T] for c in range(D // T)]
    small += gtype + [jnp.zeros((10, T), F32)]
    tail = chains[6].src
    tail[0:128, :] = ginner_ref[...].astype(B16)
    tail[128:256, :] = ghop_ref[:, :T].astype(B16)
    tail[256:640, :] = gedge_ref[...].astype(B16)
    tail[640:672, :] = (
        ghop_ref[0:32, T:] + ghop_ref[32:64, T:] + ghop_ref[64:96, T:] + ghop_ref[96:128, T:]
    ).astype(B16)
    tail[672:704, :] = jnp.concatenate(small, axis=0).astype(B16)
    tail[704:, :] = jnp.zeros((tail.shape[0] - 704, T), B16)
    while any(chain.left for chain in chains):
        for chain in chains:
            if chain.left:
                chain.step()


def unpack_kernel(*refs):
    ins, outs = refs[:7], refs[7:]
    (gqkv, gout, gg1, gg2, gup, gdown, gmeans, gwidths, ginner, gouter, ghop, gedge, gscale, gshift) = outs
    gdown[...] = ins[0][...].astype(F32)
    gup[...] = ins[1][...].astype(F32)
    gout[...] = ins[2][...].astype(F32)
    for n in range(3):
        gqkv[:, n * T : (n + 1) * T] = ins[3 + n][...].astype(F32)

    @pl.when(pl.program_id(0) == 0)
    def _():
        tail = ins[6]
        ginner[...] = tail[0:128, :].astype(F32)
        for g in range(4):
            ghop[:, g * T : (g + 1) * T] = tail[128 + 32 * g : 160 + 32 * g, :].astype(F32)
        for g in range(12):
            gedge[:, g * T : (g + 1) * T] = tail[256 + 32 * g : 288 + 32 * g, :].astype(F32)
        gouter[...] = tail[640:672, :].astype(F32)
        small = tail[672:704, :].astype(F32)
        gmeans[...] = small[0:1]
        gwidths[...] = small[1:2]
        for c in range(D // T):
            gg1[:, c * T : (c + 1) * T] = small[2 + c : 3 + c]
            gg2[:, c * T : (c + 1) * T] = small[8 + c : 9 + c]
        for c in range(4):
            gscale[:, c * T : (c + 1) * T] = small[14 + c : 15 + c]
            gshift[:, c * T : (c + 1) * T] = small[18 + c : 19 + c]


def run_unpack(sums):
    def whole(*shape):
        return pl.BlockSpec(shape, lambda j: (0, 0)), jax.ShapeDtypeStruct(shape, F32)

    def tile(columns):
        return (
            pl.BlockSpec((D, columns // 6), lambda j: (0, j)),
            jax.ShapeDtypeStruct((D, columns), F32),
        )

    outs = (
        tile(3 * D), tile(D), whole(1, D), whole(1, D), tile(D), tile(D), whole(1, T), whole(1, T),
        whole(T, T), whole(HEADS, T), whole(HEADS, 4 * T), whole(HEADS, 12 * T), whole(1, 4 * T),
        whole(1, 4 * T),
    )
    return pl.pallas_call(
        unpack_kernel,
        grid=(6,),
        in_specs=[pl.BlockSpec((D, T), lambda j: (j, 0))] * 6
        + [pl.BlockSpec(sums[6].shape, lambda j: (0, 0))],
        out_specs=[o[0] for o in outs],
        out_shape=[o[1] for o in outs],
        compiler_params=pltpu.CompilerParams(vmem_limit_bytes=32 * 1024 * 1024),
        name="unpack",
    )(*sums)


def run_compute(args):
    vm = pltpu.VMEM
    inner, outer = z_split()
    unit = 8 * inner * 16

    def padded(count):
        return -(-count // unit) * unit

    counts = [padded(6 * D)] * 6 + [padded(704)]
    out_shape = [jax.ShapeDtypeStruct((T, D), B16), jax.ShapeDtypeStruct((T, D), F32)]
    out_shape += [jax.ShapeDtypeStruct((count, T), B16) for count in counts]
    scratch = [
        vm((2, T, D), B16),
        vm((8, T), F32),
        vm((2, 8, T), F32),
        vm((2, T, D), B16),
        vm((2, T, D), B16),
        pltpu.SemaphoreType.DMA((6,)),
        pltpu.SemaphoreType.DMA((6,)),
        vm((D, W), B16),
        vm((W, D), F32),
        vm((W, 1), F32),
        vm((T, D), B16),
        vm((W, D), B16),
        vm((W, D), B16),
        vm((3, T, T), F32),
        vm((3, T, T), B16),
        vm((3, T, T), B16),
        vm((T, T), F32),
        vm((T, T), F32),
        vm((T, T), jnp.int32),
        vm((T, T), jnp.int32),
        vm((4, T, T), F32),
        vm((T, 2 * T), B16),
        vm((3 * T, T), B16),
        vm((T, T), B16),
        vm((T, T * T), B16),
        vm((T, T * T), B16),
        vm((T, T * T), F32),
        vm((T * HEADS, T), F32),
        vm((HEADS, T, T), F32),
        vm((T, D), B16),
        vm((T, D), B16),
        vm((T, D), B16),
        vm((W, D), B16),
        vm((W, D), B16),
        vm((T, T), F32),
        vm((T, PAIRS), B16),
        vm((3 * T, PAIRS), B16),
        vm((2 * T, PAIRS), B16),
        vm((T, PAIRS), B16),
        vm((T, PAIRS), B16),
        vm((T, D), F32),
        vm((3, T, T), F32),
        vm((T, T), F32),
        vm((T, 2 * T), F32),
        vm((3 * T, T), F32),
        vm((1, D), F32),
        vm((1, D), F32),
        vm((T, D), F32),
        vm((W, D), B16),
    ]
    for count in counts:
        scratch += [
            vm((count, T), B16),
            vm((count // 2, T), B16),
            vm((count // 4, T), B16),
            vm((count // 8, T), B16),
            vm((inner - 1, count // (8 * inner), T), B16),
            vm((max(outer - 1, 1), count // (8 * inner), T), B16),
            vm((count // (8 * inner), T), B16),
            pltpu.SemaphoreType.DMA((6 + 2 * (inner - 1) + outer - 1,)),
            pltpu.SemaphoreType.DMA((6 + 2 * (inner - 1) + outer - 1,)),
            pltpu.SemaphoreType.DMA,
        ]
    vspec = pl.BlockSpec(memory_space=pltpu.VMEM)
    sspec = pl.BlockSpec(memory_space=pltpu.SMEM)
    return pl.pallas_call(
        compute_kernel,
        out_shape=out_shape,
        in_specs=[sspec] + [vspec] * (len(args) - 1),
        out_specs=[vspec] * 2 + [pl.BlockSpec(memory_space=pl.ANY)] * 7,
        scratch_shapes=scratch,
        compiler_params=pltpu.CompilerParams(
            vmem_limit_bytes=60 * 1024 * 1024, collective_id=0, has_side_effects=True
        ),
        name="layer",
    )(*args)


def body(
    hidden_in,
    positions,
    atom_types,
    path_hops,
    edge_kinds,
    mol_lengths,
    qkv_weight,
    out_weight,
    attn_gain,
    ffn_gain,
    up_weight,
    down_weight,
    kernel_means,
    kernel_widths,
    kernel_inner,
    kernel_outer,
    hop_table,
    edge_table,
    atom_scale,
    atom_shift,
    out_grad,
):
    out, grad_in, *sums = run_compute(
        (
            mol_lengths,
            hidden_in[0],
            positions[0],
            atom_types,
            path_hops[0],
            edge_kinds[0],
            qkv_weight,
            out_weight,
            attn_gain[None],
            ffn_gain[None],
            up_weight,
            down_weight,
            kernel_means[None],
            kernel_widths[None],
            kernel_inner,
            kernel_outer.T,
            hop_table,
            edge_table,
            atom_scale[None],
            atom_shift[None],
            out_grad[0],
        )
    )
    grads = run_unpack(sums)
    flat = (2, 3, 6, 7, 12, 13)
    grads = [g[0] if n in flat else g for n, g in enumerate(grads)]
    grads[9] = grads[9].T
    return (out[None], grad_in[None]) + tuple(grads)


def solution(mesh):
    split3 = P("blocks", "rows", None)
    in_specs = (
        split3,
        P("blocks", None, "rows"),
        P("blocks", "rows"),
        split3,
        split3,
        P("blocks", None),
    ) + (P(),) * 14 + (split3,)
    out_specs = (split3, split3) + (P(),) * 14
    return jax.shard_map(body, mesh=mesh, in_specs=in_specs, out_specs=out_specs, check_vma=False)
```

```python
import functools

import jax
import jax.numpy as jnp
from jax import lax
from jax.experimental import pallas as pl
from jax.experimental.pallas import tpu as pltpu
from jax.sharding import PartitionSpec as P

EPS = 1e-05
NEG = -1000000000.0
SQRT_TWO_PI = 2.5066282746310002
SQRT_2_OVER_PI = 0.7978845608028654
CUBIC = 0.044715
LOG2E = 1.4426950408889634
F32 = jnp.float32
B16 = jnp.bfloat16
T = 128
W = 3 * T
D = 768
HEADS = 32
HD = 24
NN = (((1,), (0,)), ((), ()))
NT = (((1,), (1,)), ((), ()))
GROUPS = (
    (0, 1, (0, 1, 2, 3, 4)),
    (0, 2, (5,)),
    (1, 1, (6, 7, 8, 9)),
    (1, 2, (10,)),
    (2, 1, (11, 12, 13, 14, 15)),
)
ORDERS = ("cyxz", "cyxz", "cxyz", "cyxz", "cyxz", "cxyz", "cyxz", "cyxz", "cxyz", "cyxz", "cxyz", "cxyz", "cyxz", "cyxz", "cxyz", "cyxz", "cxyz", "cyxz", "cxyz")
SLOTS = {"att0": (0,), "att1": (1, 2), "att2": (3, 4), "att3": (5, 6), "att4": (7, 8), "att5": (0,), "att6": (2,), "att7": (1,), "att8": (5,), "att9": (3,), "gq1": (8,), "gq3": (4, 0), "gq6": (1,), "gq7": (9,), "gq8": (6, 3, 10), "gn1": (11, 12, 4, 0, 13, 7, 14, 1), "pair0": (2, 15, 16, 6, 3, 5, 17, 8), "pair1": (10,), "pair2": (4, 9), "pair3": (11, 0), "pair4": (7, 12, 1), "pair5": (2,), "pair6": (6, 14, 13, 3), "pair8": (5, 16, 15, 8), "pair9": (9, 4), "pair10": (17, 7, 0), "pair11": (12, 10, 2, 1, 11), "pair12": (13, 14, 6), "pair13": (16, 5, 3), "pair14": (15, 8, 9), "pair15": (4, 0, 7), "small": (17, 12, 2, 6)}
TAIL = (10, 1, 11, 0, 5, 7, 13, 18, 14, 3, 1, 16, 2, 8, 15, 9, 5, 4, 3, 17, 2, 18, 12, 6, 10, 5, 8, 4, 11, 9, 7, 13, 18, 12, 6, 14, 8, 10, 16, 11, 7, 15, 13, 17, 9, 18, 10, 12, 14, 9, 18, 11, 16, 15, 10, 12, 17, 13, 11, 18, 14, 15, 13, 16, 14, 18, 17, 15, 16, 18, 17)
CHUNK = 8
PAIRS = CHUNK * T


def mm(a, b, dims=NN):
    return lax.dot_general(a, b, dims, preferred_element_type=F32)


def gelu_parts(x):
    x2 = x * x
    cubic = (SQRT_2_OVER_PI * CUBIC) * x2
    u = x * (SQRT_2_OVER_PI + cubic)
    half = 0.5 + 0.5 * jnp.tanh(u)
    act = x * half
    slope = half + act * (1.0 - half) * (2.0 * SQRT_2_OVER_PI + 6.0 * cubic)
    return act, slope


def normalise(v):
    centre = jnp.mean(v, axis=-1, keepdims=True)
    shifted = v - centre
    spread = jnp.mean(shifted * shifted, axis=-1, keepdims=True)
    rstd = lax.rsqrt(spread + EPS)
    return shifted * rstd, rstd


def norm_back(grad, xhat, rstd, gain):
    g = grad * gain
    return rstd * (
        g
        - jnp.mean(g, axis=-1, keepdims=True)
        - xhat * jnp.mean(g * xhat, axis=-1, keepdims=True)
    )


def down(row):
    return jnp.transpose(jnp.broadcast_to(row, (T, T)))


def z_split():
    count = lax.axis_size("blocks") // 2
    inner = min(count, 4)
    return inner, count // inner


def start_all(copies):
    for copy in copies:
        copy.start()


class Chain:
    def __init__(self, place, order, src, bufs, far_buf, final, out, send, recv, local):
        c, x, y, z, inner, outer = place
        zi = z % inner
        row, block = 2 * x + c, 2 * z + y
        axes = {
            "c": (c, [(block, 2 * x + 1 - c)]),
            "x": (x, [(block, 2 * (1 - x) + c)]),
            "y": (y, [(2 * z + 1 - y, row)]),
            "z": (zi, [(2 * (z - zi + (zi + k) % inner) + y, row) for k in range(1, inner)]),
        }
        self.far = [
            (2 * (zi + inner * ((z // inner + k) % outer)) + y, row) for k in range(1, outer)
        ]
        self.src, self.bufs, self.far_buf, self.final, self.out = src, bufs, far_buf, final, out
        self.send, self.recv, self.local = send, recv, local
        self.stages = []
        start, size = 0, src.shape[0]
        for name in order:
            mine, peers = axes[name]
            size //= len(peers) + 1
            self.stages.append((mine, peers, start, size))
            start = start + mine * size
        self.start, self.size = start, size
        self.flying = []
        self.used = 0
        self.todo = [self.scatter(k) for k in range(4)]
        if outer > 1:
            self.todo += [self.exchange]
        self.todo += [self.finish] + [self.gather(k) for k in (2, 1, 0)]
        self.left = len(self.todo) + 1

    @staticmethod
    def at(start, size):
        return pl.ds(pl.multiple_of(start, 16), size)

    def go(self, src, dst, device):
        n = self.used
        self.used += 1

        def make():
            return pltpu.make_async_remote_copy(
                src_ref=src(),
                dst_ref=dst(),
                send_sem=self.send.at[n],
                recv_sem=self.recv.at[n],
                device_id=device,
                device_id_type=pl.DeviceIdType.MESH,
            )

        make().start()
        self.flying.append(make)

    def add(self, start, size, others, into=None):
        block = 16
        while block < 128 and size % (2 * block) == 0:
            block *= 2

        def one(i, _):
            here = pl.ds(pl.multiple_of(i * block, 16), block)
            there = self.at(start + i * block, block)
            total = self.src[there, :].astype(F32)
            for other in others:
                total = total + other[here, :].astype(F32)
            if into is None:
                self.src[there, :] = total.astype(B16)
            else:
                into[here, :] = total.astype(B16)
            return 0

        lax.fori_loop(0, size // block, one, 0)

    def take(self, k, into=None):
        mine, peers, start, size = self.stages[k]
        self.add(start + mine * size, size, [self.bufs[k].at[i] for i in range(len(peers))], into)

    def scatter(self, k):
        def run():
            if k > 0:
                self.take(k - 1)
            mine, peers, start, size = self.stages[k]
            for i, peer in enumerate(peers):
                self.go(
                    lambda i=i: self.src.at[
                        self.at(start + (mine + i + 1) % (len(peers) + 1) * size, size)
                    ],
                    lambda i=i: self.bufs[k].at[i],
                    peer,
                )

        return run

    def exchange(self):
        self.take(3)
        for i, peer in enumerate(self.far):
            self.go(
                lambda: self.src.at[self.at(self.start, self.size)],
                lambda i=i: self.far_buf.at[i],
                peer,
            )

    def finish(self):
        if self.far:
            others = [self.far_buf.at[i] for i in range(len(self.far))]
            self.add(self.start, self.size, others, self.final)
        else:
            self.take(3, self.final)

        def own():
            return pltpu.make_async_copy(
                self.final, self.out.at[self.at(self.start, self.size)], self.local
            )

        own().start()
        self.flying.append(own)
        for peer in self.stages[3][1]:
            self.go(lambda: self.final, lambda: self.out.at[self.at(self.start, self.size)], peer)

    def gather(self, k):
        def run():
            _, _, start, size = self.stages[k + 1]
            rows = size * (len(self.stages[k + 1][1]) + 1)
            for peer in self.stages[k][1]:
                here = lambda: self.out.at[self.at(start, rows)]
                self.go(here, here, peer)

        return run

    def step(self):
        for make in self.flying:
            make().wait()
        self.flying = []
        self.left -= 1
        if self.todo:
            self.todo.pop(0)()


def compute_kernel(
    lens_ref,
    own_ref,
    pos_ref,
    types_in_ref,
    hops_ref,
    edges_ref,
    wqkv_hbm,
    wout_hbm,
    gain1_ref,
    gain2_ref,
    wup_hbm,
    wdown_hbm,
    means_ref,
    widths_ref,
    inner_ref,
    outer_ref,
    hop_tab_ref,
    edge_tab_ref,
    scale_ref,
    shift_ref,
    cot_ref,
    out_ref,
    gin_ref,
    *rest,
):
    sums_out, rest = rest[:7], rest[7:]
    (
        hid_ref, geo_own_ref, geo_ref, gn1_send_ref, gn1_recv_ref, halo_send, halo_recv,
        n1t_ref, xhat_ref, rstd_ref, q_ref, k_ref, v_ref, m_ref, mb_ref, mt_ref, off_ref, dist_ref,
        hopi_ref, edgei_ref, cols_ref, w1_ref, w2_ref, innert_ref, feat_ref, hidden_ref, slope_ref,
        bias_ref, p_ref, mixed_ref, gmix_ref, gq_ref, gk_ref, gv_ref, goff_ref, lhsh_ref, lhse_ref,
        rhsh_ref, rhse_ref, gpre_ref, gmid_ref, gmw_ref, ginner_ref, ghop_ref, gedge_ref, gg2_ref,
        gg1_ref, gn1_ref, n1_ref, wqkv_ref, wout_ref, wup_ref, wdown_ref, weight_sems, iota_ref, g1_ref, g2_ref,
    ) = rest[:57]
    rest = rest[57:]
    row = lax.axis_index("rows")
    rows = lax.axis_size("rows")
    block = lax.axis_index("blocks")
    inner, outer = z_split()
    place = (row % 2, row // 2, block % 2, block // 2, inner, outer)
    chains = []
    for n in range(len(ORDERS)):
        src, *bufs, far_buf, final, send, recv, local = rest[10 * n : 10 * n + 10]
        if n < 9:
            out, third = sums_out[n // 3], n % 3
        elif n < 18:
            out, third = sums_out[3 + n % 3], n // 3 - 3
        else:
            out, third = sums_out[6], 0
        out = out.at[pl.ds(third * src.shape[0], src.shape[0])]
        chains.append(Chain(place, ORDERS[n], src, bufs, far_buf, final, out, send, recv, local))

    def serve(slot):
        for n in SLOTS.get(slot, ()):
            chains[n].step()

    loads = [
        pltpu.make_async_copy(src, dst, weight_sems.at[n])
        for n, (src, dst) in enumerate(
            (
                (wqkv_hbm, wqkv_ref),
                (wout_hbm, wout_ref),
                (wup_hbm, wup_ref),
                (wdown_hbm, wdown_ref),
            )
        )
    ]
    start_all(loads)
    for gain, into in ((gain1_ref, g1_ref), (gain2_ref, g2_ref)):
        for c in range(D // T):
            into[:, c * T : (c + 1) * T] = gain[c : c + 1, :]

    barrier = pltpu.get_barrier_semaphore()
    z_peers = next(s[1] for s, name in zip(chains[0].stages, ORDERS[0]) if name == "z")
    others = [(block, (row + k) % rows) for k in range(1, rows)]
    others += [(2 * (block // 2) + 1 - block % 2, row)] + z_peers + chains[0].far
    for other in others:
        pl.semaphore_signal(barrier, inc=1, device_id=other, device_id_type=pl.DeviceIdType.MESH)
    pl.semaphore_wait(barrier, len(others))

    geo_own_ref[...] = jnp.concatenate(
        [pos_ref[...].astype(F32), types_in_ref[...].astype(F32), jnp.zeros((4, T), F32)], axis=0
    )
    next_row, last_row = (block, (row + 1) % rows), (block, (row + rows - 1) % rows)

    def halo(src, dst, n, device):
        return pltpu.make_async_remote_copy(
            src_ref=src,
            dst_ref=dst,
            send_sem=halo_send.at[n],
            recv_sem=halo_recv.at[n],
            device_id=device,
            device_id_type=pl.DeviceIdType.MESH,
        )

    halos = [
        halo(geo_own_ref, geo_ref.at[0], 0, next_row),
        halo(geo_own_ref, geo_ref.at[1], 1, last_row),
        halo(own_ref, hid_ref.at[0], 2, next_row),
        halo(own_ref, hid_ref.at[1], 3, last_row),
    ]
    start_all(halos)

    mean_col = down(means_ref[...])
    inv_col = 1.0 / down(widths_ref[...])
    s_col = inv_col * ((0.5 * LOG2E) ** 0.5)
    cols_ref[0] = s_col
    cols_ref[1] = mean_col * s_col
    cols_ref[2] = jnp.log2(inv_col * (1.0 / SQRT_TWO_PI))
    cols_ref[3] = inv_col * (1.0 / (0.5 * LOG2E) ** 0.5)
    innert_ref[...] = jnp.transpose(inner_ref[...])
    outer_t = outer_ref[...]
    for g in range(4):
        w1_ref[g * HEADS : (g + 1) * HEADS, 0:T] = outer_t
        w1_ref[g * HEADS : (g + 1) * HEADS, T : 2 * T] = hop_tab_ref[:, g * T : (g + 1) * T]
    for g in range(12):
        w2_ref[g * HEADS : (g + 1) * HEADS, :] = edge_tab_ref[:, g * T : (g + 1) * T]

    iota_ref[...] = lax.broadcasted_iota(jnp.int32, (T, 2 * T), 0).astype(F32).astype(B16)

    first = (row - 1) * T
    ids_row = first + lax.broadcasted_iota(jnp.int32, (1, W), 1)
    mol_row = jnp.zeros((1, W), jnp.int32)
    end = jnp.int32(0)
    for m in range(lens_ref.shape[1]):
        end = end + lens_ref[0, m]
        mol_row = mol_row + jnp.where(ids_row >= end, 1, 0)
    mol_row = jnp.where((ids_row >= 0) & (ids_row < rows * T), mol_row, -1).astype(F32)
    mol_own = mol_row[:, T : 2 * T]
    mol_col = down(mol_own)
    scale_col = jnp.concatenate(
        [down(scale_ref[:, c * T : (c + 1) * T]) for c in range(4)], axis=0
    )
    shift_col = jnp.concatenate(
        [down(shift_ref[:, c * T : (c + 1) * T]) for c in range(4)], axis=0
    )
    kinds = lax.broadcasted_iota(jnp.int32, (4 * T, T), 0)
    for copy in halos[:2]:
        copy.wait()
    geo = jnp.concatenate([geo_ref[0], geo_own_ref[...], geo_ref[1]], axis=1)
    pos = geo[0:3]
    types = geo[3:4].astype(jnp.int32)
    sel = [jnp.zeros((T, T), F32) for _ in range(5)]
    own = None
    hop_sel = jnp.zeros((T, T), jnp.int32)
    edge_sel = jnp.zeros((T, T), jnp.int32)
    for t in range(3):
        lanes = slice(t * T, (t + 1) * T)
        mask = mol_col == jnp.broadcast_to(mol_row[:, lanes], (T, T))
        mask_t = down(mol_row[:, lanes]) == jnp.broadcast_to(mol_own, (T, T))
        m_ref[t] = mask.astype(F32)
        mb_ref[t] = mask.astype(F32).astype(B16)
        mt_ref[t] = mask_t.astype(F32).astype(B16)
        hit = kinds == types[:, lanes]
        terms = (
            pos[0:1, lanes],
            pos[1:2, lanes],
            pos[2:3, lanes],
            jnp.sum(jnp.where(hit, scale_col, 0.0), axis=0, keepdims=True),
            jnp.sum(jnp.where(hit, shift_col, 0.0), axis=0, keepdims=True),
        )
        if t == 1:
            own = terms
        sel = [jnp.where(mask, v, s) for v, s in zip(terms, sel)]
        tile = (row + (t - 1 + rows)) % rows
        at = pl.ds(pl.multiple_of(tile * T, T), T)
        hop_sel = jnp.where(mask, hops_ref[:, at], hop_sel)
        edge_sel = jnp.where(mask, edges_ref[:, at], edge_sel)
    ownc = [down(v) for v in own]
    dx, dy, dz = (ownc[c] - sel[c] for c in range(3))
    dist = jnp.sqrt(dx * dx + dy * dy + dz * dz)
    dist_ref[...] = dist
    off_ref[...] = (ownc[3] + sel[3]) * dist + ownc[4] + sel[4]
    hopi_ref[...] = hop_sel
    edgei_ref[...] = edge_sel

    def two(block, s):
        return jnp.concatenate([block[s : s + 1], block[s + 1 : s + 2]], axis=1)

    def wide(a):
        return jnp.concatenate([a, a], axis=1)

    def low16(index):
        return jnp.broadcast_to(index.astype(F32), (16, 2 * T)).astype(B16)

    def hot(index):
        rows16 = jnp.concatenate([low16(index & (T - 1))] * 8, axis=0)
        return jnp.where(iota_ref[...] == rows16, jnp.ones((), B16), jnp.zeros((), B16))

    def bit_masks(index, bits):
        wide_index = jnp.broadcast_to(index, (8, 2 * T))
        return [(wide_index & (1 << b)) != 0 for b in range(bits)]

    def pick(values, masks):
        for mask in masks:
            values = [
                jnp.where(mask, values[i + 1], values[i]) if i + 1 < len(values) else values[i]
                for i in range(0, len(values), 2)
            ]
        return values[0]

    def bias_step(c, _):
        at = pl.ds(pl.multiple_of(c * CHUNK, CHUNK), CHUNK)
        off8 = off_ref[at, :]
        hop8 = hopi_ref[at, :]
        edge8 = edgei_ref[at, :]
        for s in range(0, CHUNK, 2):
            lanes = pl.ds(pl.multiple_of(c * PAIRS + s * T, 2 * T), 2 * T)
            z = two(off8, s) * wide(cols_ref[0]) - wide(cols_ref[1])
            feat = jnp.exp2(wide(cols_ref[2]) - z * z).astype(B16)
            feat_ref[:, lanes] = feat
            pre = mm(innert_ref[...], feat)
            act, slope = gelu_parts(pre)
            hidden = act.astype(B16)
            hidden_ref[:, lanes] = hidden
            slope_ref[:, lanes] = slope
            hop = two(hop8, s)
            edge = two(edge8, s)
            low = mm(w1_ref[...], jnp.concatenate([hidden, hot(hop)], axis=0))
            high = mm(w2_ref[...], hot(edge))
            hop_bits = bit_masks(hop >> 7, 2)
            edge_bits = bit_masks(edge >> 7, 4)
            bias = jnp.concatenate(
                [
                    pick([low[g * HEADS + r : g * HEADS + r + 8] for g in range(4)], hop_bits)
                    + pick([high[g * HEADS + r : g * HEADS + r + 8] for g in range(12)], edge_bits)
                    for r in range(0, HEADS, 8)
                ],
                axis=0,
            )
            base = (c * CHUNK + s) * HEADS
            bias_ref[pl.ds(pl.multiple_of(base, HEADS), HEADS), :] = bias[:, :T]
            bias_ref[pl.ds(pl.multiple_of(base + HEADS, HEADS), HEADS), :] = bias[:, T:]
        return 0

    lax.fori_loop(0, T // CHUNK, bias_step, 0)

    for copy in halos[2:]:
        copy.wait()
    loads[0].wait()
    for t, tile_ref in enumerate((hid_ref.at[0], own_ref, hid_ref.at[1])):
        here = slice(t * T, (t + 1) * T)
        xhat, rstd = normalise(tile_ref[...].astype(F32))
        xhat_ref[here, :] = xhat
        rstd_ref[here, :] = rstd
        n1_ref[here, :] = (xhat * g1_ref[...]).astype(B16)
        for c in range(D // T):
            n1t_ref[c * T : (c + 1) * T, here] = jnp.transpose(n1_ref[here, c * T : (c + 1) * T])
    for j in range(0, D, 2 * T):
        here = slice(j, j + 2 * T)
        q_ref[:, here] = mm(n1_ref[T : 2 * T, :], wqkv_ref[:, here]).astype(B16)
        k_ref[:, here] = mm(n1_ref[...], wqkv_ref[:, D + j : D + j + 2 * T]).astype(B16)
        v_ref[:, here] = mm(n1_ref[...], wqkv_ref[:, 2 * D + j : 2 * D + j + 2 * T]).astype(B16)

    scaling = HD ** (-0.5)

    def head_mask(h, tile, tiles):
        lane = lax.broadcasted_iota(jnp.int32, (1, tiles * T), 1) + tile * T
        return ((lane >= h * HD) & (lane < (h + 1) * HD)).astype(F32)

    def spread(low):
        return jnp.concatenate([low * mb_ref[t] for t in range(3)], axis=1)

    def compact(wide_scores):
        return jnp.where(
            m_ref[0] > 0,
            wide_scores[:, :T],
            jnp.where(m_ref[1] > 0, wide_scores[:, T : 2 * T], wide_scores[:, 2 * T :]),
        )

    def attend(half, _):
        mixed_half = [None, None, None]
        for tile, tiles, heads in GROUPS:
            lanes = pl.ds(pl.multiple_of(half * W + tile * T, T), tiles * T)
            masks = [head_mask(h, tile, tiles) for h in heads]
            q = q_ref[:, lanes]
            qm = jnp.concatenate([q * m.astype(B16) for m in masks], axis=0)
            raw = mm(qm, k_ref[:, lanes], NT)
            probs = []
            for a, h in enumerate(heads):
                head = half * 16 + h
                bias = bias_ref[pl.ds(head, T, stride=HEADS), :]
                visible = (m_ref[0] + m_ref[1] + m_ref[2]) > 0
                scores = jnp.where(
                    visible, compact(raw[a * T : (a + 1) * T]) * scaling + bias, NEG
                )
                peak = jnp.max(scores, axis=-1, keepdims=True)
                weights = jnp.exp(scores - peak)
                p = weights / jnp.sum(weights, axis=-1, keepdims=True)
                p_ref[head] = p
                probs.append(spread(p.astype(B16)))
            o = mm(jnp.concatenate(probs, axis=0), v_ref[:, lanes])
            total = o[:T] * masks[0]
            for a in range(1, len(heads)):
                total = total + o[a * T : (a + 1) * T] * masks[a]
            for j in range(tiles):
                part = total[:, j * T : (j + 1) * T]
                before = mixed_half[tile + j]
                mixed_half[tile + j] = part if before is None else before + part
        for j in range(3):
            mixed_ref[:, pl.ds(pl.multiple_of(half * W + j * T, T), T)] = mixed_half[j].astype(B16)
        return 0

    lax.fori_loop(0, 2, attend, 0)

    def tr(a):
        return jnp.concatenate(
            [jnp.transpose(a[:, c * T : (c + 1) * T]) for c in range(a.shape[1] // T)], axis=0
        )

    for copy in loads[1:]:
        copy.wait()
    mixed = mixed_ref[...]
    middle = own_ref[...].astype(F32) + mm(mixed, wout_ref[...])
    xhat2, rstd2 = normalise(middle)
    n2 = (xhat2 * g2_ref[...]).astype(B16)
    act, slope = gelu_parts(mm(n2, wup_ref[...]))
    act = act.astype(B16)
    out_ref[...] = (middle + mm(act, wdown_ref[...])).astype(B16)
    cot = cot_ref[...]

    def fill(n, left, right):
        for j in range(0, D, 2 * T):
            both = mm(left, right[:, j : j + 2 * T]).astype(B16)
            chain = chains[3 * n + j // (2 * T)]
            chain.src[:D, :] = both[:, :T]
            chain.src[D:, :] = both[:, T:]
            chain.step()
            serve(f"f{3 * n + j // (2 * T)}")

    fill(0, tr(act), cot)
    grad_pre = (mm(cot, wdown_ref[...], NT) * slope).astype(B16)
    fill(1, tr(n2), grad_pre)
    gn2 = mm(grad_pre, wup_ref[...], NT)
    gg2_ref[...] = jnp.sum(gn2 * xhat2, axis=0, keepdims=True)
    gmid = cot.astype(F32) + norm_back(gn2, xhat2, rstd2, g2_ref[...])
    gmid_ref[...] = gmid
    branch = gmid.astype(B16)
    fill(2, tr(mixed), branch)
    gmix_ref[...] = mm(branch, wout_ref[...], NT).astype(B16)

    def spread_t(low):
        return jnp.concatenate([low * mt_ref[t] for t in range(3)], axis=0)

    for half in range(2):
        gq_half = [None, None, None]
        gk_half = [None, None, None]
        gv_half = [None, None, None]

        def put(into, value, tile, tiles):
            for j in range(tiles):
                part = value[:, j * T : (j + 1) * T]
                before = into[tile + j]
                into[tile + j] = part if before is None else before + part

        for group, (tile, tiles, heads) in enumerate(GROUPS):
            lanes = slice(half * W + tile * T, half * W + (tile + tiles) * T)
            masks = [head_mask(h, tile, tiles) for h in heads]
            q = q_ref[:, lanes]
            gm = gmix_ref[:, lanes]
            qm = jnp.concatenate([q * m.astype(B16) for m in masks], axis=0)
            gmm = jnp.concatenate([gm * m.astype(B16) for m in masks], axis=0)
            grad_p = mm(gmm, v_ref[:, lanes], NT)
            wide_g, tall_g, tall_p = [], [], []
            for a, h in enumerate(heads):
                head = half * 16 + h
                p = p_ref[head]
                dp = compact(grad_p[a * T : (a + 1) * T])
                gs = p * (dp - jnp.sum(p * dp, axis=-1, keepdims=True))
                bias_ref[pl.ds(head, T, stride=HEADS), :] = gs
                wide_g.append(spread(gs.astype(B16)))
                tall_g.append(spread_t(jnp.transpose(gs).astype(B16)))
                tall_p.append(spread_t(jnp.transpose(p).astype(B16)))
            o = mm(jnp.concatenate(wide_g, axis=0), k_ref[:, lanes])
            total = o[:T] * masks[0]
            for a in range(1, len(heads)):
                total = total + o[a * T : (a + 1) * T] * masks[a]
            put(gq_half, total, tile, tiles)
            put(gk_half, mm(jnp.concatenate(tall_g, axis=1), qm), tile, tiles)
            put(gv_half, mm(jnp.concatenate(tall_p, axis=1), gmm), tile, tiles)
            serve(f"att{5 * half + group}")
        for j in range(3):
            lanes = slice(half * W + j * T, half * W + (j + 1) * T)
            gq_ref[:, lanes] = (gq_half[j] * scaling).astype(B16)
            gk_ref[:, lanes] = (gk_half[j] * scaling).astype(B16)
            gv_ref[:, lanes] = gv_half[j].astype(B16)

    for n in range(9):
        part, tile = n // 3, n % 3
        source = (gq_ref, gk_ref, gv_ref)[part]
        left = n1t_ref[:, T : 2 * T] if part == 0 else n1t_ref[...]
        right = jnp.concatenate(
            [source[:, tile * T : (tile + 1) * T], source[:, (tile + 3) * T : (tile + 4) * T]], axis=1
        )
        both = mm(left, right).astype(B16)
        chains[9 + n].src[:D, :] = both[:, :T]
        chains[9 + n].src[D:, :] = both[:, T:]
        chains[9 + n].step()
        serve(f"gq{n}")
    for j in range(0, D, 2 * T):
        here = slice(j, j + 2 * T)
        part = mm(gk_ref[...], wqkv_ref[here, D : 2 * D], NT) + mm(
            gv_ref[...], wqkv_ref[here, 2 * D :], NT
        )
        gn1_ref[:, here] = part[T : 2 * T] + mm(gq_ref[...], wqkv_ref[here, :D], NT)
        gn1_send_ref[0, :, here] = part[:T].astype(B16)
        gn1_send_ref[1, :, here] = part[2 * T :].astype(B16)
        gg1_ref[:, here] = (
            jnp.sum(part[:T] * xhat_ref[0:T, here], axis=0, keepdims=True)
            + jnp.sum(gn1_ref[:, here] * xhat_ref[T : 2 * T, here], axis=0, keepdims=True)
            + jnp.sum(part[2 * T :] * xhat_ref[2 * T :, here], axis=0, keepdims=True)
        )
    back_halos = [
        halo(gn1_send_ref.at[0], gn1_recv_ref.at[0], 4, last_row),
        halo(gn1_send_ref.at[1], gn1_recv_ref.at[1], 5, next_row),
    ]
    start_all(back_halos)
    serve("gn1")
    gmw_ref[...] = jnp.zeros_like(gmw_ref)
    ginner_ref[...] = jnp.zeros_like(ginner_ref)
    ghop_ref[...] = jnp.zeros_like(ghop_ref)
    gedge_ref[...] = jnp.zeros_like(gedge_ref)

    def back_step(c, _):
        at = pl.ds(pl.multiple_of(c * CHUNK, CHUNK), CHUNK)
        off8 = off_ref[at, :]
        hop8 = hopi_ref[at, :]
        edge8 = edgei_ref[at, :]
        goff = []
        sums = [jnp.zeros((T, T), F32) for _ in range(3)]
        for s in range(0, CHUNK, 2):
            here = slice(s * T, (s + 2) * T)
            lanes = pl.ds(pl.multiple_of(c * PAIRS + s * T, 2 * T), 2 * T)
            base = (c * CHUNK + s) * HEADS
            gs = jnp.concatenate(
                [
                    bias_ref[pl.ds(pl.multiple_of(base, HEADS), HEADS), :],
                    bias_ref[pl.ds(pl.multiple_of(base + HEADS, HEADS), HEADS), :],
                ],
                axis=1,
            )
            hop = two(hop8, s)
            edge = two(edge8, s)
            low_gs = gs.astype(B16)
            halves = (low_gs[:16], low_gs[16:])
            for index, count, into in ((hop, 4, lhsh_ref), (edge, 12, lhse_ref)):
                group16 = low16(index >> 7)
                for g in range(count):
                    mask = group16 == jnp.full((), g, B16)
                    for r in range(2):
                        into[g * HEADS + 16 * r : g * HEADS + 16 * r + 16, here] = jnp.where(
                            mask, halves[r], jnp.zeros((), B16)
                        )
            rhsh_ref[0:T, here] = hot(hop)
            rhsh_ref[T : 2 * T, here] = hidden_ref[:, lanes]
            rhse_ref[:, here] = hot(edge)
            grad_hidden = mm(outer_ref[...], low_gs, (((0,), (0,)), ((), ())))
            gpre = (grad_hidden * slope_ref[:, lanes]).astype(B16)
            gpre_ref[:, here] = gpre
            gfeat = mm(inner_ref[...], gpre)
            z = two(off8, s) * wide(cols_ref[0]) - wide(cols_ref[1])
            a = gfeat * jnp.exp2(wide(cols_ref[2]) - z * z)
            az = a * z
            azz = az * z
            goff.append(jnp.sum(az * wide(cols_ref[3]), axis=0, keepdims=True))
            sums[0] = sums[0] + az[:, :T] + az[:, T:]
            sums[1] = sums[1] + azz[:, :T] + azz[:, T:]
            sums[2] = sums[2] + a[:, :T] + a[:, T:]
        for n in range(3):
            gmw_ref[n] = gmw_ref[n] + sums[n]
        goff_ref[at, :] = jnp.concatenate(
            [-g[:, n * T : (n + 1) * T] for g in goff for n in range(2)], axis=0
        ) * (LOG2E ** 0.0)
        ghop_ref[...] += mm(lhsh_ref[...], rhsh_ref[...], NT)
        gedge_ref[...] += mm(lhse_ref[...], rhse_ref[...], NT)
        ginner_ref[...] += mm(
            feat_ref[:, pl.ds(pl.multiple_of(c * PAIRS, PAIRS), PAIRS)], gpre_ref[...], NT
        )
        for k in range(T // CHUNK):
            if f"pair{k}" in SLOTS:
                pl.when(c == k)(functools.partial(serve, f"pair{k}"))
        return 0

    lax.fori_loop(0, T // CHUNK, back_step, 0)
    goff = goff_ref[...]
    gdist = goff * dist_ref[...]
    flat = []
    for value in (gdist, goff):
        query = jnp.sum(jnp.transpose(value), axis=0, keepdims=True)
        parts = [jnp.sum(value * m_ref[t], axis=0, keepdims=True) for t in range(3)]
        parts[1] = parts[1] + query
        flat.append(parts)
    gtype = []
    for n in range(2):
        acc = jnp.zeros((4 * T, T), F32)
        for t in range(3):
            hit = kinds == types[:, t * T : (t + 1) * T]
            acc = acc + jnp.where(hit, flat[n][t], 0.0)
        gtype += [
            jnp.sum(jnp.transpose(acc[c * T : (c + 1) * T]), axis=0, keepdims=True)
            for c in range(4)
        ]
    inv = 1.0 / widths_ref[...]
    back_scale = (2.0 / LOG2E) ** 0.5
    s0, s1, s2 = (jnp.sum(jnp.transpose(gmw_ref[n]), axis=0, keepdims=True) for n in range(3))
    small = [s0 * inv * back_scale, (s1 * (back_scale * back_scale) - s2) * inv]
    for gain in (gg1_ref[...], gg2_ref[...]):
        small += [gain[:, c * T : (c + 1) * T] for c in range(D // T)]
    small += gtype + [jnp.zeros((10, T), F32)]
    tail = chains[18].src
    tail[0:128, :] = ginner_ref[...].astype(B16)
    tail[128:256, :] = ghop_ref[:, :T].astype(B16)
    tail[256:640, :] = gedge_ref[...].astype(B16)
    tail[640:672, :] = (
        ghop_ref[0:32, T:] + ghop_ref[32:64, T:] + ghop_ref[64:96, T:] + ghop_ref[96:128, T:]
    ).astype(B16)
    tail[672:704, :] = jnp.concatenate(small, axis=0).astype(B16)
    tail[704:, :] = jnp.zeros((tail.shape[0] - 704, T), B16)
    chains[18].step()
    serve("small")
    for copy in back_halos:
        copy.wait()
    from_next = jnp.where(row < rows - 1, gn1_recv_ref[0].astype(F32), 0.0)
    from_last = jnp.where(row > 0, gn1_recv_ref[1].astype(F32), 0.0)
    gin_ref[...] = gmid_ref[...] + norm_back(
        gn1_ref[...] + from_next + from_last,
        xhat_ref[T : 2 * T, :],
        rstd_ref[T : 2 * T, :],
        g1_ref[...],
    )
    for n in TAIL:
        chains[n].step()
    while any(chain.left for chain in chains):
        for chain in chains:
            if chain.left:
                chain.step()


def unpack_kernel(*refs):
    ins, outs = refs[:7], refs[7:]
    (gqkv, gout, gg1, gg2, gup, gdown, gmeans, gwidths, ginner, gouter, ghop, gedge, gscale, gshift) = outs
    for t in range(D // T):
        here = slice(t * T, (t + 1) * T)
        gdown[:, here] = ins[0][t].astype(F32)
        gup[:, here] = ins[1][t].astype(F32)
        gout[:, here] = ins[2][t].astype(F32)
        for n in range(3):
            gqkv[:, (3 * t + n) * T : (3 * t + n + 1) * T] = ins[3 + n][t].astype(F32)

    @pl.when(pl.program_id(0) == 0)
    def _():
        tail = ins[6]
        ginner[...] = tail[0:128, :].astype(F32)
        for g in range(4):
            ghop[:, g * T : (g + 1) * T] = tail[128 + 32 * g : 160 + 32 * g, :].astype(F32)
        for g in range(12):
            gedge[:, g * T : (g + 1) * T] = tail[256 + 32 * g : 288 + 32 * g, :].astype(F32)
        gouter[...] = tail[640:672, :].astype(F32)
        small = tail[672:704, :].astype(F32)
        gmeans[...] = small[0:1]
        gwidths[...] = small[1:2]
        gg1[...] = small[2:8]
        gg2[...] = small[8:14]
        for c in range(4):
            gscale[:, c * T : (c + 1) * T] = small[14 + c : 15 + c]
            gshift[:, c * T : (c + 1) * T] = small[18 + c : 19 + c]


def run_unpack(sums):
    def whole(*shape):
        return pl.BlockSpec(shape, lambda j: (0, 0)), jax.ShapeDtypeStruct(shape, F32)

    def rows(columns):
        return (
            pl.BlockSpec((T, columns), lambda j: (j, 0)),
            jax.ShapeDtypeStruct((D, columns), F32),
        )

    outs = (
        rows(3 * D), rows(D), whole(6, T), whole(6, T), rows(D), rows(D), whole(1, T), whole(1, T),
        whole(T, T), whole(HEADS, T), whole(HEADS, 4 * T), whole(HEADS, 12 * T), whole(1, 4 * T),
        whole(1, 4 * T),
    )
    tiles = [value.reshape(6, D, T) for value in sums[:6]]
    return pl.pallas_call(
        unpack_kernel,
        grid=(D // T,),
        in_specs=[pl.BlockSpec((6, T, T), lambda j: (0, j, 0))] * 6
        + [pl.BlockSpec(sums[6].shape, lambda j: (0, 0))],
        out_specs=[o[0] for o in outs],
        out_shape=[o[1] for o in outs],
        compiler_params=pltpu.CompilerParams(vmem_limit_bytes=60 * 1024 * 1024),
        name="unpack",
    )(*tiles, sums[6])


def run_compute(args):
    vm = pltpu.VMEM
    inner, outer = z_split()
    unit = 8 * inner * 16

    def padded(count):
        return -(-count // unit) * unit

    counts = [padded(2 * D)] * 18 + [padded(704)]
    out_shape = [jax.ShapeDtypeStruct((T, D), B16), jax.ShapeDtypeStruct((T, D), F32)]
    out_shape += [jax.ShapeDtypeStruct((3 * counts[0], T), B16)] * 6
    out_shape += [jax.ShapeDtypeStruct((counts[18], T), B16)]
    scratch = [
        vm((2, T, D), B16),
        vm((8, T), F32),
        vm((2, 8, T), F32),
        vm((2, T, D), B16),
        vm((2, T, D), B16),
        pltpu.SemaphoreType.DMA((6,)),
        pltpu.SemaphoreType.DMA((6,)),
        vm((D, W), B16),
        vm((W, D), F32),
        vm((W, 1), F32),
        vm((T, D), B16),
        vm((W, D), B16),
        vm((W, D), B16),
        vm((3, T, T), F32),
        vm((3, T, T), B16),
        vm((3, T, T), B16),
        vm((T, T), F32),
        vm((T, T), F32),
        vm((T, T), jnp.int32),
        vm((T, T), jnp.int32),
        vm((4, T, T), F32),
        vm((T, 2 * T), B16),
        vm((3 * T, T), B16),
        vm((T, T), B16),
        vm((T, T * T), B16),
        vm((T, T * T), B16),
        vm((T, T * T), F32),
        vm((T * HEADS, T), F32),
        vm((HEADS, T, T), F32),
        vm((T, D), B16),
        vm((T, D), B16),
        vm((T, D), B16),
        vm((W, D), B16),
        vm((W, D), B16),
        vm((T, T), F32),
        vm((T, PAIRS), B16),
        vm((3 * T, PAIRS), B16),
        vm((2 * T, PAIRS), B16),
        vm((T, PAIRS), B16),
        vm((T, PAIRS), B16),
        vm((T, D), F32),
        vm((3, T, T), F32),
        vm((T, T), F32),
        vm((T, 2 * T), F32),
        vm((3 * T, T), F32),
        vm((1, D), F32),
        vm((1, D), F32),
        vm((T, D), F32),
        vm((W, D), B16),
        vm((D, 3 * D), B16),
        vm((D, D), B16),
        vm((D, D), B16),
        vm((D, D), B16),
        pltpu.SemaphoreType.DMA((4,)),
        vm((T, 2 * T), B16),
        vm((1, D), F32),
        vm((1, D), F32),
    ]
    for count, order in zip(counts, ORDERS):
        size = count
        scratch.append(vm((count, T), B16))
        for name in order:
            ways = inner if name == "z" else 2
            size //= ways
            scratch.append(vm((ways - 1, size, T), B16))
        scratch += [
            vm((max(outer - 1, 1), size, T), B16),
            vm((size, T), B16),
            pltpu.SemaphoreType.DMA((6 + 2 * (inner - 1) + outer - 1,)),
            pltpu.SemaphoreType.DMA((6 + 2 * (inner - 1) + outer - 1,)),
            pltpu.SemaphoreType.DMA,
        ]
    vspec = pl.BlockSpec(memory_space=pltpu.VMEM)
    sspec = pl.BlockSpec(memory_space=pltpu.SMEM)
    aspec = pl.BlockSpec(memory_space=pl.ANY)
    return pl.pallas_call(
        compute_kernel,
        out_shape=out_shape,
        in_specs=[
            sspec if n == 0 else aspec if n in (6, 7, 10, 11) else vspec for n in range(len(args))
        ],
        out_specs=[vspec] * 2 + [pl.BlockSpec(memory_space=pl.ANY)] * 7,
        scratch_shapes=scratch,
        compiler_params=pltpu.CompilerParams(
            vmem_limit_bytes=60 * 1024 * 1024, collective_id=0, has_side_effects=True
        ),
        name="layer",
    )(*args)


def body(
    hidden_in,
    positions,
    atom_types,
    path_hops,
    edge_kinds,
    mol_lengths,
    qkv_weight,
    out_weight,
    attn_gain,
    ffn_gain,
    up_weight,
    down_weight,
    kernel_means,
    kernel_widths,
    kernel_inner,
    kernel_outer,
    hop_table,
    edge_table,
    atom_scale,
    atom_shift,
    out_grad,
):
    out, grad_in, *sums = run_compute(
        (
            mol_lengths,
            hidden_in[0],
            positions[0],
            atom_types,
            path_hops[0],
            edge_kinds[0],
            qkv_weight,
            out_weight,
            attn_gain.reshape(6, T),
            ffn_gain.reshape(6, T),
            up_weight,
            down_weight,
            kernel_means[None],
            kernel_widths[None],
            kernel_inner,
            kernel_outer.T,
            hop_table,
            edge_table,
            atom_scale[None],
            atom_shift[None],
            out_grad[0],
        )
    )
    grads = run_unpack(sums)
    flat = (2, 3, 6, 7, 12, 13)
    grads = [g.reshape(-1) if n in flat else g for n, g in enumerate(grads)]
    grads[9] = grads[9].T
    return (out[None], grad_in[None]) + tuple(grads)


def solution(mesh):
    split3 = P("blocks", "rows", None)
    in_specs = (
        split3,
        P("blocks", None, "rows"),
        P("blocks", "rows"),
        split3,
        split3,
        P("blocks", None),
    ) + (P(),) * 14 + (split3,)
    out_specs = (split3, split3) + (P(),) * 14
    return jax.shard_map(body, mesh=mesh, in_specs=in_specs, out_specs=out_specs, check_vma=False)
```

```python
import functools

import jax
import jax.numpy as jnp
from jax import lax
from jax.experimental import pallas as pl
from jax.experimental.pallas import tpu as pltpu
from jax.sharding import PartitionSpec as P

EPS = 1e-05
NEG = -1000000000.0
SQRT_TWO_PI = 2.5066282746310002
SQRT_2_OVER_PI = 0.7978845608028654
CUBIC = 0.044715
LOG2E = 1.4426950408889634
F32 = jnp.float32
B16 = jnp.bfloat16
T = 128
W = 3 * T
D = 768
HEADS = 32
HD = 24
NN = (((1,), (0,)), ((), ()))
NT = (((1,), (1,)), ((), ()))
GROUPS = (
    (0, 1, (0, 1, 2, 3, 4)),
    (0, 2, (5,)),
    (1, 1, (6, 7, 8, 9)),
    (1, 2, (10,)),
    (2, 1, (11, 12, 13, 14, 15)),
)
ORDERS = ("cxyz", "cyxz", "cyzx", "cxyz", "cxyz", "cxyz", "cyxz", "cyxz", "cxyz", "cxyz", "cyxz", "cxyz", "cxyz", "cxyz", "cyxz", "cyxz", "cyxz", "cyxz", ("c", "xyz"))
SLOTS = {"f4": (0,), "f6": (1,), "f7": (2,), "f8": (3,), "att0": (4,), "att1": (6, 5), "att2": (7, 8), "att3": (0,), "att4": (1,), "att5": (3,), "att6": (2,), "att8": (4, 6), "gq0": (5,), "gq3": (7,), "gq4": (9,), "gq5": (0, 8, 10), "gq6": (2, 11), "gq7": (1, 3, 12), "gn1": (6, 4, 13, 5), "pair0": (7, 17, 8, 0), "pair1": (1, 3, 10, 2), "pair2": (6, 11, 14, 16), "pair3": (15, 4, 5, 9), "pair4": (17, 7, 8, 12), "pair5": (1, 11, 0, 13), "pair6": (3, 10, 6, 2), "pair7": (17, 4, 14, 16), "pair8": (1, 7, 5, 15), "pair9": (11, 6, 8, 12), "pair10": (10, 9, 14, 0), "pair11": (3, 13, 7, 2), "pair12": (11, 17, 16, 4), "pair13": (1, 10, 15, 12), "pair14": (1, 5, 0, 14), "pair15": (3, 6, 13, 8), "small": (17, 3, 9, 7)}
TAIL = (4, 10, 0, 6, 16, 15, 18, 12, 7, 2, 5, 4, 14, 11, 2, 13, 5, 8, 9, 17, 16, 10, 8, 15, 10, 12, 14, 18, 13, 11, 9, 16, 11, 17, 15, 17, 12, 14, 12, 14, 18, 13, 16, 18, 13, 15, 9, 16, 15, 9)
CHUNK = 8
PAIRS = CHUNK * T


def mm(a, b, dims=NN):
    return lax.dot_general(a, b, dims, preferred_element_type=F32)


def gelu_parts(x):
    x2 = x * x
    cubic = (SQRT_2_OVER_PI * CUBIC) * x2
    u = x * (SQRT_2_OVER_PI + cubic)
    half = 0.5 + 0.5 * jnp.tanh(u)
    act = x * half
    slope = half + act * (1.0 - half) * (2.0 * SQRT_2_OVER_PI + 6.0 * cubic)
    return act, slope


def normalise(v):
    centre = jnp.mean(v, axis=-1, keepdims=True)
    shifted = v - centre
    spread = jnp.mean(shifted * shifted, axis=-1, keepdims=True)
    rstd = lax.rsqrt(spread + EPS)
    return shifted * rstd, rstd


def norm_back(grad, xhat, rstd, gain):
    g = grad * gain
    return rstd * (
        g
        - jnp.mean(g, axis=-1, keepdims=True)
        - xhat * jnp.mean(g * xhat, axis=-1, keepdims=True)
    )


def down(row):
    return jnp.transpose(jnp.broadcast_to(row, (T, T)))


def z_split():
    count = lax.axis_size("blocks") // 2
    inner = min(count, 4)
    return inner, count // inner


class Chain:
    def __init__(self, place, order, src, bufs, far_buf, final, out, send, recv, local):
        c, x, y, z, inner, outer = place
        zi = z % inner
        row, block = 2 * x + c, 2 * z + y
        axes = {
            "c": (c, [(block, 2 * x + 1 - c)]),
            "x": (x, [(block, 2 * (1 - x) + c)]),
            "y": (y, [(2 * z + 1 - y, row)]),
            "z": (zi, [(2 * (z - zi + (zi + k) % inner) + y, row) for k in range(1, inner)]),
        }
        chip = (2 * x + y) * inner + zi
        chips = [(chip + k) % (4 * inner) for k in range(1, 4 * inner)]
        axes["xyz"] = (
            chip,
            [
                (2 * (z - zi + n % inner) + n // inner % 2, 2 * (n // (2 * inner)) + c)
                for n in chips
            ],
        )
        self.far = [
            (2 * (zi + inner * ((z // inner + k) % outer)) + y, row) for k in range(1, outer)
        ]
        self.src, self.bufs, self.far_buf, self.final, self.out = src, bufs, far_buf, final, out
        self.send, self.recv, self.local = send, recv, local
        self.stages = []
        start, size = 0, src.shape[0]
        for name in order:
            mine, peers = axes[name]
            size //= len(peers) + 1
            self.stages.append((mine, peers, start, size))
            start = start + mine * size
        self.start, self.size = start, size
        self.flying = []
        self.used = 0
        last = len(order) - 1
        self.todo = [self.scatter(k) for k in range(last + 1)]
        if outer > 1:
            self.todo += [self.exchange]
        self.todo += [self.finish] + [self.gather(k) for k in range(last - 1, -1, -1)]
        self.left = len(self.todo) + 1

    @staticmethod
    def at(start, size):
        return pl.ds(pl.multiple_of(start, 16), size)

    def go(self, src, dst, device):
        n = self.used
        self.used += 1

        def make():
            return pltpu.make_async_remote_copy(
                src_ref=src(),
                dst_ref=dst(),
                send_sem=self.send.at[n],
                recv_sem=self.recv.at[n],
                device_id=device,
                device_id_type=pl.DeviceIdType.MESH,
            )

        make().start()
        self.flying.append(make)

    def add(self, start, size, others, into=None):
        wide = F32 if len(others) > 1 else B16
        block = max(n for n in range(16, 257, 16) if size % n == 0)

        def one(i, _):
            here = pl.ds(pl.multiple_of(i * block, 16), block)
            there = self.at(start + i * block, block)
            total = self.src[there, :].astype(wide)
            for other in others:
                total = total + other[here, :].astype(wide)
            if into is None:
                self.src[there, :] = total.astype(B16)
            else:
                into[here, :] = total.astype(B16)
            return 0

        if size == block:
            one(0, 0)
        else:
            lax.fori_loop(0, size // block, one, 0)

    def take(self, k, into=None):
        mine, peers, start, size = self.stages[k]
        self.add(start + mine * size, size, [self.bufs[k].at[i] for i in range(len(peers))], into)

    def scatter(self, k):
        def run():
            if k > 0:
                self.take(k - 1)
            mine, peers, start, size = self.stages[k]
            for i, peer in enumerate(peers):
                self.go(
                    lambda i=i: self.src.at[
                        self.at(start + (mine + i + 1) % (len(peers) + 1) * size, size)
                    ],
                    lambda i=i: self.bufs[k].at[i],
                    peer,
                )

        return run

    def exchange(self):
        self.take(-1)
        for i, peer in enumerate(self.far):
            self.go(
                lambda: self.src.at[self.at(self.start, self.size)],
                lambda i=i: self.far_buf.at[i],
                peer,
            )

    def finish(self):
        if self.far:
            others = [self.far_buf.at[i] for i in range(len(self.far))]
            self.add(self.start, self.size, others, self.final)
        else:
            self.take(-1, self.final)

        def own():
            return pltpu.make_async_copy(
                self.final, self.out.at[self.at(self.start, self.size)], self.local
            )

        own().start()
        self.flying.append(own)
        for peer in self.stages[-1][1]:
            self.go(lambda: self.final, lambda: self.out.at[self.at(self.start, self.size)], peer)

    def gather(self, k):
        def run():
            _, _, start, size = self.stages[k + 1]
            rows = size * (len(self.stages[k + 1][1]) + 1)
            for peer in self.stages[k][1]:
                here = lambda: self.out.at[self.at(start, rows)]
                self.go(here, here, peer)

        return run

    def step(self):
        if not self.left:
            return
        for make in self.flying:
            make().wait()
        self.flying = []
        self.left -= 1
        if self.todo:
            self.todo.pop(0)()


def compute_kernel(lens_ref, *rest):
    inputs, rest = rest[:20], rest[20:]
    out_hbm, gin_hbm, *rest = rest
    sums_out, rest = rest[:7], rest[7:]
    (
        hid_ref, geo_own_ref, geo_ref, gn1_send_ref, gn1_recv_ref, halo_send, halo_recv,
        n1t_ref, xhat_ref, rstd_ref, q_ref, k_ref, v_ref, m_ref, mb_ref, mt_ref, off_ref, dist_ref,
        hopi_ref, edgei_ref, cols_ref, w1_ref, w2_ref, innert_ref, feat_ref, hidden_ref, slope_ref,
        bias_ref, p_ref, mixed_ref, gmix_ref, gq_ref, gk_ref, gv_ref, goff_ref, lhsh_ref, lhse_ref,
        rhsh_ref, rhse_ref, gpre_ref, gmid_ref, gmw_ref, ginner_ref, ghop_ref, gedge_ref, gg2_ref,
        gg1_ref, gn1_ref, n1_ref, iota_ref, g1_ref, g2_ref, out_ref, gin_ref, out_sems, load_sems,
    ) = rest[:56]
    held, rest = rest[56:76], rest[76:]
    (
        own_ref, pos_ref, types_in_ref, hops_ref, edges_ref, wqkv_ref, wout_ref, gain1_ref, gain2_ref, wup_ref,
        wdown_ref, means_ref, widths_ref, inner_ref, outer_ref, hop_tab_ref, edge_tab_ref, scale_ref, shift_ref,
        cot_ref,
    ) = held
    row = lax.axis_index("rows")
    rows = lax.axis_size("rows")
    block = lax.axis_index("blocks")
    inner, outer = z_split()
    place = (row % 2, row // 2, block % 2, block // 2, inner, outer)
    chains = []
    for n in range(len(ORDERS)):
        count = 6 + len(ORDERS[n])
        src, *bufs, far_buf, final, send, recv, local = rest[:count]
        rest = rest[count:]
        if n < 9:
            out, third = sums_out[n // 3], n % 3
        elif n < 18:
            out, third = sums_out[3 + n % 3], n // 3 - 3
        else:
            out, third = sums_out[6], 0
        out = out.at[pl.ds(third * src.shape[0], src.shape[0])]
        chains.append(Chain(place, ORDERS[n], src, bufs, far_buf, final, out, send, recv, local))

    def serve(slot):
        for n in SLOTS.get(slot, ()):
            chains[n].step()

    loads = [
        pltpu.make_async_copy(src, dst, load_sems.at[n])
        for n, (src, dst) in enumerate(zip(inputs, held))
    ]
    late = (5, 6, 9, 10, 19)
    for n in (1, 2, 0):
        loads[n].start()
    for n in range(3, 20):
        if n not in late:
            loads[n].start()
    for n in late:
        loads[n].start()

    barrier = pltpu.get_barrier_semaphore()
    z_now = block // 2
    near = [
        (2 * (z_now - z_now % inner + (z_now + i) % inner) + (block + j) % 2, 2 * ((row // 2 + k) % 2) + row % 2)
        for i in range(inner)
        for j in range(2)
        for k in range(2)
        if i + j + k > 0
    ]
    others = [(block, 2 * (row // 2) + 1 - row % 2), (block, 2 * (1 - row // 2) + 1 - row % 2)]
    others += near + chains[0].far
    for other in others:
        pl.semaphore_signal(barrier, inc=1, device_id=other, device_id_type=pl.DeviceIdType.MESH)
    for n in (1, 2):
        loads[n].wait()
    geo_own_ref[...] = jnp.concatenate(
        [pos_ref[...].astype(F32), types_in_ref[...].astype(F32), jnp.zeros((4, T), F32)], axis=0
    )
    loads[0].wait()
    pl.semaphore_wait(barrier, len(others))

    next_row, last_row = (block, (row + 1) % rows), (block, (row + rows - 1) % rows)

    def halo(src, dst, n, device):
        return pltpu.make_async_remote_copy(
            src_ref=src,
            dst_ref=dst,
            send_sem=halo_send.at[n],
            recv_sem=halo_recv.at[n],
            device_id=device,
            device_id_type=pl.DeviceIdType.MESH,
        )

    def neighbours(forward, backward, n):
        to_next = lambda: halo(*forward, n, next_row)
        to_last = lambda: halo(*backward, n + 1, last_row)

        def start():
            pl.when(row < rows - 1)(lambda: to_next().start())
            pl.when(row > 0)(lambda: to_last().start())

        def wait():
            @pl.when(row < rows - 1)
            def _():
                to_next().wait_send()
                to_last().wait_recv()

            @pl.when(row > 0)
            def _():
                to_last().wait_send()
                to_next().wait_recv()

        return start, wait

    @pl.when(row == 0)
    def _():
        geo_ref[0] = jnp.zeros((8, T), F32)
        hid_ref[0] = jnp.zeros((T, D), B16)

    @pl.when(row == rows - 1)
    def _():
        geo_ref[1] = jnp.zeros((8, T), F32)
        hid_ref[1] = jnp.zeros((T, D), B16)

    geo_start, geo_wait = neighbours((geo_own_ref, geo_ref.at[0]), (geo_own_ref, geo_ref.at[1]), 0)
    hid_start, hid_wait = neighbours((own_ref, hid_ref.at[0]), (own_ref, hid_ref.at[1]), 2)
    geo_start()
    hid_start()
    for n in range(3, 20):
        if n not in late:
            loads[n].wait()
    for gain, into in ((gain1_ref, g1_ref), (gain2_ref, g2_ref)):
        for c in range(D // T):
            into[:, c * T : (c + 1) * T] = gain[c : c + 1, :]

    mean_col = down(means_ref[...])
    inv_col = 1.0 / down(widths_ref[...])
    s_col = inv_col * ((0.5 * LOG2E) ** 0.5)
    cols_ref[0] = s_col
    cols_ref[1] = mean_col * s_col
    cols_ref[2] = jnp.log2(inv_col * (1.0 / SQRT_TWO_PI))
    cols_ref[3] = inv_col * (1.0 / (0.5 * LOG2E) ** 0.5)
    innert_ref[...] = jnp.transpose(inner_ref[...])
    outer_t = outer_ref[...]
    for g in range(4):
        w1_ref[g * HEADS : (g + 1) * HEADS, 0:T] = outer_t
        w1_ref[g * HEADS : (g + 1) * HEADS, T : 2 * T] = hop_tab_ref[:, g * T : (g + 1) * T]
    for g in range(12):
        w2_ref[g * HEADS : (g + 1) * HEADS, :] = edge_tab_ref[:, g * T : (g + 1) * T]

    iota_ref[...] = lax.broadcasted_iota(jnp.int32, (T, 2 * T), 0).astype(F32).astype(B16)

    first = (row - 1) * T
    ids_row = first + lax.broadcasted_iota(jnp.int32, (1, W), 1)
    mol_row = jnp.zeros((1, W), jnp.int32)
    end = jnp.int32(0)
    for m in range(lens_ref.shape[1]):
        end = end + lens_ref[0, m]
        mol_row = mol_row + jnp.where(ids_row >= end, 1, 0)
    mol_row = jnp.where((ids_row >= 0) & (ids_row < rows * T), mol_row, -1).astype(F32)
    mol_own = mol_row[:, T : 2 * T]
    mol_col = down(mol_own)
    scale_col = jnp.concatenate(
        [down(scale_ref[:, c * T : (c + 1) * T]) for c in range(4)], axis=0
    )
    shift_col = jnp.concatenate(
        [down(shift_ref[:, c * T : (c + 1) * T]) for c in range(4)], axis=0
    )
    kinds = lax.broadcasted_iota(jnp.int32, (4 * T, T), 0)
    geo_wait()
    geo = jnp.concatenate([geo_ref[0], geo_own_ref[...], geo_ref[1]], axis=1)
    pos = geo[0:3]
    types = geo[3:4].astype(jnp.int32)
    sel = [jnp.zeros((T, T), F32) for _ in range(5)]
    own = None
    hop_sel = jnp.zeros((T, T), jnp.int32)
    edge_sel = jnp.zeros((T, T), jnp.int32)
    for t in range(3):
        lanes = slice(t * T, (t + 1) * T)
        mask = mol_col == jnp.broadcast_to(mol_row[:, lanes], (T, T))
        mask_t = down(mol_row[:, lanes]) == jnp.broadcast_to(mol_own, (T, T))
        m_ref[t] = mask.astype(F32)
        mb_ref[t] = mask.astype(F32).astype(B16)
        mt_ref[t] = mask_t.astype(F32).astype(B16)
        hit = kinds == types[:, lanes]
        terms = (
            pos[0:1, lanes],
            pos[1:2, lanes],
            pos[2:3, lanes],
            jnp.sum(jnp.where(hit, scale_col, 0.0), axis=0, keepdims=True),
            jnp.sum(jnp.where(hit, shift_col, 0.0), axis=0, keepdims=True),
        )
        if t == 1:
            own = terms
        sel = [jnp.where(mask, v, s) for v, s in zip(terms, sel)]
        tile = (row + (t - 1 + rows)) % rows
        at = pl.ds(pl.multiple_of(tile * T, T), T)
        hop_sel = jnp.where(mask, hops_ref[:, at], hop_sel)
        edge_sel = jnp.where(mask, edges_ref[:, at], edge_sel)
    ownc = [down(v) for v in own]
    dx, dy, dz = (ownc[c] - sel[c] for c in range(3))
    dist = jnp.sqrt(dx * dx + dy * dy + dz * dz)
    dist_ref[...] = dist
    off_ref[...] = (ownc[3] + sel[3]) * dist + ownc[4] + sel[4]
    hopi_ref[...] = hop_sel
    edgei_ref[...] = edge_sel

    def two(block, s):
        return jnp.concatenate([block[s : s + 1], block[s + 1 : s + 2]], axis=1)

    def wide(a):
        return jnp.concatenate([a, a], axis=1)

    def low16(index):
        return jnp.broadcast_to(index.astype(F32), (16, 2 * T)).astype(B16)

    def hot(index):
        rows16 = jnp.concatenate([low16(index & (T - 1))] * 8, axis=0)
        return jnp.where(iota_ref[...] == rows16, jnp.ones((), B16), jnp.zeros((), B16))

    def bit_masks(index, bits):
        wide_index = jnp.broadcast_to(index, (8, 2 * T))
        return [(wide_index & (1 << b)) != 0 for b in range(bits)]

    def pick(values, masks):
        for mask in masks:
            values = [
                jnp.where(mask, values[i + 1], values[i]) if i + 1 < len(values) else values[i]
                for i in range(0, len(values), 2)
            ]
        return values[0]

    def bias_step(c, _):
        at = pl.ds(pl.multiple_of(c * CHUNK, CHUNK), CHUNK)
        off8 = off_ref[at, :]
        hop8 = hopi_ref[at, :]
        edge8 = edgei_ref[at, :]
        for s in range(0, CHUNK, 2):
            lanes = pl.ds(pl.multiple_of(c * PAIRS + s * T, 2 * T), 2 * T)
            z = two(off8, s) * wide(cols_ref[0]) - wide(cols_ref[1])
            feat = jnp.exp2(wide(cols_ref[2]) - z * z).astype(B16)
            feat_ref[:, lanes] = feat
            pre = mm(innert_ref[...], feat)
            act, slope = gelu_parts(pre)
            hidden = act.astype(B16)
            hidden_ref[:, lanes] = hidden
            slope_ref[:, lanes] = slope
            hop = two(hop8, s)
            edge = two(edge8, s)
            low = mm(w1_ref[...], jnp.concatenate([hidden, hot(hop)], axis=0))
            high = mm(w2_ref[...], hot(edge))
            hop_bits = bit_masks(hop >> 7, 2)
            edge_bits = bit_masks(edge >> 7, 4)
            bias = jnp.concatenate(
                [
                    pick([low[g * HEADS + r : g * HEADS + r + 8] for g in range(4)], hop_bits)
                    + pick([high[g * HEADS + r : g * HEADS + r + 8] for g in range(12)], edge_bits)
                    for r in range(0, HEADS, 8)
                ],
                axis=0,
            )
            base = (c * CHUNK + s) * HEADS
            bias_ref[pl.ds(pl.multiple_of(base, HEADS), HEADS), :] = bias[:, :T]
            bias_ref[pl.ds(pl.multiple_of(base + HEADS, HEADS), HEADS), :] = bias[:, T:]
        return 0

    lax.fori_loop(0, T // CHUNK, bias_step, 0)

    hid_wait()
    loads[5].wait()
    for t, tile_ref in enumerate((hid_ref.at[0], own_ref, hid_ref.at[1])):
        here = slice(t * T, (t + 1) * T)
        xhat, rstd = normalise(tile_ref[...].astype(F32))
        xhat_ref[here, :] = xhat
        rstd_ref[here, :] = rstd
        n1_ref[here, :] = (xhat * g1_ref[...]).astype(B16)
        for c in range(D // T):
            n1t_ref[c * T : (c + 1) * T, here] = jnp.transpose(n1_ref[here, c * T : (c + 1) * T])
    for j in range(0, D, 2 * T):
        here = slice(j, j + 2 * T)
        q_ref[:, here] = mm(n1_ref[T : 2 * T, :], wqkv_ref[:, here]).astype(B16)
        k_ref[:, here] = mm(n1_ref[...], wqkv_ref[:, D + j : D + j + 2 * T]).astype(B16)
        v_ref[:, here] = mm(n1_ref[...], wqkv_ref[:, 2 * D + j : 2 * D + j + 2 * T]).astype(B16)

    scaling = HD ** (-0.5)

    def head_mask(h, tile, tiles):
        lane = lax.broadcasted_iota(jnp.int32, (1, tiles * T), 1) + tile * T
        return ((lane >= h * HD) & (lane < (h + 1) * HD)).astype(F32)

    def spread(low):
        return jnp.concatenate([low * mb_ref[t] for t in range(3)], axis=1)

    def compact(wide_scores):
        return jnp.where(
            m_ref[0] > 0,
            wide_scores[:, :T],
            jnp.where(m_ref[1] > 0, wide_scores[:, T : 2 * T], wide_scores[:, 2 * T :]),
        )

    def attend(half, _):
        mixed_half = [None, None, None]
        for tile, tiles, heads in GROUPS:
            lanes = pl.ds(pl.multiple_of(half * W + tile * T, T), tiles * T)
            masks = [head_mask(h, tile, tiles) for h in heads]
            q = q_ref[:, lanes]
            qm = jnp.concatenate([q * m.astype(B16) for m in masks], axis=0)
            raw = mm(qm, k_ref[:, lanes], NT)
            probs = []
            for a, h in enumerate(heads):
                head = half * 16 + h
                bias = bias_ref[pl.ds(head, T, stride=HEADS), :]
                visible = (m_ref[0] + m_ref[1] + m_ref[2]) > 0
                scores = jnp.where(
                    visible, compact(raw[a * T : (a + 1) * T]) * scaling + bias, NEG
                )
                peak = jnp.max(scores, axis=-1, keepdims=True)
                weights = jnp.exp(scores - peak)
                p = weights / jnp.sum(weights, axis=-1, keepdims=True)
                p_ref[head] = p
                probs.append(spread(p.astype(B16)))
            o = mm(jnp.concatenate(probs, axis=0), v_ref[:, lanes])
            total = o[:T] * masks[0]
            for a in range(1, len(heads)):
                total = total + o[a * T : (a + 1) * T] * masks[a]
            for j in range(tiles):
                part = total[:, j * T : (j + 1) * T]
                before = mixed_half[tile + j]
                mixed_half[tile + j] = part if before is None else before + part
        for j in range(3):
            mixed_ref[:, pl.ds(pl.multiple_of(half * W + j * T, T), T)] = mixed_half[j].astype(B16)
        return 0

    lax.fori_loop(0, 2, attend, 0)

    def tr(a):
        return jnp.concatenate(
            [jnp.transpose(a[:, c * T : (c + 1) * T]) for c in range(a.shape[1] // T)], axis=0
        )

    for n in late[1:]:
        loads[n].wait()
    mixed = mixed_ref[...]
    middle = own_ref[...].astype(F32) + mm(mixed, wout_ref[...])
    xhat2, rstd2 = normalise(middle)
    n2 = (xhat2 * g2_ref[...]).astype(B16)
    act, slope = gelu_parts(mm(n2, wup_ref[...]))
    act = act.astype(B16)
    out_ref[...] = (middle + mm(act, wdown_ref[...])).astype(B16)
    out_copy = pltpu.make_async_copy(out_ref, out_hbm, out_sems.at[0])
    out_copy.start()
    cot = cot_ref[...]

    def fill(n, left, right):
        for j in range(0, D, 2 * T):
            both = mm(left, right[:, j : j + 2 * T]).astype(B16)
            chain = chains[3 * n + j // (2 * T)]
            chain.src[:D, :] = both[:, :T]
            chain.src[D:, :] = both[:, T:]
            chain.step()
            serve(f"f{3 * n + j // (2 * T)}")

    fill(0, tr(act), cot)
    grad_pre = (mm(cot, wdown_ref[...], NT) * slope).astype(B16)
    fill(1, tr(n2), grad_pre)
    gn2 = mm(grad_pre, wup_ref[...], NT)
    gg2_ref[...] = jnp.sum(gn2 * xhat2, axis=0, keepdims=True)
    gmid = cot.astype(F32) + norm_back(gn2, xhat2, rstd2, g2_ref[...])
    gmid_ref[...] = gmid
    branch = gmid.astype(B16)
    fill(2, tr(mixed), branch)
    gmix_ref[...] = mm(branch, wout_ref[...], NT).astype(B16)

    def spread_t(low):
        return jnp.concatenate([low * mt_ref[t] for t in range(3)], axis=0)

    for half in range(2):
        gq_half = [None, None, None]
        gk_half = [None, None, None]
        gv_half = [None, None, None]

        def put(into, value, tile, tiles):
            for j in range(tiles):
                part = value[:, j * T : (j + 1) * T]
                before = into[tile + j]
                into[tile + j] = part if before is None else before + part

        for group, (tile, tiles, heads) in enumerate(GROUPS):
            lanes = slice(half * W + tile * T, half * W + (tile + tiles) * T)
            masks = [head_mask(h, tile, tiles) for h in heads]
            q = q_ref[:, lanes]
            gm = gmix_ref[:, lanes]
            qm = jnp.concatenate([q * m.astype(B16) for m in masks], axis=0)
            gmm = jnp.concatenate([gm * m.astype(B16) for m in masks], axis=0)
            grad_p = mm(gmm, v_ref[:, lanes], NT)
            wide_g, tall_g, tall_p = [], [], []
            for a, h in enumerate(heads):
                head = half * 16 + h
                p = p_ref[head]
                dp = compact(grad_p[a * T : (a + 1) * T])
                gs = p * (dp - jnp.sum(p * dp, axis=-1, keepdims=True))
                bias_ref[pl.ds(head, T, stride=HEADS), :] = gs
                wide_g.append(spread(gs.astype(B16)))
                tall_g.append(spread_t(jnp.transpose(gs).astype(B16)))
                tall_p.append(spread_t(jnp.transpose(p).astype(B16)))
            o = mm(jnp.concatenate(wide_g, axis=0), k_ref[:, lanes])
            total = o[:T] * masks[0]
            for a in range(1, len(heads)):
                total = total + o[a * T : (a + 1) * T] * masks[a]
            put(gq_half, total, tile, tiles)
            put(gk_half, mm(jnp.concatenate(tall_g, axis=1), qm), tile, tiles)
            put(gv_half, mm(jnp.concatenate(tall_p, axis=1), gmm), tile, tiles)
            serve(f"att{5 * half + group}")
        for j in range(3):
            lanes = slice(half * W + j * T, half * W + (j + 1) * T)
            gq_ref[:, lanes] = (gq_half[j] * scaling).astype(B16)
            gk_ref[:, lanes] = (gk_half[j] * scaling).astype(B16)
            gv_ref[:, lanes] = gv_half[j].astype(B16)

    for n in range(9):
        part, tile = n // 3, n % 3
        source = (gq_ref, gk_ref, gv_ref)[part]
        left = n1t_ref[:, T : 2 * T] if part == 0 else n1t_ref[...]
        right = jnp.concatenate(
            [source[:, tile * T : (tile + 1) * T], source[:, (tile + 3) * T : (tile + 4) * T]], axis=1
        )
        both = mm(left, right).astype(B16)
        chains[9 + n].src[:D, :] = both[:, :T]
        chains[9 + n].src[D:, :] = both[:, T:]
        chains[9 + n].step()
        serve(f"gq{n}")
    for j in range(0, D, 2 * T):
        here = slice(j, j + 2 * T)
        part = mm(gk_ref[...], wqkv_ref[here, D : 2 * D], NT) + mm(
            gv_ref[...], wqkv_ref[here, 2 * D :], NT
        )
        gn1_ref[:, here] = part[T : 2 * T] + mm(gq_ref[...], wqkv_ref[here, :D], NT)
        gn1_send_ref[0, :, here] = part[:T].astype(B16)
        gn1_send_ref[1, :, here] = part[2 * T :].astype(B16)
        gg1_ref[:, here] = (
            jnp.sum(part[:T] * xhat_ref[0:T, here], axis=0, keepdims=True)
            + jnp.sum(gn1_ref[:, here] * xhat_ref[T : 2 * T, here], axis=0, keepdims=True)
            + jnp.sum(part[2 * T :] * xhat_ref[2 * T :, here], axis=0, keepdims=True)
        )
    gn1_start, gn1_wait = neighbours(
        (gn1_send_ref.at[1], gn1_recv_ref.at[1]), (gn1_send_ref.at[0], gn1_recv_ref.at[0]), 4
    )
    gn1_start()
    serve("gn1")
    gmw_ref[...] = jnp.zeros_like(gmw_ref)
    ginner_ref[...] = jnp.zeros_like(ginner_ref)
    ghop_ref[...] = jnp.zeros_like(ghop_ref)
    gedge_ref[...] = jnp.zeros_like(gedge_ref)

    def back_step(c, _):
        at = pl.ds(pl.multiple_of(c * CHUNK, CHUNK), CHUNK)
        off8 = off_ref[at, :]
        hop8 = hopi_ref[at, :]
        edge8 = edgei_ref[at, :]
        goff = []
        sums = [jnp.zeros((T, T), F32) for _ in range(3)]
        for s in range(0, CHUNK, 2):
            here = slice(s * T, (s + 2) * T)
            lanes = pl.ds(pl.multiple_of(c * PAIRS + s * T, 2 * T), 2 * T)
            base = (c * CHUNK + s) * HEADS
            gs = jnp.concatenate(
                [
                    bias_ref[pl.ds(pl.multiple_of(base, HEADS), HEADS), :],
                    bias_ref[pl.ds(pl.multiple_of(base + HEADS, HEADS), HEADS), :],
                ],
                axis=1,
            )
            hop = two(hop8, s)
            edge = two(edge8, s)
            low_gs = gs.astype(B16)
            halves = (low_gs[:16], low_gs[16:])
            for index, count, into in ((hop, 4, lhsh_ref), (edge, 12, lhse_ref)):
                group16 = low16(index >> 7)
                for g in range(count):
                    mask = group16 == jnp.full((), g, B16)
                    for r in range(2):
                        into[g * HEADS + 16 * r : g * HEADS + 16 * r + 16, here] = jnp.where(
                            mask, halves[r], jnp.zeros((), B16)
                        )
            rhsh_ref[0:T, here] = hot(hop)
            rhsh_ref[T : 2 * T, here] = hidden_ref[:, lanes]
            rhse_ref[:, here] = hot(edge)
            grad_hidden = mm(outer_ref[...], low_gs, (((0,), (0,)), ((), ())))
            gpre = (grad_hidden * slope_ref[:, lanes]).astype(B16)
            gpre_ref[:, here] = gpre
            gfeat = mm(inner_ref[...], gpre)
            z = two(off8, s) * wide(cols_ref[0]) - wide(cols_ref[1])
            a = gfeat * jnp.exp2(wide(cols_ref[2]) - z * z)
            az = a * z
            azz = az * z
            goff.append(jnp.sum(az * wide(cols_ref[3]), axis=0, keepdims=True))
            sums[0] = sums[0] + az[:, :T] + az[:, T:]
            sums[1] = sums[1] + azz[:, :T] + azz[:, T:]
            sums[2] = sums[2] + a[:, :T] + a[:, T:]
        for n in range(3):
            gmw_ref[n] = gmw_ref[n] + sums[n]
        goff_ref[at, :] = jnp.concatenate(
            [-g[:, n * T : (n + 1) * T] for g in goff for n in range(2)], axis=0
        ) * (LOG2E ** 0.0)
        ghop_ref[...] += mm(lhsh_ref[...], rhsh_ref[...], NT)
        gedge_ref[...] += mm(lhse_ref[...], rhse_ref[...], NT)
        ginner_ref[...] += mm(
            feat_ref[:, pl.ds(pl.multiple_of(c * PAIRS, PAIRS), PAIRS)], gpre_ref[...], NT
        )
        for k in range(T // CHUNK):
            if f"pair{k}" in SLOTS:
                pl.when(c == k)(functools.partial(serve, f"pair{k}"))
        return 0

    lax.fori_loop(0, T // CHUNK, back_step, 0)
    goff = goff_ref[...]
    gdist = goff * dist_ref[...]
    flat = []
    for value in (gdist, goff):
        query = jnp.sum(jnp.transpose(value), axis=0, keepdims=True)
        parts = [jnp.sum(value * m_ref[t], axis=0, keepdims=True) for t in range(3)]
        parts[1] = parts[1] + query
        flat.append(parts)
    gtype = []
    for n in range(2):
        acc = jnp.zeros((4 * T, T), F32)
        for t in range(3):
            hit = kinds == types[:, t * T : (t + 1) * T]
            acc = acc + jnp.where(hit, flat[n][t], 0.0)
        gtype += [
            jnp.sum(jnp.transpose(acc[c * T : (c + 1) * T]), axis=0, keepdims=True)
            for c in range(4)
        ]
    inv = 1.0 / widths_ref[...]
    back_scale = (2.0 / LOG2E) ** 0.5
    s0, s1, s2 = (jnp.sum(jnp.transpose(gmw_ref[n]), axis=0, keepdims=True) for n in range(3))
    small = [s0 * inv * back_scale, (s1 * (back_scale * back_scale) - s2) * inv]
    for gain in (gg1_ref[...], gg2_ref[...]):
        small += [gain[:, c * T : (c + 1) * T] for c in range(D // T)]
    small += gtype + [jnp.zeros((10, T), F32)]
    tail = chains[18].src
    tail[0:128, :] = ginner_ref[...].astype(B16)
    tail[128:256, :] = ghop_ref[:, :T].astype(B16)
    tail[256:640, :] = gedge_ref[...].astype(B16)
    tail[640:672, :] = (
        ghop_ref[0:32, T:] + ghop_ref[32:64, T:] + ghop_ref[64:96, T:] + ghop_ref[96:128, T:]
    ).astype(B16)
    tail[672:704, :] = jnp.concatenate(small, axis=0).astype(B16)
    tail[704:, :] = jnp.zeros((tail.shape[0] - 704, T), B16)
    chains[18].step()
    serve("small")
    gn1_wait()
    from_next = jnp.where(row < rows - 1, gn1_recv_ref[0].astype(F32), 0.0)
    from_last = jnp.where(row > 0, gn1_recv_ref[1].astype(F32), 0.0)
    gin_ref[...] = gmid_ref[...] + norm_back(
        gn1_ref[...] + from_next + from_last,
        xhat_ref[T : 2 * T, :],
        rstd_ref[T : 2 * T, :],
        g1_ref[...],
    )
    gin_copy = pltpu.make_async_copy(gin_ref, gin_hbm, out_sems.at[1])
    gin_copy.start()
    for n in TAIL:
        chains[n].step()
    while any(chain.left for chain in chains):
        for chain in chains:
            if chain.left:
                chain.step()
    out_copy.wait()
    gin_copy.wait()


def unpack_kernel(*refs):
    ins, outs = refs[:7], refs[7:]
    (gqkv, gout, gg1, gg2, gup, gdown, gmeans, gwidths, ginner, gouter, ghop, gedge, gscale, gshift) = outs
    for t in range(D // T):
        here = slice(t * T, (t + 1) * T)
        gdown[:, here] = ins[0][t].astype(F32)
        gup[:, here] = ins[1][t].astype(F32)
        gout[:, here] = ins[2][t].astype(F32)
        for n in range(3):
            gqkv[:, (3 * t + n) * T : (3 * t + n + 1) * T] = ins[3 + n][t].astype(F32)

    @pl.when(pl.program_id(0) == 0)
    def _():
        tail = ins[6]
        ginner[...] = tail[0:128, :].astype(F32)
        for g in range(4):
            ghop[:, g * T : (g + 1) * T] = tail[128 + 32 * g : 160 + 32 * g, :].astype(F32)
        for g in range(12):
            gedge[:, g * T : (g + 1) * T] = tail[256 + 32 * g : 288 + 32 * g, :].astype(F32)
        gouter[...] = tail[640:672, :].astype(F32)
        small = tail[672:704, :].astype(F32)
        gmeans[...] = small[0:1]
        gwidths[...] = small[1:2]
        gg1[...] = small[2:8]
        gg2[...] = small[8:14]
        for c in range(4):
            gscale[:, c * T : (c + 1) * T] = small[14 + c : 15 + c]
            gshift[:, c * T : (c + 1) * T] = small[18 + c : 19 + c]


def run_unpack(sums):
    def whole(*shape):
        return pl.BlockSpec(shape, lambda j: (0, 0)), jax.ShapeDtypeStruct(shape, F32)

    step = 384

    def rows(columns):
        return (
            pl.BlockSpec((step, columns), lambda j: (j, 0)),
            jax.ShapeDtypeStruct((D, columns), F32),
        )

    outs = (
        rows(3 * D), rows(D), whole(6, T), whole(6, T), rows(D), rows(D), whole(1, T), whole(1, T),
        whole(T, T), whole(HEADS, T), whole(HEADS, 4 * T), whole(HEADS, 12 * T), whole(1, 4 * T),
        whole(1, 4 * T),
    )
    tiles = [value.reshape(6, D, T) for value in sums[:6]]
    return pl.pallas_call(
        unpack_kernel,
        grid=(D // step,),
        in_specs=[pl.BlockSpec((6, step, T), lambda j: (0, j, 0))] * 6
        + [pl.BlockSpec(sums[6].shape, lambda j: (0, 0))],
        out_specs=[o[0] for o in outs],
        out_shape=[o[1] for o in outs],
        compiler_params=pltpu.CompilerParams(vmem_limit_bytes=60 * 1024 * 1024),
        name="unpack",
    )(*tiles, sums[6])


def run_compute(args):
    vm = pltpu.VMEM
    inner, outer = z_split()
    unit = 8 * inner * 16

    def padded(count):
        return -(-count // unit) * unit

    counts = [padded(2 * D)] * 18 + [padded(704)]
    out_shape = [jax.ShapeDtypeStruct((T, D), B16), jax.ShapeDtypeStruct((T, D), F32)]
    out_shape += [jax.ShapeDtypeStruct((3 * counts[0], T), B16)] * 6
    out_shape += [jax.ShapeDtypeStruct((counts[18], T), B16)]
    scratch = [
        vm((2, T, D), B16),
        vm((8, T), F32),
        vm((2, 8, T), F32),
        vm((2, T, D), B16),
        vm((2, T, D), B16),
        pltpu.SemaphoreType.DMA((6,)),
        pltpu.SemaphoreType.DMA((6,)),
        vm((D, W), B16),
        vm((W, D), F32),
        vm((W, 1), F32),
        vm((T, D), B16),
        vm((W, D), B16),
        vm((W, D), B16),
        vm((3, T, T), F32),
        vm((3, T, T), B16),
        vm((3, T, T), B16),
        vm((T, T), F32),
        vm((T, T), F32),
        vm((T, T), jnp.int32),
        vm((T, T), jnp.int32),
        vm((4, T, T), F32),
        vm((T, 2 * T), B16),
        vm((3 * T, T), B16),
        vm((T, T), B16),
        vm((T, T * T), B16),
        vm((T, T * T), B16),
        vm((T, T * T), F32),
        vm((T * HEADS, T), F32),
        vm((HEADS, T, T), F32),
        vm((T, D), B16),
        vm((T, D), B16),
        vm((T, D), B16),
        vm((W, D), B16),
        vm((W, D), B16),
        vm((T, T), F32),
        vm((T, PAIRS), B16),
        vm((3 * T, PAIRS), B16),
        vm((2 * T, PAIRS), B16),
        vm((T, PAIRS), B16),
        vm((T, PAIRS), B16),
        vm((T, D), F32),
        vm((3, T, T), F32),
        vm((T, T), F32),
        vm((T, 2 * T), F32),
        vm((3 * T, T), F32),
        vm((1, D), F32),
        vm((1, D), F32),
        vm((T, D), F32),
        vm((W, D), B16),
        vm((T, 2 * T), B16),
        vm((1, D), F32),
        vm((1, D), F32),
        vm((T, D), B16),
        vm((T, D), F32),
        pltpu.SemaphoreType.DMA((2,)),
        pltpu.SemaphoreType.DMA((20,)),
    ]
    scratch += [vm(arg.shape, arg.dtype) for arg in args[1:]]
    for count, order in zip(counts, ORDERS):
        size = count
        copies = outer - 1
        scratch.append(vm((count, T), B16))
        for name in order:
            ways = {"z": inner, "xyz": 4 * inner}.get(name, 2)
            size //= ways
            copies += 2 * (ways - 1)
            scratch.append(vm((ways - 1, size, T), B16))
        scratch += [
            vm((max(outer - 1, 1), size, T), B16),
            vm((size, T), B16),
            pltpu.SemaphoreType.DMA((copies,)),
            pltpu.SemaphoreType.DMA((copies,)),
            pltpu.SemaphoreType.DMA,
        ]
    sspec = pl.BlockSpec(memory_space=pltpu.SMEM)
    aspec = pl.BlockSpec(memory_space=pl.ANY)
    return pl.pallas_call(
        compute_kernel,
        out_shape=out_shape,
        in_specs=[sspec] + [aspec] * (len(args) - 1),
        out_specs=[aspec] * len(out_shape),
        scratch_shapes=scratch,
        compiler_params=pltpu.CompilerParams(
            vmem_limit_bytes=60 * 1024 * 1024, collective_id=0, has_side_effects=True
        ),
        name="layer",
    )(*args)


def body(
    hidden_in,
    positions,
    atom_types,
    path_hops,
    edge_kinds,
    mol_lengths,
    qkv_weight,
    out_weight,
    attn_gain,
    ffn_gain,
    up_weight,
    down_weight,
    kernel_means,
    kernel_widths,
    kernel_inner,
    kernel_outer,
    hop_table,
    edge_table,
    atom_scale,
    atom_shift,
    out_grad,
):
    out, grad_in, *sums = run_compute(
        (
            mol_lengths,
            hidden_in[0],
            positions[0],
            atom_types,
            path_hops[0],
            edge_kinds[0],
            qkv_weight,
            out_weight,
            attn_gain.reshape(6, T),
            ffn_gain.reshape(6, T),
            up_weight,
            down_weight,
            kernel_means[None],
            kernel_widths[None],
            kernel_inner,
            kernel_outer.T,
            hop_table,
            edge_table,
            atom_scale[None],
            atom_shift[None],
            out_grad[0],
        )
    )
    grads = run_unpack(sums)
    flat = (2, 3, 6, 7, 12, 13)
    grads = [g.reshape(-1) if n in flat else g for n, g in enumerate(grads)]
    grads[9] = grads[9].T
    return (out[None], grad_in[None]) + tuple(grads)


def solution(mesh):
    split3 = P("blocks", "rows", None)
    in_specs = (
        split3,
        P("blocks", None, "rows"),
        P("blocks", "rows"),
        split3,
        split3,
        P("blocks", None),
    ) + (P(),) * 14 + (split3,)
    out_specs = (split3, split3) + (P(),) * 14
    return jax.shard_map(body, mesh=mesh, in_specs=in_specs, out_specs=out_specs, check_vma=False)
```

```python
import functools

import jax
import jax.numpy as jnp
from jax import lax
from jax.experimental import pallas as pl
from jax.experimental.pallas import tpu as pltpu
from jax.sharding import PartitionSpec as P

EPS = 1e-05
NEG = -1000000000.0
SQRT_TWO_PI = 2.5066282746310002
SQRT_2_OVER_PI = 0.7978845608028654
CUBIC = 0.044715
LOG2E = 1.4426950408889634
F32 = jnp.float32
B16 = jnp.bfloat16
T = 128
W = 3 * T
D = 768
HEADS = 32
HD = 24
NN = (((1,), (0,)), ((), ()))
NT = (((1,), (1,)), ((), ()))
GROUPS = (
    (0, 1, (0, 1, 2, 3, 4)),
    (0, 2, (5,)),
    (1, 1, (6, 7, 8, 9)),
    (1, 2, (10,)),
    (2, 1, (11, 12, 13, 14, 15)),
)
ORDERS = ("cyxz", "cxyz", "cxyz", "cyxz", "cxyz", "cyzx", "cxyz", "cxyz", "cyxz", "cxyz", "cyxz", "cyzx", "cyxz", "cxyz", "cxyz", "cyxz", "cxyz", "cxyz", ("c", "xyz"))
SLOTS = {"f4": (0,), "f6": (1,), "f7": (2,), "f8": (3,), "att0": (4,), "att1": (5, 6), "att2": (7, 8, 0), "att3": (1,), "att4": (3,), "att5": (2,), "att6": (5,), "att7": (4,), "att9": (8, 6), "gq0": (1,), "gq2": (2,), "gq4": (5, 9, 7, 4), "gq5": (10,), "gq6": (0, 11), "gq7": (6, 12), "gq8": (1, 13, 3), "gn1": (5, 4, 7, 16), "pair0": (9, 10, 8, 15), "pair1": (1, 6, 14, 17), "pair2": (0, 2, 4, 13), "pair3": (5, 7, 3, 9), "pair4": (6, 16, 8, 11), "pair5": (0, 1, 10, 15), "pair6": (4, 2, 14, 12), "pair7": (5, 6, 7, 17), "pair8": (0, 16, 3, 13), "pair9": (1, 8, 9, 2), "pair10": (15, 1, 5, 14), "pair11": (4, 7, 10, 5), "pair12": (16, 4, 17, 13), "pair13": (6, 9, 0, 3), "pair14": (8, 6, 15, 11), "pair15": (10, 0, 2, 14), "small": (9, 16, 12, 2)}
TAIL = (17, 7, 11, 13, 3, 18, 15, 10, 7, 3, 14, 8, 12, 16, 9, 8, 11, 17, 13, 9, 15, 12, 10, 18, 16, 14, 10, 11, 17, 16, 13, 15, 12, 13, 15, 14, 11, 18, 14, 17, 12, 11, 18, 17, 12)
CHUNK = 8
PAIRS = CHUNK * T


def mm(a, b, dims=NN):
    return lax.dot_general(a, b, dims, preferred_element_type=F32)


def gelu_parts(x):
    x2 = x * x
    cubic = (SQRT_2_OVER_PI * CUBIC) * x2
    u = x * (SQRT_2_OVER_PI + cubic)
    half = 0.5 + 0.5 * jnp.tanh(u)
    act = x * half
    slope = half + act * (1.0 - half) * (2.0 * SQRT_2_OVER_PI + 6.0 * cubic)
    return act, slope


def normalise(v):
    centre = jnp.mean(v, axis=-1, keepdims=True)
    shifted = v - centre
    spread = jnp.mean(shifted * shifted, axis=-1, keepdims=True)
    rstd = lax.rsqrt(spread + EPS)
    return shifted * rstd, rstd


def norm_back(grad, xhat, rstd, gain):
    g = grad * gain
    return rstd * (
        g
        - jnp.mean(g, axis=-1, keepdims=True)
        - xhat * jnp.mean(g * xhat, axis=-1, keepdims=True)
    )


def down(row):
    return jnp.transpose(jnp.broadcast_to(row, (T, T)))


def z_split():
    count = lax.axis_size("blocks") // 2
    inner = min(count, 4)
    return inner, count // inner


class Chain:
    def __init__(self, place, order, src, bufs, far_buf, final, out, send, recv, local):
        c, x, y, z, inner, outer = place
        zi = z % inner
        row, block = 2 * x + c, 2 * z + y
        axes = {
            "c": (c, [(block, 2 * x + 1 - c)]),
            "x": (x, [(block, 2 * (1 - x) + c)]),
            "y": (y, [(2 * z + 1 - y, row)]),
            "z": (zi, [(2 * (z - zi + (zi + k) % inner) + y, row) for k in range(1, inner)]),
        }
        chip = (2 * x + y) * inner + zi
        chips = [(chip + k) % (4 * inner) for k in range(1, 4 * inner)]
        axes["xyz"] = (
            chip,
            [
                (2 * (z - zi + n % inner) + n // inner % 2, 2 * (n // (2 * inner)) + c)
                for n in chips
            ],
        )
        self.far = [
            (2 * (zi + inner * ((z // inner + k) % outer)) + y, row) for k in range(1, outer)
        ]
        self.src, self.bufs, self.far_buf, self.final, self.out = src, bufs, far_buf, final, out
        self.send, self.recv, self.local = send, recv, local
        self.stages = []
        start, size = 0, src.shape[0]
        for name in order:
            mine, peers = axes[name]
            size //= len(peers) + 1
            self.stages.append((mine, peers, start, size))
            start = start + mine * size
        self.start, self.size = start, size
        self.flying = []
        self.used = 0
        last = len(order) - 1
        self.todo = [self.scatter(k) for k in range(last + 1)]
        if outer > 1:
            self.todo += [self.exchange]
        self.todo += [self.finish] + [self.gather(k) for k in range(last - 1, -1, -1)]
        self.left = len(self.todo) + 1

    @staticmethod
    def at(start, size):
        return pl.ds(pl.multiple_of(start, 16), size)

    def go(self, src, dst, device):
        n = self.used
        self.used += 1

        def make():
            return pltpu.make_async_remote_copy(
                src_ref=src(),
                dst_ref=dst(),
                send_sem=self.send.at[n],
                recv_sem=self.recv.at[n],
                device_id=device,
                device_id_type=pl.DeviceIdType.MESH,
            )

        make().start()
        self.flying.append(make)

    def add(self, start, size, others, into=None):
        wide = F32 if len(others) > 1 else B16
        block = max(n for n in range(16, 257, 16) if size % n == 0)

        def one(i, _):
            here = pl.ds(pl.multiple_of(i * block, 16), block)
            there = self.at(start + i * block, block)
            total = self.src[there, :].astype(wide)
            for other in others:
                total = total + other[here, :].astype(wide)
            if into is None:
                self.src[there, :] = total.astype(B16)
            else:
                into[here, :] = total.astype(B16)
            return 0

        if size == block:
            one(0, 0)
        else:
            lax.fori_loop(0, size // block, one, 0)

    def take(self, k, into=None):
        mine, peers, start, size = self.stages[k]
        self.add(start + mine * size, size, [self.bufs[k].at[i] for i in range(len(peers))], into)

    def scatter(self, k):
        def run():
            if k > 0:
                self.take(k - 1)
            mine, peers, start, size = self.stages[k]
            for i, peer in enumerate(peers):
                self.go(
                    lambda i=i: self.src.at[
                        self.at(start + (mine + i + 1) % (len(peers) + 1) * size, size)
                    ],
                    lambda i=i: self.bufs[k].at[i],
                    peer,
                )

        return run

    def exchange(self):
        self.take(-1)
        for i, peer in enumerate(self.far):
            self.go(
                lambda: self.src.at[self.at(self.start, self.size)],
                lambda i=i: self.far_buf.at[i],
                peer,
            )

    def finish(self):
        if self.far:
            others = [self.far_buf.at[i] for i in range(len(self.far))]
            self.add(self.start, self.size, others, self.final)
        else:
            self.take(-1, self.final)

        def own():
            return pltpu.make_async_copy(
                self.final, self.out.at[self.at(self.start, self.size)], self.local
            )

        own().start()
        self.flying.append(own)
        for peer in self.stages[-1][1]:
            self.go(lambda: self.final, lambda: self.out.at[self.at(self.start, self.size)], peer)

    def gather(self, k):
        def run():
            _, _, start, size = self.stages[k + 1]
            rows = size * (len(self.stages[k + 1][1]) + 1)
            for peer in self.stages[k][1]:
                here = lambda: self.out.at[self.at(start, rows)]
                self.go(here, here, peer)

        return run

    def step(self):
        if not self.left:
            return
        for make in self.flying:
            make().wait()
        self.flying = []
        self.left -= 1
        if self.todo:
            self.todo.pop(0)()


def compute_kernel(lens_ref, *rest):
    inputs, rest = rest[:20], rest[20:]
    out_hbm, gin_hbm, *rest = rest
    sums_out, rest = rest[:7], rest[7:]
    (
        hid_ref, geo_own_ref, geo_ref, gn1_send_ref, gn1_recv_ref, halo_send, halo_recv,
        n1t_ref, xhat_ref, rstd_ref, q_ref, k_ref, v_ref, m_ref, mb_ref, mt_ref, off_ref, dist_ref,
        hopi_ref, edgei_ref, cols_ref, w1_ref, w2_ref, innert_ref, feat_ref, hidden_ref, slope_ref,
        bias_ref, p_ref, mixed_ref, gmix_ref, gq_ref, gk_ref, gv_ref, goff_ref, lhsh_ref, lhse_ref,
        rhsh_ref, rhse_ref, gpre_ref, gmid_ref, gmw_ref, ginner_ref, ghop_ref, gedge_ref, gg2_ref,
        gg1_ref, gn1_ref, n1_ref, iota_ref, g1_ref, g2_ref, out_ref, gin_ref, out_sems, load_sems,
    ) = rest[:56]
    held, rest = rest[56:76], rest[76:]
    (
        own_ref, pos_ref, types_in_ref, hops_ref, edges_ref, wqkv_ref, wout_ref, gain1_ref, gain2_ref, wup_ref,
        wdown_ref, means_ref, widths_ref, inner_ref, outer_ref, hop_tab_ref, edge_tab_ref, scale_ref, shift_ref,
        cot_ref,
    ) = held
    row = lax.axis_index("rows")
    rows = lax.axis_size("rows")
    block = lax.axis_index("blocks")
    inner, outer = z_split()
    place = (row % 2, row // 2, block % 2, block // 2, inner, outer)
    chains = []
    for n in range(len(ORDERS)):
        count = 6 + len(ORDERS[n])
        src, *bufs, far_buf, final, send, recv, local = rest[:count]
        rest = rest[count:]
        if n < 9:
            out, third = sums_out[n // 3], n % 3
        elif n < 18:
            out, third = sums_out[3 + n % 3], n // 3 - 3
        else:
            out, third = sums_out[6], 0
        out = out.at[pl.ds(third * src.shape[0], src.shape[0])]
        chains.append(Chain(place, ORDERS[n], src, bufs, far_buf, final, out, send, recv, local))

    def serve(slot):
        for n in SLOTS.get(slot, ()):
            chains[n].step()

    loads = [
        pltpu.make_async_copy(src, dst, load_sems.at[n])
        for n, (src, dst) in enumerate(zip(inputs, held))
    ]
    late = (5, 6, 9, 10, 19)
    for n in (1, 2, 0):
        loads[n].start()
    for n in range(3, 20):
        if n not in late:
            loads[n].start()
    for n in late:
        loads[n].start()

    barrier = pltpu.get_barrier_semaphore()
    z_now = block // 2
    near = [
        (2 * (z_now - z_now % inner + (z_now + i) % inner) + (block + j) % 2, 2 * ((row // 2 + k) % 2) + row % 2)
        for i in range(inner)
        for j in range(2)
        for k in range(2)
        if i + j + k > 0
    ]
    others = [(block, 2 * (row // 2) + 1 - row % 2), (block, 2 * (1 - row // 2) + 1 - row % 2)]
    others += near + chains[0].far
    for other in others:
        pl.semaphore_signal(barrier, inc=1, device_id=other, device_id_type=pl.DeviceIdType.MESH)
    for n in (1, 2):
        loads[n].wait()
    geo_own_ref[...] = jnp.concatenate(
        [pos_ref[...].astype(F32), types_in_ref[...].astype(F32), jnp.zeros((4, T), F32)], axis=0
    )
    loads[0].wait()
    pl.semaphore_wait(barrier, len(others))

    next_row, last_row = (block, (row + 1) % rows), (block, (row + rows - 1) % rows)

    def halo(src, dst, n, device):
        return pltpu.make_async_remote_copy(
            src_ref=src,
            dst_ref=dst,
            send_sem=halo_send.at[n],
            recv_sem=halo_recv.at[n],
            device_id=device,
            device_id_type=pl.DeviceIdType.MESH,
        )

    def neighbours(forward, backward, n):
        to_next = lambda: halo(*forward, n, next_row)
        to_last = lambda: halo(*backward, n + 1, last_row)

        def start():
            pl.when(row < rows - 1)(lambda: to_next().start())
            pl.when(row > 0)(lambda: to_last().start())

        def wait():
            @pl.when(row < rows - 1)
            def _():
                to_next().wait_send()
                to_last().wait_recv()

            @pl.when(row > 0)
            def _():
                to_last().wait_send()
                to_next().wait_recv()

        return start, wait

    @pl.when(row == 0)
    def _():
        geo_ref[0] = jnp.zeros((8, T), F32)
        hid_ref[0] = jnp.zeros((T, D), B16)

    @pl.when(row == rows - 1)
    def _():
        geo_ref[1] = jnp.zeros((8, T), F32)
        hid_ref[1] = jnp.zeros((T, D), B16)

    geo_start, geo_wait = neighbours((geo_own_ref, geo_ref.at[0]), (geo_own_ref, geo_ref.at[1]), 0)
    hid_start, hid_wait = neighbours((own_ref, hid_ref.at[0]), (own_ref, hid_ref.at[1]), 2)
    geo_start()
    hid_start()
    for n in range(3, 20):
        if n not in late:
            loads[n].wait()
    for gain, into in ((gain1_ref, g1_ref), (gain2_ref, g2_ref)):
        for c in range(D // T):
            into[:, c * T : (c + 1) * T] = gain[c : c + 1, :]

    mean_col = down(means_ref[...])
    inv_col = 1.0 / down(widths_ref[...])
    s_col = inv_col * ((0.5 * LOG2E) ** 0.5)
    cols_ref[0] = s_col
    cols_ref[1] = mean_col * s_col
    cols_ref[2] = jnp.log2(inv_col * (1.0 / SQRT_TWO_PI))
    cols_ref[3] = inv_col * (1.0 / (0.5 * LOG2E) ** 0.5)
    innert_ref[...] = jnp.transpose(inner_ref[...])
    outer_t = outer_ref[...]
    for g in range(4):
        w1_ref[g * HEADS : (g + 1) * HEADS, 0:T] = outer_t
        w1_ref[g * HEADS : (g + 1) * HEADS, T : 2 * T] = hop_tab_ref[:, g * T : (g + 1) * T]
    for g in range(12):
        w2_ref[g * HEADS : (g + 1) * HEADS, :] = edge_tab_ref[:, g * T : (g + 1) * T]

    iota_ref[...] = lax.broadcasted_iota(jnp.int32, (T, 2 * T), 0).astype(F32).astype(B16)

    first = (row - 1) * T
    ids_row = first + lax.broadcasted_iota(jnp.int32, (1, W), 1)
    mol_row = jnp.zeros((1, W), jnp.int32)
    end = jnp.int32(0)
    for m in range(lens_ref.shape[1]):
        end = end + lens_ref[0, m]
        mol_row = mol_row + jnp.where(ids_row >= end, 1, 0)
    mol_row = jnp.where((ids_row >= 0) & (ids_row < rows * T), mol_row, -1).astype(F32)
    mol_own = mol_row[:, T : 2 * T]
    mol_col = down(mol_own)
    scale_col = jnp.concatenate(
        [down(scale_ref[:, c * T : (c + 1) * T]) for c in range(4)], axis=0
    )
    shift_col = jnp.concatenate(
        [down(shift_ref[:, c * T : (c + 1) * T]) for c in range(4)], axis=0
    )
    kinds = lax.broadcasted_iota(jnp.int32, (4 * T, T), 0)
    geo_wait()
    geo = jnp.concatenate([geo_ref[0], geo_own_ref[...], geo_ref[1]], axis=1)
    pos = geo[0:3]
    types = geo[3:4].astype(jnp.int32)
    sel = [jnp.zeros((T, T), F32) for _ in range(5)]
    own = None
    hop_sel = jnp.zeros((T, T), jnp.int32)
    edge_sel = jnp.zeros((T, T), jnp.int32)
    for t in range(3):
        lanes = slice(t * T, (t + 1) * T)
        mask = mol_col == jnp.broadcast_to(mol_row[:, lanes], (T, T))
        mask_t = down(mol_row[:, lanes]) == jnp.broadcast_to(mol_own, (T, T))
        m_ref[t] = mask.astype(F32)
        mb_ref[t] = mask.astype(F32).astype(B16)
        mt_ref[t] = mask_t.astype(F32).astype(B16)
        hit = kinds == types[:, lanes]
        terms = (
            pos[0:1, lanes],
            pos[1:2, lanes],
            pos[2:3, lanes],
            jnp.sum(jnp.where(hit, scale_col, 0.0), axis=0, keepdims=True),
            jnp.sum(jnp.where(hit, shift_col, 0.0), axis=0, keepdims=True),
        )
        if t == 1:
            own = terms
        sel = [jnp.where(mask, v, s) for v, s in zip(terms, sel)]
        tile = (row + (t - 1 + rows)) % rows
        at = pl.ds(pl.multiple_of(tile * T, T), T)
        hop_sel = jnp.where(mask, hops_ref[:, at], hop_sel)
        edge_sel = jnp.where(mask, edges_ref[:, at], edge_sel)
    ownc = [down(v) for v in own]
    dx, dy, dz = (ownc[c] - sel[c] for c in range(3))
    dist = jnp.sqrt(dx * dx + dy * dy + dz * dz)
    dist_ref[...] = dist
    off_ref[...] = (ownc[3] + sel[3]) * dist + ownc[4] + sel[4]
    hopi_ref[...] = hop_sel
    edgei_ref[...] = edge_sel

    def two(block, s):
        return jnp.concatenate([block[s : s + 1], block[s + 1 : s + 2]], axis=1)

    def wide(a):
        return jnp.concatenate([a, a], axis=1)

    def low16(index):
        return jnp.broadcast_to(index.astype(F32), (16, 2 * T)).astype(B16)

    def hot(index):
        rows16 = jnp.concatenate([low16(index & (T - 1))] * 8, axis=0)
        return jnp.where(iota_ref[...] == rows16, jnp.ones((), B16), jnp.zeros((), B16))

    def bit_masks(index, bits):
        wide_index = jnp.broadcast_to(index, (8, 2 * T))
        return [(wide_index & (1 << b)) != 0 for b in range(bits)]

    def pick(values, masks):
        for mask in masks:
            values = [
                jnp.where(mask, values[i + 1], values[i]) if i + 1 < len(values) else values[i]
                for i in range(0, len(values), 2)
            ]
        return values[0]

    def bias_step(c, _):
        at = pl.ds(pl.multiple_of(c * CHUNK, CHUNK), CHUNK)
        off8 = off_ref[at, :]
        hop8 = hopi_ref[at, :]
        edge8 = edgei_ref[at, :]
        for first_pair in range(0, CHUNK, 8):
            steps = range(first_pair, first_pair + 8, 2)
            lanes = [pl.ds(pl.multiple_of(c * PAIRS + s * T, 2 * T), 2 * T) for s in steps]
            highs = [mm(w2_ref[...], hot(two(edge8, s))) for s in steps]
            pres = []
            for s, at in zip(steps, lanes):
                z = two(off8, s) * wide(cols_ref[0]) - wide(cols_ref[1])
                feat = jnp.exp2(wide(cols_ref[2]) - z * z).astype(B16)
                feat_ref[:, at] = feat
                pres.append(mm(innert_ref[...], feat))
            lows = []
            for s, at, pre in zip(steps, lanes, pres):
                act, slope = gelu_parts(pre)
                hidden = act.astype(B16)
                hidden_ref[:, at] = hidden
                slope_ref[:, at] = slope
                lows.append(mm(w1_ref[...], jnp.concatenate([hidden, hot(two(hop8, s))], axis=0)))
            for s, low, high in zip(steps, lows, highs):
                hop_bits = bit_masks(two(hop8, s) >> 7, 2)
                edge_bits = bit_masks(two(edge8, s) >> 7, 4)
                bias = jnp.concatenate(
                    [
                        pick([low[g * HEADS + r : g * HEADS + r + 8] for g in range(4)], hop_bits)
                        + pick([high[g * HEADS + r : g * HEADS + r + 8] for g in range(12)], edge_bits)
                        for r in range(0, HEADS, 8)
                    ],
                    axis=0,
                )
                base = (c * CHUNK + s) * HEADS
                bias_ref[pl.ds(pl.multiple_of(base, HEADS), HEADS), :] = bias[:, :T]
                bias_ref[pl.ds(pl.multiple_of(base + HEADS, HEADS), HEADS), :] = bias[:, T:]
        return 0

    lax.fori_loop(0, T // CHUNK, bias_step, 0)

    hid_wait()
    loads[5].wait()
    for t, tile_ref in enumerate((hid_ref.at[0], own_ref, hid_ref.at[1])):
        here = slice(t * T, (t + 1) * T)
        xhat, rstd = normalise(tile_ref[...].astype(F32))
        xhat_ref[here, :] = xhat
        rstd_ref[here, :] = rstd
        n1_ref[here, :] = (xhat * g1_ref[...]).astype(B16)
        for c in range(D // T):
            n1t_ref[c * T : (c + 1) * T, here] = jnp.transpose(n1_ref[here, c * T : (c + 1) * T])
    for j in range(0, D, 2 * T):
        here = slice(j, j + 2 * T)
        q_ref[:, here] = mm(n1_ref[T : 2 * T, :], wqkv_ref[:, here]).astype(B16)
        k_ref[:, here] = mm(n1_ref[...], wqkv_ref[:, D + j : D + j + 2 * T]).astype(B16)
        v_ref[:, here] = mm(n1_ref[...], wqkv_ref[:, 2 * D + j : 2 * D + j + 2 * T]).astype(B16)

    scaling = HD ** (-0.5)

    def head_mask(h, tile, tiles):
        lane = lax.broadcasted_iota(jnp.int32, (1, tiles * T), 1) + tile * T
        return ((lane >= h * HD) & (lane < (h + 1) * HD)).astype(F32)

    def spread(low):
        return jnp.concatenate([low * mb_ref[t] for t in range(3)], axis=1)

    def compact(wide_scores):
        return jnp.where(
            m_ref[0] > 0,
            wide_scores[:, :T],
            jnp.where(m_ref[1] > 0, wide_scores[:, T : 2 * T], wide_scores[:, 2 * T :]),
        )

    def attend(half, _):
        mixed_half = [None, None, None]

        def lanes_of(group):
            tile, tiles, _ = GROUPS[group]
            return pl.ds(pl.multiple_of(half * W + tile * T, T), tiles * T)

        def raw_of(group):
            tile, tiles, heads = GROUPS[group]
            q = q_ref[:, lanes_of(group)]
            qm = [q * head_mask(h, tile, tiles).astype(B16) for h in heads]
            return mm(jnp.concatenate(qm, axis=0), k_ref[:, lanes_of(group)], NT)

        raw_next = raw_of(0)
        for group, (tile, tiles, heads) in enumerate(GROUPS):
            lanes = lanes_of(group)
            masks = [head_mask(h, tile, tiles) for h in heads]
            raw = raw_next
            if group + 1 < len(GROUPS):
                raw_next = raw_of(group + 1)
            probs = []
            for a, h in enumerate(heads):
                head = half * 16 + h
                bias = bias_ref[pl.ds(head, T, stride=HEADS), :]
                visible = (m_ref[0] + m_ref[1] + m_ref[2]) > 0
                scores = jnp.where(
                    visible, compact(raw[a * T : (a + 1) * T]) * scaling + bias, NEG
                )
                peak = jnp.max(scores, axis=-1, keepdims=True)
                weights = jnp.exp(scores - peak)
                p = weights / jnp.sum(weights, axis=-1, keepdims=True)
                p_ref[head] = p
                probs.append(spread(p.astype(B16)))
            o = mm(jnp.concatenate(probs, axis=0), v_ref[:, lanes])
            total = o[:T] * masks[0]
            for a in range(1, len(heads)):
                total = total + o[a * T : (a + 1) * T] * masks[a]
            for j in range(tiles):
                part = total[:, j * T : (j + 1) * T]
                before = mixed_half[tile + j]
                mixed_half[tile + j] = part if before is None else before + part
        for j in range(3):
            mixed_ref[:, pl.ds(pl.multiple_of(half * W + j * T, T), T)] = mixed_half[j].astype(B16)
        return 0

    lax.fori_loop(0, 2, attend, 0)

    def tr(a):
        return jnp.concatenate(
            [jnp.transpose(a[:, c * T : (c + 1) * T]) for c in range(a.shape[1] // T)], axis=0
        )

    for n in late[1:]:
        loads[n].wait()
    mixed = mixed_ref[...]
    middle = own_ref[...].astype(F32) + mm(mixed, wout_ref[...])
    xhat2, rstd2 = normalise(middle)
    n2 = (xhat2 * g2_ref[...]).astype(B16)
    act, slope = gelu_parts(mm(n2, wup_ref[...]))
    act = act.astype(B16)
    out_ref[...] = (middle + mm(act, wdown_ref[...])).astype(B16)
    out_copy = pltpu.make_async_copy(out_ref, out_hbm, out_sems.at[0])
    out_copy.start()
    cot = cot_ref[...]

    def fill(n, left, right):
        for j in range(0, D, 2 * T):
            both = mm(left, right[:, j : j + 2 * T]).astype(B16)
            chain = chains[3 * n + j // (2 * T)]
            chain.src[:D, :] = both[:, :T]
            chain.src[D:, :] = both[:, T:]
            chain.step()
            serve(f"f{3 * n + j // (2 * T)}")

    fill(0, tr(act), cot)
    grad_pre = (mm(cot, wdown_ref[...], NT) * slope).astype(B16)
    fill(1, tr(n2), grad_pre)
    gn2 = mm(grad_pre, wup_ref[...], NT)
    gg2_ref[...] = jnp.sum(gn2 * xhat2, axis=0, keepdims=True)
    gmid = cot.astype(F32) + norm_back(gn2, xhat2, rstd2, g2_ref[...])
    gmid_ref[...] = gmid
    branch = gmid.astype(B16)
    fill(2, tr(mixed), branch)
    gmix_ref[...] = mm(branch, wout_ref[...], NT).astype(B16)

    def spread_t(low):
        return jnp.concatenate([low * mt_ref[t] for t in range(3)], axis=0)

    for half in range(2):
        gq_half = [None, None, None]
        gk_half = [None, None, None]
        gv_half = [None, None, None]

        def put(into, value, tile, tiles):
            for j in range(tiles):
                part = value[:, j * T : (j + 1) * T]
                before = into[tile + j]
                into[tile + j] = part if before is None else before + part

        for group, (tile, tiles, heads) in enumerate(GROUPS):
            lanes = slice(half * W + tile * T, half * W + (tile + tiles) * T)
            masks = [head_mask(h, tile, tiles) for h in heads]
            q = q_ref[:, lanes]
            gm = gmix_ref[:, lanes]
            qm = jnp.concatenate([q * m.astype(B16) for m in masks], axis=0)
            gmm = jnp.concatenate([gm * m.astype(B16) for m in masks], axis=0)
            grad_p = mm(gmm, v_ref[:, lanes], NT)
            wide_g, tall_g, tall_p = [], [], []
            for a, h in enumerate(heads):
                head = half * 16 + h
                p = p_ref[head]
                dp = compact(grad_p[a * T : (a + 1) * T])
                gs = p * (dp - jnp.sum(p * dp, axis=-1, keepdims=True))
                bias_ref[pl.ds(head, T, stride=HEADS), :] = gs
                wide_g.append(spread(gs.astype(B16)))
                tall_g.append(spread_t(jnp.transpose(gs).astype(B16)))
                tall_p.append(spread_t(jnp.transpose(p).astype(B16)))
            o = mm(jnp.concatenate(wide_g, axis=0), k_ref[:, lanes])
            total = o[:T] * masks[0]
            for a in range(1, len(heads)):
                total = total + o[a * T : (a + 1) * T] * masks[a]
            put(gq_half, total, tile, tiles)
            put(gk_half, mm(jnp.concatenate(tall_g, axis=1), qm), tile, tiles)
            put(gv_half, mm(jnp.concatenate(tall_p, axis=1), gmm), tile, tiles)
            serve(f"att{5 * half + group}")
        for j in range(3):
            lanes = slice(half * W + j * T, half * W + (j + 1) * T)
            gq_ref[:, lanes] = (gq_half[j] * scaling).astype(B16)
            gk_ref[:, lanes] = (gk_half[j] * scaling).astype(B16)
            gv_ref[:, lanes] = gv_half[j].astype(B16)

    for n in range(9):
        part, tile = n // 3, n % 3
        source = (gq_ref, gk_ref, gv_ref)[part]
        left = n1t_ref[:, T : 2 * T] if part == 0 else n1t_ref[...]
        right = jnp.concatenate(
            [source[:, tile * T : (tile + 1) * T], source[:, (tile + 3) * T : (tile + 4) * T]], axis=1
        )
        both = mm(left, right).astype(B16)
        chains[9 + n].src[:D, :] = both[:, :T]
        chains[9 + n].src[D:, :] = both[:, T:]
        chains[9 + n].step()
        serve(f"gq{n}")
    for j in range(0, D, 2 * T):
        here = slice(j, j + 2 * T)
        part = mm(gk_ref[...], wqkv_ref[here, D : 2 * D], NT) + mm(
            gv_ref[...], wqkv_ref[here, 2 * D :], NT
        )
        gn1_ref[:, here] = part[T : 2 * T] + mm(gq_ref[...], wqkv_ref[here, :D], NT)
        gn1_send_ref[0, :, here] = part[:T].astype(B16)
        gn1_send_ref[1, :, here] = part[2 * T :].astype(B16)
        gg1_ref[:, here] = (
            jnp.sum(part[:T] * xhat_ref[0:T, here], axis=0, keepdims=True)
            + jnp.sum(gn1_ref[:, here] * xhat_ref[T : 2 * T, here], axis=0, keepdims=True)
            + jnp.sum(part[2 * T :] * xhat_ref[2 * T :, here], axis=0, keepdims=True)
        )
    gn1_start, gn1_wait = neighbours(
        (gn1_send_ref.at[1], gn1_recv_ref.at[1]), (gn1_send_ref.at[0], gn1_recv_ref.at[0]), 4
    )
    gn1_start()
    serve("gn1")
    gmw_ref[...] = jnp.zeros_like(gmw_ref)
    ginner_ref[...] = jnp.zeros_like(ginner_ref)
    ghop_ref[...] = jnp.zeros_like(ghop_ref)
    gedge_ref[...] = jnp.zeros_like(gedge_ref)

    def back_step(c, _):
        at = pl.ds(pl.multiple_of(c * CHUNK, CHUNK), CHUNK)
        off8 = off_ref[at, :]
        hop8 = hopi_ref[at, :]
        edge8 = edgei_ref[at, :]
        goff = []
        sums = [jnp.zeros((T, T), F32) for _ in range(3)]
        for s in range(0, CHUNK, 2):
            here = slice(s * T, (s + 2) * T)
            lanes = pl.ds(pl.multiple_of(c * PAIRS + s * T, 2 * T), 2 * T)
            base = (c * CHUNK + s) * HEADS
            gs = jnp.concatenate(
                [
                    bias_ref[pl.ds(pl.multiple_of(base, HEADS), HEADS), :],
                    bias_ref[pl.ds(pl.multiple_of(base + HEADS, HEADS), HEADS), :],
                ],
                axis=1,
            )
            hop = two(hop8, s)
            edge = two(edge8, s)
            low_gs = gs.astype(B16)
            halves = (low_gs[:16], low_gs[16:])
            for index, count, into in ((hop, 4, lhsh_ref), (edge, 12, lhse_ref)):
                group16 = low16(index >> 7)
                for g in range(count):
                    mask = group16 == jnp.full((), g, B16)
                    for r in range(2):
                        into[g * HEADS + 16 * r : g * HEADS + 16 * r + 16, here] = jnp.where(
                            mask, halves[r], jnp.zeros((), B16)
                        )
            rhsh_ref[0:T, here] = hot(hop)
            rhsh_ref[T : 2 * T, here] = hidden_ref[:, lanes]
            rhse_ref[:, here] = hot(edge)
            grad_hidden = mm(outer_ref[...], low_gs, (((0,), (0,)), ((), ())))
            gpre = (grad_hidden * slope_ref[:, lanes]).astype(B16)
            gpre_ref[:, here] = gpre
            gfeat = mm(inner_ref[...], gpre)
            z = two(off8, s) * wide(cols_ref[0]) - wide(cols_ref[1])
            a = gfeat * jnp.exp2(wide(cols_ref[2]) - z * z)
            az = a * z
            azz = az * z
            goff.append(jnp.sum(az * wide(cols_ref[3]), axis=0, keepdims=True))
            sums[0] = sums[0] + az[:, :T] + az[:, T:]
            sums[1] = sums[1] + azz[:, :T] + azz[:, T:]
            sums[2] = sums[2] + a[:, :T] + a[:, T:]
        for n in range(3):
            gmw_ref[n] = gmw_ref[n] + sums[n]
        goff_ref[at, :] = jnp.concatenate(
            [-g[:, n * T : (n + 1) * T] for g in goff for n in range(2)], axis=0
        ) * (LOG2E ** 0.0)
        ghop_ref[...] += mm(lhsh_ref[...], rhsh_ref[...], NT)
        gedge_ref[...] += mm(lhse_ref[...], rhse_ref[...], NT)
        ginner_ref[...] += mm(
            feat_ref[:, pl.ds(pl.multiple_of(c * PAIRS, PAIRS), PAIRS)], gpre_ref[...], NT
        )
        for k in range(T // CHUNK):
            if f"pair{k}" in SLOTS:
                pl.when(c == k)(functools.partial(serve, f"pair{k}"))
        return 0

    lax.fori_loop(0, T // CHUNK, back_step, 0)
    goff = goff_ref[...]
    gdist = goff * dist_ref[...]
    flat = []
    for value in (gdist, goff):
        query = jnp.sum(jnp.transpose(value), axis=0, keepdims=True)
        parts = [jnp.sum(value * m_ref[t], axis=0, keepdims=True) for t in range(3)]
        parts[1] = parts[1] + query
        flat.append(parts)
    gtype = []
    for n in range(2):
        acc = jnp.zeros((4 * T, T), F32)
        for t in range(3):
            hit = kinds == types[:, t * T : (t + 1) * T]
            acc = acc + jnp.where(hit, flat[n][t], 0.0)
        gtype += [
            jnp.sum(jnp.transpose(acc[c * T : (c + 1) * T]), axis=0, keepdims=True)
            for c in range(4)
        ]
    inv = 1.0 / widths_ref[...]
    back_scale = (2.0 / LOG2E) ** 0.5
    s0, s1, s2 = (jnp.sum(jnp.transpose(gmw_ref[n]), axis=0, keepdims=True) for n in range(3))
    small = [s0 * inv * back_scale, (s1 * (back_scale * back_scale) - s2) * inv]
    for gain in (gg1_ref[...], gg2_ref[...]):
        small += [gain[:, c * T : (c + 1) * T] for c in range(D // T)]
    small += gtype + [jnp.zeros((10, T), F32)]
    tail = chains[18].src
    tail[0:128, :] = ginner_ref[...].astype(B16)
    tail[128:256, :] = ghop_ref[:, :T].astype(B16)
    tail[256:640, :] = gedge_ref[...].astype(B16)
    tail[640:672, :] = (
        ghop_ref[0:32, T:] + ghop_ref[32:64, T:] + ghop_ref[64:96, T:] + ghop_ref[96:128, T:]
    ).astype(B16)
    tail[672:704, :] = jnp.concatenate(small, axis=0).astype(B16)
    tail[704:, :] = jnp.zeros((tail.shape[0] - 704, T), B16)
    chains[18].step()
    serve("small")
    gn1_wait()
    from_next = jnp.where(row < rows - 1, gn1_recv_ref[0].astype(F32), 0.0)
    from_last = jnp.where(row > 0, gn1_recv_ref[1].astype(F32), 0.0)
    gin_ref[...] = gmid_ref[...] + norm_back(
        gn1_ref[...] + from_next + from_last,
        xhat_ref[T : 2 * T, :],
        rstd_ref[T : 2 * T, :],
        g1_ref[...],
    )
    gin_copy = pltpu.make_async_copy(gin_ref, gin_hbm, out_sems.at[1])
    gin_copy.start()
    for n in TAIL:
        chains[n].step()
    while any(chain.left for chain in chains):
        for chain in chains:
            if chain.left:
                chain.step()
    out_copy.wait()
    gin_copy.wait()


def unpack_kernel(*refs):
    ins, outs = refs[:7], refs[7:]
    (gqkv, gout, gg1, gg2, gup, gdown, gmeans, gwidths, ginner, gouter, ghop, gedge, gscale, gshift) = outs
    for t in range(D // T):
        here = slice(t * T, (t + 1) * T)
        gdown[:, here] = ins[0][t].astype(F32)
        gup[:, here] = ins[1][t].astype(F32)
        gout[:, here] = ins[2][t].astype(F32)
        for n in range(3):
            gqkv[:, (3 * t + n) * T : (3 * t + n + 1) * T] = ins[3 + n][t].astype(F32)

    @pl.when(pl.program_id(0) == 0)
    def _():
        tail = ins[6]
        ginner[...] = tail[0:128, :].astype(F32)
        for g in range(4):
            ghop[:, g * T : (g + 1) * T] = tail[128 + 32 * g : 160 + 32 * g, :].astype(F32)
        for g in range(12):
            gedge[:, g * T : (g + 1) * T] = tail[256 + 32 * g : 288 + 32 * g, :].astype(F32)
        gouter[...] = tail[640:672, :].astype(F32)
        small = tail[672:704, :].astype(F32)
        gmeans[...] = small[0:1]
        gwidths[...] = small[1:2]
        gg1[...] = small[2:8]
        gg2[...] = small[8:14]
        for c in range(4):
            gscale[:, c * T : (c + 1) * T] = small[14 + c : 15 + c]
            gshift[:, c * T : (c + 1) * T] = small[18 + c : 19 + c]


def run_unpack(sums):
    def whole(*shape):
        return pl.BlockSpec(shape, lambda j: (0, 0)), jax.ShapeDtypeStruct(shape, F32)

    step = 384

    def rows(columns):
        return (
            pl.BlockSpec((step, columns), lambda j: (j, 0)),
            jax.ShapeDtypeStruct((D, columns), F32),
        )

    outs = (
        rows(3 * D), rows(D), whole(6, T), whole(6, T), rows(D), rows(D), whole(1, T), whole(1, T),
        whole(T, T), whole(HEADS, T), whole(HEADS, 4 * T), whole(HEADS, 12 * T), whole(1, 4 * T),
        whole(1, 4 * T),
    )
    tiles = [value.reshape(6, D, T) for value in sums[:6]]
    return pl.pallas_call(
        unpack_kernel,
        grid=(D // step,),
        in_specs=[pl.BlockSpec((6, step, T), lambda j: (0, j, 0))] * 6
        + [pl.BlockSpec(sums[6].shape, lambda j: (0, 0))],
        out_specs=[o[0] for o in outs],
        out_shape=[o[1] for o in outs],
        compiler_params=pltpu.CompilerParams(vmem_limit_bytes=60 * 1024 * 1024),
        name="unpack",
    )(*tiles, sums[6])


def run_compute(args):
    vm = pltpu.VMEM
    inner, outer = z_split()
    unit = 8 * inner * 16

    def padded(count):
        return -(-count // unit) * unit

    counts = [padded(2 * D)] * 18 + [padded(704)]
    out_shape = [jax.ShapeDtypeStruct((T, D), B16), jax.ShapeDtypeStruct((T, D), F32)]
    out_shape += [jax.ShapeDtypeStruct((3 * counts[0], T), B16)] * 6
    out_shape += [jax.ShapeDtypeStruct((counts[18], T), B16)]
    scratch = [
        vm((2, T, D), B16),
        vm((8, T), F32),
        vm((2, 8, T), F32),
        vm((2, T, D), B16),
        vm((2, T, D), B16),
        pltpu.SemaphoreType.DMA((6,)),
        pltpu.SemaphoreType.DMA((6,)),
        vm((D, W), B16),
        vm((W, D), F32),
        vm((W, 1), F32),
        vm((T, D), B16),
        vm((W, D), B16),
        vm((W, D), B16),
        vm((3, T, T), F32),
        vm((3, T, T), B16),
        vm((3, T, T), B16),
        vm((T, T), F32),
        vm((T, T), F32),
        vm((T, T), jnp.int32),
        vm((T, T), jnp.int32),
        vm((4, T, T), F32),
        vm((T, 2 * T), B16),
        vm((3 * T, T), B16),
        vm((T, T), B16),
        vm((T, T * T), B16),
        vm((T, T * T), B16),
        vm((T, T * T), F32),
        vm((T * HEADS, T), F32),
        vm((HEADS, T, T), F32),
        vm((T, D), B16),
        vm((T, D), B16),
        vm((T, D), B16),
        vm((W, D), B16),
        vm((W, D), B16),
        vm((T, T), F32),
        vm((T, PAIRS), B16),
        vm((3 * T, PAIRS), B16),
        vm((2 * T, PAIRS), B16),
        vm((T, PAIRS), B16),
        vm((T, PAIRS), B16),
        vm((T, D), F32),
        vm((3, T, T), F32),
        vm((T, T), F32),
        vm((T, 2 * T), F32),
        vm((3 * T, T), F32),
        vm((1, D), F32),
        vm((1, D), F32),
        vm((T, D), F32),
        vm((W, D), B16),
        vm((T, 2 * T), B16),
        vm((1, D), F32),
        vm((1, D), F32),
        vm((T, D), B16),
        vm((T, D), F32),
        pltpu.SemaphoreType.DMA((2,)),
        pltpu.SemaphoreType.DMA((20,)),
    ]
    scratch += [vm(arg.shape, arg.dtype) for arg in args[1:]]
    for count, order in zip(counts, ORDERS):
        size = count
        copies = outer - 1
        scratch.append(vm((count, T), B16))
        for name in order:
            ways = {"z": inner, "xyz": 4 * inner}.get(name, 2)
            size //= ways
            copies += 2 * (ways - 1)
            scratch.append(vm((ways - 1, size, T), B16))
        scratch += [
            vm((max(outer - 1, 1), size, T), B16),
            vm((size, T), B16),
            pltpu.SemaphoreType.DMA((copies,)),
            pltpu.SemaphoreType.DMA((copies,)),
            pltpu.SemaphoreType.DMA,
        ]
    sspec = pl.BlockSpec(memory_space=pltpu.SMEM)
    aspec = pl.BlockSpec(memory_space=pl.ANY)
    return pl.pallas_call(
        compute_kernel,
        out_shape=out_shape,
        in_specs=[sspec] + [aspec] * (len(args) - 1),
        out_specs=[aspec] * len(out_shape),
        scratch_shapes=scratch,
        compiler_params=pltpu.CompilerParams(
            vmem_limit_bytes=60 * 1024 * 1024, collective_id=0, has_side_effects=True
        ),
        name="layer",
    )(*args)


def body(
    hidden_in,
    positions,
    atom_types,
    path_hops,
    edge_kinds,
    mol_lengths,
    qkv_weight,
    out_weight,
    attn_gain,
    ffn_gain,
    up_weight,
    down_weight,
    kernel_means,
    kernel_widths,
    kernel_inner,
    kernel_outer,
    hop_table,
    edge_table,
    atom_scale,
    atom_shift,
    out_grad,
):
    out, grad_in, *sums = run_compute(
        (
            mol_lengths,
            hidden_in[0],
            positions[0],
            atom_types,
            path_hops[0],
            edge_kinds[0],
            qkv_weight,
            out_weight,
            attn_gain.reshape(6, T),
            ffn_gain.reshape(6, T),
            up_weight,
            down_weight,
            kernel_means[None],
            kernel_widths[None],
            kernel_inner,
            kernel_outer.T,
            hop_table,
            edge_table,
            atom_scale[None],
            atom_shift[None],
            out_grad[0],
        )
    )
    grads = run_unpack(sums)
    flat = (2, 3, 6, 7, 12, 13)
    grads = [g.reshape(-1) if n in flat else g for n, g in enumerate(grads)]
    grads[9] = grads[9].T
    return (out[None], grad_in[None]) + tuple(grads)


def solution(mesh):
    split3 = P("blocks", "rows", None)
    in_specs = (
        split3,
        P("blocks", None, "rows"),
        P("blocks", "rows"),
        split3,
        split3,
        P("blocks", None),
    ) + (P(),) * 14 + (split3,)
    out_specs = (split3, split3) + (P(),) * 14
    return jax.shard_map(body, mesh=mesh, in_specs=in_specs, out_specs=out_specs, check_vma=False)
```
